512 devices in a mesh: leaf: 128 (over z, y, core), rhs: 4 (over x).
Axes of the slice: x: 4, y: 8, z: 8, core: 2. Of those that a mesh axis runs over, the one named last changes fastest.
Arguments:
- right_sides: float32 [64, 131072], P('rhs', 'leaf'), may hold values from -8 to 8
- leaf_inverse: float32 [131072, 1024], P('leaf', 'rhs'), may hold values from -1 to 5, as said below
- bases: bfloat16 [7, 128, 131072], P(None, None, 'leaf'), may hold values from -1 to 1
- ordering: int32 [128, 1024], P('leaf'), may hold values from 0 to 1023, as said below
Outputs:
- solution: float32 [64, 131072], P('rhs', 'leaf')
The draws below stay inside these ranges and needn't reach their ends.
Inputs may be any that keep to these rules, and one draw needn't show every extreme that they name: `leaf_inverse`: each leaf's block of 1024 rows is symmetric positive definite. `ordering`: each row is a permutation of 0 to 1023.
All inputs are finite; a program needn't handle non-finite values.
Results may differ from the reference program's by a relative error of at most 0.0003.
Values sent between devices are 32-bit elements; how exact they have to be, the bound alone decides.
No kernel may reach another device: no remote copies, remote signals or barrier semaphores. Data moves between devices by JAX's collectives and lax.ppermute only.
A program may use at most 64 MiB of HBM per device.

```python
import math
import jax
import jax.numpy as jnp
from jax import lax

LEAF = 1024
R = 128
RHS = 64
LEVELS = 7
NPTS = 131072
N_LEAF = 128


def basis_and_order(key):
    order_key = jax.random.fold_in(key, 7)
    leaf_keys = jax.random.split(order_key, N_LEAF)
    ordering = jax.vmap(lambda single: jax.random.permutation(single, LEAF))(leaf_keys).astype(jnp.int32)
    noise_key = jax.random.fold_in(key, 11)
    heights = jnp.arange(1, LEVELS + 1, dtype=jnp.float32)
    scales = 2.0 / jnp.sqrt(LEAF * 2.0 ** heights)
    noise = jax.random.normal(noise_key, (LEVELS, R, NPTS))
    basis_rows = jnp.clip(noise * scales[:, None, None], -1.0, 1.0)
    return (basis_rows, ordering)


def draw_bases(key, part):
    return basis_and_order(key)[0].astype(jnp.bfloat16)


def draw_ordering(key, part):
    return basis_and_order(key)[1]


def draw_right_sides(key, part):
    basis_rows, ordering = basis_and_order(key)
    tree_order = jnp.zeros((RHS, NPTS), jnp.float32)
    for height in range(LEVELS):
        node_span = LEAF * 2 ** (height + 1)
        groups = NPTS // node_span
        spread = (node_span / (4.0 * R)) ** 0.5
        mixing = jax.random.normal(jax.random.fold_in(key, 40 + height), (groups, R, RHS)) * spread
        level_term = jnp.einsum('rns,nrk->kns', basis_rows[height].reshape(R, groups, node_span), mixing)
        tree_order = tree_order + level_term.reshape(RHS, NPTS)
    tree_order = 0.5 * tree_order + 0.5 * jax.random.normal(jax.random.fold_in(key, 50), (RHS, NPTS))
    tree_order = jnp.clip(tree_order, -8.0, 8.0)
    by_leaf = tree_order.reshape(RHS, N_LEAF, LEAF)
    leaf_ids = jnp.arange(N_LEAF, dtype=jnp.int32)[:, None]
    data_order = jnp.zeros_like(by_leaf).at[:, leaf_ids, ordering].set(by_leaf)
    return data_order.reshape(RHS, NPTS)


def draw_leaf_inverse(key, part):
    diag_key = jax.random.fold_in(key, 21)
    off_key = jax.random.fold_in(key, 22)
    diagonal = jnp.exp(jax.random.uniform(diag_key, (N_LEAF, LEAF), minval=math.log(0.5), maxval=math.log(2.0)))
    raw_values = jnp.clip(jax.random.normal(off_key, (N_LEAF, LEAF, LEAF)), -3.0, 3.0)
    off_part = (raw_values + jnp.transpose(raw_values, (0, 2, 1))) * (0.2 / math.sqrt(2.0 * LEAF))
    matrix = off_part + diagonal[:, :, None] * jnp.eye(LEAF, dtype=jnp.float32)
    return jnp.clip(matrix, -1.0, 5.0).reshape(NPTS, LEAF)


def setup_inputs(seed: int = 0) -> dict:
    splits = jax.random.split(jax.random.key(seed), 5)
    return {
        "right_sides": draw_right_sides(jax.random.fold_in(splits[4], 71), 0),
        "leaf_inverse": draw_leaf_inverse(jax.random.fold_in(splits[4], 71), 0),
        "bases": draw_bases(jax.random.fold_in(splits[4], 71), 0),
        "ordering": draw_ordering(jax.random.fold_in(splits[4], 71), 0),
    }


def solve_factor(factor, values):
    middle = lax.linalg.triangular_solve(factor, values, left_side=True, lower=True)
    return lax.linalg.triangular_solve(factor, middle, left_side=True, lower=True, transpose_a=True)

def reference(right_sides, leaf_inverse, bases, ordering):
    highest = lax.Precision.HIGHEST
    by_leaf = right_sides.reshape(RHS, N_LEAF, LEAF)
    tree_order = jnp.take_along_axis(by_leaf, ordering[None, :, :], axis=2)
    basis_rows = bases.astype(jnp.float32)
    stacked = jnp.concatenate([tree_order, basis_rows.reshape(LEVELS * R, N_LEAF, LEAF)], 0)
    inverses = leaf_inverse.reshape(N_LEAF, LEAF, LEAF)
    applied = jnp.einsum('cip,iqp->ciq', stacked, inverses, precision=highest)
    applied = applied.reshape(RHS + LEVELS * R, NPTS)
    solved = applied[:RHS]
    pending = [applied[RHS + offset * R:RHS + (offset + 1) * R] for offset in range(LEVELS)]
    for height in range(LEVELS):
        node_span = LEAF * 2 ** (height + 1)
        groups = NPTS // node_span
        level_basis = basis_rows[height].reshape(R, groups, node_span)
        level_solved = pending[height].reshape(R, groups, node_span)
        carried = jnp.concatenate([solved] + pending[height + 1:], 0)
        column_count = carried.shape[0]
        grouped = carried.reshape(column_count, groups, node_span)
        capacity = jnp.einsum('rgp,sgp->grs', level_basis, level_solved, precision=highest)
        capacity = capacity + jnp.eye(R, dtype=jnp.float32)
        projected = jnp.einsum('rgp,cgp->grc', level_basis, grouped, precision=highest)
        factor = jnp.linalg.cholesky(capacity)
        weights = solve_factor(factor, projected)
        grouped = grouped - jnp.einsum('grc,rgp->cgp', weights, level_solved, precision=highest)
        carried = grouped.reshape(column_count, NPTS)
        solved = carried[:RHS]
        later = [carried[RHS + offset * R:RHS + (offset + 1) * R] for offset in range(LEVELS - height - 1)]
        pending = pending[:height + 1] + later
    untangled = solved.reshape(RHS, N_LEAF, LEAF)
    leaf_ids = jnp.arange(N_LEAF, dtype=jnp.int32)[:, None]
    result = jnp.zeros_like(untangled).at[:, leaf_ids, ordering].set(untangled)
    return result.reshape(RHS, NPTS)
```

```python
import functools

import jax
import jax.numpy as jnp
from jax import lax
from jax.experimental import pallas as pl
from jax.experimental.pallas import tpu as pltpu
from jax.sharding import PartitionSpec as P

HIGHEST = lax.Precision.HIGHEST
NN = (((1,), (0,)), ((), ()))
NT = (((1,), (1,)), ((), ()))


def exact_dot(left, right, dims):
    return lax.dot_general(left, right, dims, precision=HIGHEST, preferred_element_type=jnp.float32)


def short_dot(left, right, dims):
    return lax.dot_general(left, right, dims, preferred_element_type=jnp.float32)


def three_parts(values):
    high = values.astype(jnp.bfloat16)
    rest = values - high.astype(jnp.float32)
    middle = rest.astype(jnp.bfloat16)
    low = (rest - middle.astype(jnp.float32)).astype(jnp.bfloat16)
    return high, middle, low


def dot_left_parts(left, right16, dims):
    high, middle, low = three_parts(left)
    return short_dot(low, right16, dims) + short_dot(middle, right16, dims) + short_dot(high, right16, dims)


def dot_right_parts(left16, right, dims):
    high, middle, low = three_parts(right)
    return short_dot(left16, low, dims) + short_dot(left16, middle, dims) + short_dot(left16, high, dims)


def inverse_of(capacity):
    size = capacity.shape[0]
    shape = (size, size)
    eye = jnp.where(
        lax.broadcasted_iota(jnp.int32, shape, 0) == lax.broadcasted_iota(jnp.int32, shape, 1), 1.0, 0.0
    )
    bound = jnp.max(jnp.sum(jnp.abs(capacity), axis=1, keepdims=True), axis=0, keepdims=True)
    scale = 2.0 / (1.0 + bound)
    begin = 2.0 * scale * eye - scale * scale * capacity
    guess = begin
    short = capacity.astype(jnp.bfloat16)
    for _ in range(4):
        guess16 = guess.astype(jnp.bfloat16)
        factor = 2.0 * eye - short_dot(short, guess16, NN)
        guess = short_dot(guess16, factor.astype(jnp.bfloat16), NN)

    def unfinished(state):
        return (state[1] == 0) | ((state[1] < 80) & jnp.logical_not(state[2] < 1e-6))

    def improve(state):
        inverse, count, _ = state
        residual = eye - exact_dot(capacity, inverse, NN)
        size2 = jnp.sum(residual * residual)
        better = inverse + exact_dot(inverse, residual, NN)
        restart = (count == 0) & jnp.logical_not(size2 < 0.25)
        return jnp.where(restart, begin, better), count + 1, size2

    return lax.while_loop(unfinished, improve, (guess, 0, jnp.float32(1.0)))[0]


def run(body, outs, *args):
    vmem = pl.BlockSpec(memory_space=pltpu.VMEM)
    return pl.pallas_call(
        body,
        out_shape=[jax.ShapeDtypeStruct(shape, jnp.float32) for shape in outs],
        in_specs=[vmem] * len(args),
        out_specs=[vmem] * len(outs),
        compiler_params=pltpu.CompilerParams(vmem_limit_bytes=48 * 1024 * 1024),
    )(*args)


def one_hot(order):
    size = order.shape[1]
    rows = lax.broadcasted_iota(jnp.int32, (size, size), 0)
    return jnp.where(rows == order, 1.0, 0.0).astype(jnp.bfloat16)


def start_body(sides, order, inverse_cols, bases, send):
    levels, rank, leaf = bases.shape
    groups, _, piece = send.shape
    share = rank // groups
    own = sides.shape[0]
    tree = dot_left_parts(sides[...], one_hot(order[...]), NN)
    applied = dot_right_parts(bases[...].reshape(levels * rank, leaf), inverse_cols[...], NN)
    for group in range(groups):
        for level in range(levels):
            low = level * rank + group * share
            send[group, level * share : (level + 1) * share, :] = applied[low : low + share]
        for part in range(groups):
            low = levels * share + part * own
            send[group, low : low + own, :] = tree[:, part * piece : (part + 1) * piece]


def gram_body(got, bases, gram, tree):
    levels, rank, leaf = bases.shape
    groups = got.shape[0]
    share = rank // groups
    sides = tree.shape[0]
    own = sides // groups
    rows = levels * share
    applied = jnp.concatenate([got[group, :rows, :] for group in range(groups)], 1)
    for group in range(groups):
        low = rows
        tree[group * own : (group + 1) * own, :] = jnp.concatenate(
            [got[group, low + part * own : low + (part + 1) * own, :] for part in range(groups)], 1
        )
    product = dot_left_parts(applied, bases[...].reshape(levels * rank, leaf), NT)
    with_sides = exact_dot(applied, tree[...], NT)
    block = lambda level, column: product[
        level * share : (level + 1) * share, column * rank : (column + 1) * rank
    ]
    at = 0

    def put(value):
        nonlocal at
        gram[at : at + value.shape[0], :] = value
        at += value.shape[0]

    for level in range(levels):
        put(block(level, 0))
    for column in (1, 2, 3):
        for level in range(column, 4):
            put(block(level, column))
    put(
        jnp.concatenate(
            [
                with_sides[: 4 * share],
                jnp.concatenate([with_sides[4 * share :], jnp.zeros((share, sides), jnp.float32)], 0),
            ],
            1,
        )
    )
    for column in (1, 2, 3):
        for level in (4, 5, 6):
            put(block(level, column))
    for column in (4, 5, 6):
        for level in range(column, 7):
            put(block(level, column))


def first_body(everyone, mine, arrived, second, third, fourth, border, weights):
    groups = everyone.shape[0]
    rank = everyone.shape[2]
    share = rank // groups
    sides = rank // 2
    joined = lambda low: jnp.concatenate(
        [everyone[group, low : low + share, :] for group in range(groups)], 0
    )
    eye = jnp.where(
        lax.broadcasted_iota(jnp.int32, (rank, rank), 0) == lax.broadcasted_iota(jnp.int32, (rank, rank), 1),
        1.0,
        0.0,
    )
    inverse = inverse_of(joined(0) + eye)
    turned = [joined((13 + pair) * share).T for pair in range(4)]
    side_rows = lambda level: (turned[level] if level < 4 else turned[level - 4])[
        (0 if level < 4 else sides) : (sides if level < 4 else 2 * sides)
    ]
    upper = jnp.concatenate([joined(level * share) for level in range(1, 7)] + [side_rows(0)], 0)
    scaled = exact_dot(upper, inverse, NN)
    weights[...] = scaled
    own_sum = lambda low, count: (
        mine[low * share : (low + count) * share, :] + arrived[low * share : (low + count) * share, :]
    )
    own_scaled = exact_dot(own_sum(4, 3), inverse, NN)
    side_scaled = scaled[6 * rank :]
    block = lambda level: upper[(level - 1) * rank : level * rank]
    place = 7
    low_own = 17
    for column, panel in ((1, second), (2, third), (3, fourth)):
        at = 0
        factors = jnp.concatenate([scaled[(column - 1) * rank : 3 * rank], own_scaled, side_scaled], 0)
        update = exact_dot(factors, block(column), NT)
        for level in range(column, 4):
            panel[at : at + rank, :] = joined(place * share) - update[at : at + rank]
            place += 1
            at += rank
        panel[at : at + 3 * share, :] = own_sum(low_own, 3) - update[at : at + 3 * share]
        at += 3 * share
        low_own += 3
        panel[at : at + sides, :] = side_rows(column) - update[at : at + sides]
    at = 0
    for column in (4, 5, 6):
        count = 7 - column
        rows = count * share
        factors = jnp.concatenate([own_scaled[(column - 4) * share :], side_scaled], 0)
        update = exact_dot(factors, block(column), NT)
        border[at : at + rows, :] = own_sum(low_own, count) - update[:rows]
        low_own += count
        at += rows
        border[at : at + sides, :] = side_rows(column) - update[rows:]
        at += sides


def factor_body(mine, arrived, upper, weights, inverse):
    rank = mine.shape[1]
    total = mine[...] + arrived[...]
    eye = jnp.where(
        lax.broadcasted_iota(jnp.int32, (rank, rank), 0) == lax.broadcasted_iota(jnp.int32, (rank, rank), 1),
        1.0,
        0.0,
    )
    inverse[...] = inverse_of(total[:rank] + eye)
    upper[...] = total[rank:]
    weights[...] = exact_dot(total[rank:], inverse[...], NN)


def update_body(count, *refs):
    mine, arrived, upper, weights = refs[:4]
    panels = refs[4:]
    rank = upper.shape[1]
    height = upper.shape[0]
    at = 0
    for step in range(count):
        rows = height - step * rank
        update = exact_dot(weights[step * rank :, :], upper[step * rank : (step + 1) * rank, :], NT)
        panels[step][...] = mine[at : at + rows, :] + arrived[at : at + rows, :] - update
        at += rows


def border_body(rows_before, mine, arrived, weights, inverse, everyone, border, far_weights):
    groups, rows, rank = everyone.shape
    share = rank // groups
    sides = rank // 2
    far = jnp.concatenate(
        [everyone[group, level * share : (level + 1) * share, :] for level in range(3) for group in range(groups)], 0
    )
    far_weights[...] = exact_dot(far, inverse[...], NN)
    at = 0
    for column in range(3):
        count = (3 - column) * share + sides
        factors = weights[rows_before + column * share :, :]
        update = exact_dot(factors, far[column * rank : (column + 1) * rank], NT)
        border[at : at + count, :] = mine[at : at + count, :] + arrived[at : at + count, :] - update
        at += count


def spread_body(everyone, mine, arrived, upper, weights, inverse, fifth, rest, far_weights):
    groups, _, rank = everyone.shape
    share = rank // groups
    sides = rank // 2
    joined = lambda low: jnp.concatenate(
        [everyone[group, low * share : (low + 1) * share, :] for group in range(groups)], 0
    )
    far = jnp.concatenate([joined(0), joined(1), joined(2)], 0)
    scaled = exact_dot(far, inverse[...], NN)
    far_weights[...] = scaled
    factors = jnp.concatenate([scaled, weights[3 * share :, :]], 0)
    place = 3
    side_at = 0
    at = 0
    for column in range(3):
        update = exact_dot(factors[column * rank :], far[column * rank : (column + 1) * rank], NT)
        panel = fifth if column == 0 else rest
        side_at += (3 - column) * share
        for level in range(column, 3):
            low = (level - column) * rank
            panel[at : at + rank, :] = joined(place) - update[low : low + rank]
            place += 1
            at += rank
        low = (3 - column) * rank
        panel[at : at + sides, :] = (
            mine[side_at : side_at + sides, :] + arrived[side_at : side_at + sides, :] - update[low:]
        )
        side_at += sides
        at = 0 if column == 0 else at + sides


def finish_body(
    mine, arrived, w1, w2, f2, w3, f3, w4, f4, w5, w6, tree, bases, inverse_cols, solved
):
    levels, rank, leaf = bases.shape
    sides = tree.shape[0]
    total = mine[...] + arrived[...]
    eye = jnp.where(
        lax.broadcasted_iota(jnp.int32, (rank, rank), 0) == lax.broadcasted_iota(jnp.int32, (rank, rank), 1),
        1.0,
        0.0,
    )
    top = exact_dot(total[rank:], inverse_of(total[:rank] + eye), NN)
    last = lambda ref: ref[ref.shape[0] - sides :, :]
    found = top

    def lower(side_part, blocks):
        return side_part - exact_dot(found, blocks, NN)

    found = jnp.concatenate([lower(last(w6), w6[:rank, :]), found], 1)
    found = jnp.concatenate([lower(last(w5), w5[: 2 * rank, :]), found], 1)
    found = jnp.concatenate([lower(last(w4), f4[...]), found], 1)
    found = jnp.concatenate([lower(last(w3), jnp.concatenate([w3[:rank, :], f3[...]], 0)), found], 1)
    found = jnp.concatenate([lower(last(w2), jnp.concatenate([w2[: 2 * rank, :], f2[...]], 0)), found], 1)
    found = jnp.concatenate([lower(last(w1), w1[: 6 * rank, :]), found], 1)
    rest = tree[...] - dot_left_parts(found, bases[...].reshape(levels * rank, leaf), NN)
    solved[...] = exact_dot(rest, inverse_cols[...], NN)


def untangle_body(solved, order, out):
    groups = solved.shape[0]
    whole = jnp.concatenate([solved[group] for group in range(groups)], 1)
    out[...] = dot_left_parts(whole, one_hot(order[...]), NT)


def to_all(block, axis):
    count = lax.axis_size(axis)
    return lax.all_to_all(jnp.broadcast_to(block[None], (count,) + block.shape), axis, 0, 0)


def route(height):
    pairs = []
    for leaf in range(128):
        if height in (4, 7):
            low = 1 if height == 4 else 4
            ring = (leaf >> low) & 7
            pairs.append((leaf, leaf & ~(7 << low) | ((ring ^ 6) << low)))
        else:
            pairs.append((leaf, leaf ^ (1 << (height - 1))))
    return pairs


def local(right_sides, leaf_inverse, bases, ordering):
    own, leaf = right_sides.shape
    piece = leaf_inverse.shape[1]
    levels, rank, _ = bases.shape
    groups = lax.axis_size("rhs")
    share = rank // groups
    sides = own * groups
    swap = lambda block, height: lax.ppermute(block, "leaf", route(height))

    (send,) = run(
        start_body, [(groups, levels * share + sides, piece)], right_sides, ordering, leaf_inverse, bases
    )
    got = lax.all_to_all(send, "rhs", 0, 0)
    shared_rows = 17 * share
    gram, tree = run(gram_body, [(shared_rows + 15 * share, rank), (sides, leaf)], got, bases)
    other = swap(gram, 1)
    everyone = to_all(gram[:shared_rows] + other[:shared_rows], "rhs")

    mine_rows = 3 * share + sides
    panels = [(step * rank + mine_rows, rank) for step in (3, 2, 1)]
    border_shape = (6 * share + 3 * sides, rank)
    p2, p3, p4, border, w1 = run(
        first_body, panels + [border_shape, (6 * rank + sides, rank)], everyone, gram, other
    )

    square = (rank, rank)
    kept = []
    panel, later = p2, jnp.concatenate([p3, p4], 0)
    for height in (2, 3, 4):
        near = (4 - height) * rank
        arrived = swap(panel, height)
        if height < 4:
            later_arrived = swap(later, height)
        border_arrived = swap(border, height)
        upper_shape = (near + mine_rows, rank)
        upper, weights, inverse = run(factor_body, [upper_shape, upper_shape, square], panel, arrived)
        if height < 4:
            shapes = [(step * rank + mine_rows, rank) for step in range(4 - height, 0, -1)]
            updated = run(
                functools.partial(update_body, len(shapes)), shapes, later, later_arrived, upper, weights
            )
            panel = updated[0]
            later = updated[-1]
            spread = to_all(upper[near : near + 3 * share], "rhs")
            border, far = run(
                functools.partial(border_body, near),
                [border_shape, (3 * rank, rank)],
                border,
                border_arrived,
                weights,
                inverse,
                spread,
            )
            kept += [weights, far]
        else:
            total = border + border_arrived
            pieces = [upper[: 3 * share], total[: 3 * share]]
            at = 3 * share + sides
            pieces.append(total[at : at + 2 * share])
            at += 2 * share + sides
            pieces.append(total[at : at + share])
            spread = to_all(jnp.concatenate(pieces, 0), "rhs")
            panel, later, far = run(
                spread_body,
                [(3 * rank + sides, rank), (3 * rank + 2 * sides, rank), (3 * rank, rank)],
                spread,
                border,
                border_arrived,
                upper,
                weights,
                inverse,
            )
            kept += [weights, far]

    for height in (5, 6):
        arrived = swap(panel, height)
        later_arrived = swap(later, height)
        upper_shape = ((7 - height) * rank + sides, rank)
        upper, weights, inverse = run(factor_body, [upper_shape, upper_shape, square], panel, arrived)
        shapes = [(step * rank + sides, rank) for step in range(7 - height, 0, -1)]
        updated = run(
            functools.partial(update_body, len(shapes)), shapes, later, later_arrived, upper, weights
        )
        panel = updated[0]
        later = updated[-1]
        kept.append(weights)

    arrived = swap(panel, 7)
    (solved,) = run(
        finish_body, [(sides, piece)], panel, arrived, w1, *kept, tree, bases, leaf_inverse
    )
    back = lax.all_to_all(solved.reshape(groups, own, piece), "rhs", 0, 0)
    (result,) = run(untangle_body, [(own, leaf)], back, ordering)
    return result


def solution(mesh):
    placed = (P("rhs", "leaf"), P("leaf", "rhs"), P(None, None, "leaf"), P("leaf", None))
    return jax.shard_map(
        local, mesh=mesh, in_specs=placed, out_specs=P("rhs", "leaf"), check_vma=False
    )
```

```python
import functools

import jax
import jax.numpy as jnp
from jax import lax
from jax.experimental import pallas as pl
from jax.experimental.pallas import tpu as pltpu
from jax.sharding import PartitionSpec as P

HIGHEST = lax.Precision.HIGHEST
NN = (((1,), (0,)), ((), ()))
NT = (((1,), (1,)), ((), ()))


def exact_dot(left, right, dims):
    return lax.dot_general(left, right, dims, precision=HIGHEST, preferred_element_type=jnp.float32)


def short_dot(left, right, dims):
    return lax.dot_general(left, right, dims, preferred_element_type=jnp.float32)


def three_parts(values):
    high = values.astype(jnp.bfloat16)
    rest = values - high.astype(jnp.float32)
    middle = rest.astype(jnp.bfloat16)
    low = (rest - middle.astype(jnp.float32)).astype(jnp.bfloat16)
    return high, middle, low


def dot_left_parts(left, right16, dims):
    high, middle, low = three_parts(left)
    return short_dot(low, right16, dims) + short_dot(middle, right16, dims) + short_dot(high, right16, dims)


def dot_right_parts(left16, right, dims):
    high, middle, low = three_parts(right)
    return short_dot(left16, low, dims) + short_dot(left16, middle, dims) + short_dot(left16, high, dims)


def inverse_of(capacity):
    size = capacity.shape[0]
    shape = (size, size)
    eye = jnp.where(
        lax.broadcasted_iota(jnp.int32, shape, 0) == lax.broadcasted_iota(jnp.int32, shape, 1), 1.0, 0.0
    )
    bound = jnp.max(jnp.sum(jnp.abs(capacity), axis=1, keepdims=True), axis=0, keepdims=True)
    scale = 2.0 / (1.0 + bound)
    begin = 2.0 * scale * eye - scale * scale * capacity
    guess = begin
    short = capacity.astype(jnp.bfloat16)
    for _ in range(4):
        guess16 = guess.astype(jnp.bfloat16)
        factor = 2.0 * eye - short_dot(short, guess16, NN)
        guess = short_dot(guess16, factor.astype(jnp.bfloat16), NN)

    def unfinished(state):
        return (state[1] == 0) | ((state[1] < 80) & jnp.logical_not(state[2] < 1e-6))

    def improve(state):
        inverse, count, _ = state
        residual = eye - exact_dot(capacity, inverse, NN)
        size2 = jnp.sum(residual * residual)
        better = inverse + exact_dot(inverse, residual, NN)
        restart = (count == 0) & jnp.logical_not(size2 < 0.25)
        return jnp.where(restart, begin, better), count + 1, size2

    return lax.while_loop(unfinished, improve, (guess, 0, jnp.float32(1.0)))[0]


def run(body, outs, *args, cost=3):
    vmem = pl.BlockSpec(memory_space=pltpu.VMEM)
    return pl.pallas_call(
        body,
        out_shape=[jax.ShapeDtypeStruct(shape, jnp.float32) for shape in outs],
        in_specs=[vmem] * len(args),
        out_specs=[vmem] * len(outs),
        cost_estimate=pl.CostEstimate(flops=cost * 1_000_000_000, bytes_accessed=0, transcendentals=0),
        compiler_params=pltpu.CompilerParams(vmem_limit_bytes=48 * 1024 * 1024),
    )(*args)


def one_hot(order):
    size = order.shape[1]
    rows = lax.broadcasted_iota(jnp.int32, (size, size), 0)
    return jnp.where(rows == order, 1.0, 0.0).astype(jnp.bfloat16)


def identity(size):
    shape = (size, size)
    return jnp.where(
        lax.broadcasted_iota(jnp.int32, shape, 0) == lax.broadcasted_iota(jnp.int32, shape, 1), 1.0, 0.0
    )


def stacked(everyone, low, count):
    return jnp.concatenate([everyone[group, low : low + count, :] for group in range(everyone.shape[0])], 0)


def start_body(sides, order, inverse_cols, bases, send, tree):
    levels, rank, leaf = bases.shape
    groups, _, piece = send.shape
    share = rank // groups
    tree[...] = dot_left_parts(sides[...], one_hot(order[...]), NN)
    applied = dot_right_parts(bases[...].reshape(levels * rank, leaf), inverse_cols[...], NN)
    for group in range(groups):
        for level in range(levels):
            low = level * rank + group * share
            send[group, level * share : (level + 1) * share, :] = applied[low : low + share]
        send[group, levels * share :, :] = tree[:, group * piece : (group + 1) * piece]


def gram_body(got, send, bases, gram):
    levels, rank, leaf = bases.shape
    groups, rows, piece = got.shape
    share = rank // groups
    own = rows - levels * share
    applied = jnp.concatenate([got[group, : levels * share, :] for group in range(groups)], 1)
    product = dot_left_parts(applied, bases[...].reshape(levels * rank, leaf), NT)
    at = 0
    for column in range(levels):
        count = (levels - column) * share
        gram[at : at + count, :] = product[column * share :, column * rank : (column + 1) * rank]
        at += count
    sides = stacked(got, levels * share, own)
    for level in range(levels):
        block = exact_dot(sides, stacked(send, level * share, share), NT)
        for group in range(groups):
            low = at + (group * levels + level) * own
            gram[low : low + own, :] = block[group * own : (group + 1) * own]


def first_body(everyone, mine, arrived, panel, weights, own_weights, inverse, side_upper):
    groups, _, rank = everyone.shape
    share = rank // groups
    own = side_upper.shape[0]
    far = jnp.concatenate([stacked(everyone, level * share, share) for level in range(1, 7)], 0)
    inverse[...] = inverse_of(stacked(everyone, 0, share) + identity(rank))
    side_row = lambda level: sum(
        everyone[group, 7 * share + level * own : 7 * share + (level + 1) * own, :] for group in range(groups)
    )
    side_upper[...] = side_row(0)
    upper = jnp.concatenate([mine[share : 7 * share, :] + arrived[share : 7 * share, :], side_upper[...]], 0)
    own_weights[...] = exact_dot(upper, inverse[...], NN)
    update = exact_dot(own_weights[...], far[:rank], NT)
    panel[: 6 * share, :] = mine[7 * share : 13 * share, :] + arrived[7 * share : 13 * share, :] - update[: 6 * share]
    panel[6 * share :, :] = side_row(1) - update[6 * share :]
    weights[...] = far


def first_rest_body(everyone, mine, arrived, far, own_weights, rest):
    groups, _, rank = everyone.shape
    share = rank // groups
    own = own_weights.shape[0] - 6 * share
    side_row = lambda level: sum(
        everyone[group, 7 * share + level * own : 7 * share + (level + 1) * own, :] for group in range(groups)
    )
    at = 0
    source = 13 * share
    for column in range(2, 7):
        count = (7 - column) * share
        update = exact_dot(own_weights[(column - 1) * share :, :], far[(column - 1) * rank : column * rank, :], NT)
        rest[at : at + count, :] = (
            mine[source : source + count, :] + arrived[source : source + count, :] - update[:count]
        )
        rest[at + count : at + count + own, :] = side_row(column) - update[count:]
        source += count
        at += count + own


def level_body(everyone, mine, arrived, later, later_arrived, panel, far, own_weights, inverse):
    groups, rows, rank = everyone.shape
    share = rank // groups
    above = rows // share - 1
    far[...] = jnp.concatenate([stacked(everyone, level * share, share) for level in range(1, above + 1)], 0)
    inverse[...] = inverse_of(stacked(everyone, 0, share) + identity(rank))
    own_weights[...] = exact_dot(mine[share:, :] + arrived[share:, :], inverse[...], NN)
    count = panel.shape[0]
    panel[...] = later[:count, :] + later_arrived[:count, :] - exact_dot(own_weights[...], far[:rank, :], NT)


def level_rest_body(later, later_arrived, far, own_weights, rest):
    rank = far.shape[1]
    share = rank // 4
    at = 0
    source = own_weights.shape[0]
    for column in range(1, far.shape[0] // rank):
        count = own_weights.shape[0] - column * share
        update = exact_dot(own_weights[column * share :, :], far[column * rank : (column + 1) * rank, :], NT)
        rest[at : at + count, :] = (
            later[source : source + count, :] + later_arrived[source : source + count, :] - update
        )
        source += count
        at += count


def spread_body(everyone, fifth, far, weights, side_weights, inverse):
    groups, _, rank = everyone.shape
    share = rank // groups
    own = fifth.shape[0] - 3 * rank
    own = own // groups
    blocks = [stacked(everyone, level * share, share) for level in range(4)]
    inverse[...] = inverse_of(blocks[0] + identity(rank))
    far[: 3 * rank, :] = jnp.concatenate(blocks[1:], 0)
    far[3 * rank :, :] = stacked(everyone, 4 * share, own)
    weights[...] = exact_dot(far[...], inverse[...], NN)
    update = exact_dot(weights[...], far[:rank, :], NT)
    at = 4 * share + own
    for level in range(3):
        fifth[level * rank : (level + 1) * rank, :] = (
            stacked(everyone, at + level * share, share) - update[level * rank : (level + 1) * rank]
        )
    fifth[3 * rank :, :] = stacked(everyone, at + 3 * share, own) - update[3 * rank :]
    side_weights[...] = weights[3 * rank :, :]


def spread_rest_body(everyone, far, weights, rest):
    groups, _, rank = everyone.shape
    share = rank // groups
    own = (far.shape[0] - 3 * rank) // groups
    source = 7 * share + 2 * own
    at = 0
    for column in (1, 2):
        update = exact_dot(weights[column * rank :, :], far[column * rank : (column + 1) * rank, :], NT)
        for level in range(column, 3):
            low = (level - column) * rank
            rest[at : at + rank, :] = stacked(everyone, source, share) - update[low : low + rank]
            at += rank
            source += share
        rest[at : at + groups * own, :] = stacked(everyone, source, own) - update[(3 - column) * rank :]
        at += groups * own
        source += own


def factor_body(mine, arrived, later, later_arrived, panel, upper, weights):
    rank = mine.shape[1]
    upper[...] = mine[rank:, :] + arrived[rank:, :]
    inverse = inverse_of(mine[:rank, :] + arrived[:rank, :] + identity(rank))
    weights[...] = exact_dot(upper[...], inverse, NN)
    count = panel.shape[0]
    panel[...] = later[:count, :] + later_arrived[:count, :] - exact_dot(weights[...], upper[:rank, :], NT)


def factor_rest_body(later, later_arrived, upper, weights, rest):
    rank = upper.shape[1]
    source = weights.shape[0]
    rest[...] = (
        later[source:, :] + later_arrived[source:, :]
        - exact_dot(weights[rank:, :], upper[rank : 2 * rank, :], NT)
    )


def prepare_body(
    tree, everyone, send, inverse_cols, f1, i1, f2, i2, f3, i3, w4, w5, w6, base, slope
):
    groups, _, rank = everyone.shape
    share = rank // groups
    sides = base.shape[0]
    own = sides // groups
    none = jnp.zeros((rank, rank), jnp.float32)
    found = jnp.concatenate([jnp.zeros((sides, rank), jnp.float32), identity(rank)], 0)

    def lower(side_weights, blocks):
        return jnp.concatenate([side_weights, none], 0) - exact_dot(found, blocks, NN)

    for weights in (w6, w5, w4):
        count = weights.shape[0] - sides
        found = jnp.concatenate([lower(weights[count:, :], weights[:count, :]), found], 1)
    source = everyone.shape[1] - 3 * own
    for level, far, inverse in ((2, f3, i3), (1, f2, i2), (0, f1, i1)):
        low = source + level * own
        side_weights = exact_dot(stacked(everyone, low, own), inverse[...], NN)
        blocks = exact_dot(far[...], inverse[...], NN)
        found = jnp.concatenate([lower(side_weights, blocks), found], 1)
    applied = jnp.concatenate([stacked(send, level * share, share) for level in range(7)], 0)
    total = exact_dot(found, applied, NN)
    base[...] = exact_dot(tree[...], inverse_cols[...], NN) - total[:sides]
    slope[...] = total[sides:]


def finish_body(mine, arrived, base, slope, solved):
    rank = mine.shape[1]
    inverse = inverse_of(mine[:rank, :] + arrived[:rank, :] + identity(rank))
    top = exact_dot(mine[rank:, :] + arrived[rank:, :], inverse, NN)
    solved[...] = base[...] - exact_dot(top, slope[...], NN)


def untangle_body(solved, order, out):
    groups = solved.shape[0]
    whole = jnp.concatenate([solved[group] for group in range(groups)], 1)
    out[...] = dot_left_parts(whole, one_hot(order[...]), NT)


def to_all(block, axis):
    count = lax.axis_size(axis)
    return lax.all_to_all(jnp.broadcast_to(block[None], (count,) + block.shape), axis, 0, 0)


def route(height):
    pairs = []
    for leaf in range(128):
        if height in (4, 7):
            low = 1 if height == 4 else 4
            ring = (leaf >> low) & 7
            pairs.append((leaf, leaf & ~(7 << low) | ((ring ^ 6) << low)))
        else:
            pairs.append((leaf, leaf ^ (1 << (height - 1))))
    return pairs


def local(right_sides, leaf_inverse, bases, ordering):
    own, leaf = right_sides.shape
    piece = leaf_inverse.shape[1]
    levels, rank, _ = bases.shape
    groups = lax.axis_size("rhs")
    share = rank // groups
    sides = own * groups
    square = (rank, rank)
    swap = lambda block, height: lax.ppermute(block, "leaf", route(height))

    send, tree = run(
        start_body,
        [(groups, levels * share + own, piece), (own, leaf)],
        right_sides,
        ordering,
        leaf_inverse,
        bases,
    )
    got = lax.all_to_all(send, "rhs", 0, 0)
    rows = 28 * share
    (gram,) = run(gram_body, [(rows + groups * levels * own, rank)], got, send, bases)
    other = swap(gram, 1)
    total = gram + other
    shared = jnp.broadcast_to(total[: 7 * share][None], (groups, 7 * share, rank))
    parts = total[rows:].reshape(groups, levels * own, rank)
    everyone = lax.all_to_all(jnp.concatenate([shared, parts], 1), "rhs", 0, 0)

    panel, far1, own_weights, inverse1, side1 = run(
        first_body,
        [(6 * share + own, rank), (6 * rank, rank), (6 * share + own, rank), square, (own, rank)],
        everyone,
        gram,
        other,
    )
    arrived = swap(panel, 2)
    (later,) = run(
        first_rest_body, [(15 * share + 5 * own, rank)], everyone, gram, other, far1, own_weights
    )
    far, inverses, side_uppers = [far1], [inverse1], [side1]
    for height in (2, 3):
        above = 7 - height
        later_arrived = swap(later, height)
        near = panel[: (above + 1) * share] + arrived[: (above + 1) * share]
        near, later = lax.optimization_barrier((near, later))
        everyone = to_all(near, "rhs")
        side_uppers.append(panel[(above + 1) * share :] + arrived[(above + 1) * share :])
        next_panel, level_far, own_weights, inverse = run(
            level_body,
            [(above * share + own, rank), (above * rank, rank), (above * share + own, rank), square],
            everyone,
            panel,
            arrived,
            later,
            later_arrived,
        )
        arrived = swap(next_panel, height + 1)
        rest_rows = above * (above - 1) // 2 * share + (above - 1) * own
        (later,) = run(
            level_rest_body, [(rest_rows, rank)], later, later_arrived, level_far, own_weights
        )
        panel = next_panel
        far.append(level_far)
        inverses.append(inverse)

    later_arrived = swap(later, 4)
    everyone = to_all(
        jnp.concatenate([panel + arrived, later + later_arrived] + side_uppers, 0), "rhs"
    )
    upper_shape = (3 * rank + sides, rank)
    panel, upper, weights, _, _ = run(
        spread_body, [upper_shape, upper_shape, upper_shape, (sides, rank), square], everyone
    )
    arrived = swap(panel, 5)
    (later,) = run(spread_rest_body, [(3 * rank + 2 * sides, rank)], everyone, upper, weights)
    later_arrived = swap(later, 5)
    kept = [weights]
    tree, later = lax.optimization_barrier((tree, later))
    whole_tree = to_all(tree, "rhs").reshape(sides, leaf)
    next_panel, upper, weights = run(
        factor_body,
        [(2 * rank + sides, rank)] * 3,
        panel,
        arrived,
        later,
        later_arrived,
    )
    kept.append(weights)
    arrived = swap(next_panel, 6)
    (later,) = run(factor_rest_body, [(rank + sides, rank)], later, later_arrived, upper, weights)
    later_arrived = swap(later, 6)
    panel, upper, weights = run(
        factor_body,
        [(rank + sides, rank)] * 3,
        next_panel,
        arrived,
        later,
        later_arrived,
    )
    kept.append(weights)
    arrived = swap(panel, 7)
    pairs = [item for pair in zip(far, inverses) for item in pair]
    base, slope = run(
        prepare_body, [(sides, piece), (rank, piece)], whole_tree, everyone, send, leaf_inverse, *pairs, *kept
    )
    (solved,) = run(finish_body, [(sides, piece)], panel, arrived, base, slope)
    back = lax.all_to_all(solved.reshape(groups, own, piece), "rhs", 0, 0)
    (result,) = run(untangle_body, [(own, leaf)], back, ordering)
    return result


def solution(mesh):
    placed = (P("rhs", "leaf"), P("leaf", "rhs"), P(None, None, "leaf"), P("leaf", None))
    return jax.shard_map(
        local, mesh=mesh, in_specs=placed, out_specs=P("rhs", "leaf"), check_vma=False
    )
```

```python
import functools

import jax
import jax.numpy as jnp
from jax import lax
from jax.experimental import pallas as pl
from jax.experimental.pallas import tpu as pltpu
from jax.sharding import PartitionSpec as P

HIGHEST = lax.Precision.HIGHEST
VMEM_BYTES = 24 * 1024 * 1024
NN = (((1,), (0,)), ((), ()))
NT = (((1,), (1,)), ((), ()))


def exact_dot(left, right, dims):
    return lax.dot_general(left, right, dims, precision=HIGHEST, preferred_element_type=jnp.float32)


def short_dot(left, right, dims):
    return lax.dot_general(left, right, dims, preferred_element_type=jnp.float32)


def three_parts(values):
    high = values.astype(jnp.bfloat16)
    rest = values - high.astype(jnp.float32)
    middle = rest.astype(jnp.bfloat16)
    low = (rest - middle.astype(jnp.float32)).astype(jnp.bfloat16)
    return high, middle, low


def dot_left_parts(left, right16, dims):
    high, middle, low = three_parts(left)
    return short_dot(low, right16, dims) + short_dot(middle, right16, dims) + short_dot(high, right16, dims)


def dot_right_parts(left16, right, dims):
    high, middle, low = three_parts(right)
    return short_dot(left16, low, dims) + short_dot(left16, middle, dims) + short_dot(left16, high, dims)


def two_parts(values):
    high = values.astype(jnp.bfloat16)
    return high, (values - high.astype(jnp.float32)).astype(jnp.bfloat16)


def close_dot(left, right):
    left_high, left_low = two_parts(left)
    right_high, right_low = two_parts(right)
    small = short_dot(left_high, right_low, NN) + short_dot(left_low, right_high, NN)
    return small + short_dot(left_high, right_high, NN)


def inverse_of(capacity):
    eye = identity(capacity.shape[0])
    bound = jnp.max(jnp.sum(jnp.abs(capacity), axis=1, keepdims=True), axis=0, keepdims=True)
    scale = 2.0 / (1.0 + bound)
    begin = 2.0 * scale * eye - scale * scale * capacity
    guess = begin
    short = capacity.astype(jnp.bfloat16)
    for _ in range(4):
        guess16 = guess.astype(jnp.bfloat16)
        factor = 2.0 * eye - short_dot(short, guess16, NN)
        guess = short_dot(guess16, factor.astype(jnp.bfloat16), NN)

    def improve(inverse):
        residual = eye - exact_dot(capacity, inverse, NN)
        size2 = jnp.sum(jnp.sum(residual * residual, axis=1, keepdims=True), axis=0, keepdims=True)
        return inverse + close_dot(inverse, residual), size2

    better, size2 = improve(guess)
    better = jnp.where(size2 < 0.25, better, begin)
    better, size2 = improve(better)

    def unfinished(state):
        return (state[1] < 80) & jnp.logical_not(state[2] < 1e-6)

    def again(state):
        inverse, size2 = improve(state[0])
        return inverse, state[1] + 1, size2[0, 0]

    return lax.while_loop(unfinished, again, (better, 0, size2[0, 0]))[0]


def run(body, outs, *args, place=None):
    vmem = pl.BlockSpec(memory_space=pltpu.VMEM)
    scalars = [] if place is None else [place]
    return pl.pallas_call(
        body,
        out_shape=[jax.ShapeDtypeStruct(shape, jnp.float32) for shape in outs],
        in_specs=[pl.BlockSpec(memory_space=pltpu.SMEM)] * len(scalars) + [vmem] * len(args),
        out_specs=[vmem] * len(outs),
        cost_estimate=pl.CostEstimate(flops=3_000_000_000, bytes_accessed=0, transcendentals=0),
        compiler_params=pltpu.CompilerParams(vmem_limit_bytes=VMEM_BYTES),
    )(*scalars, *args)


def run_loading(body, outs, *args):
    def loading(*refs):
        count = len(args)
        sources, rest = refs[:count], refs[count:]
        results, held, done = rest[: len(outs)], rest[len(outs) : -1], rest[-1]
        copies = [
            pltpu.make_async_copy(source, target, done.at[place])
            for place, (source, target) in enumerate(zip(sources, held))
        ]
        for copy in copies:
            copy.start()
        for copy in copies:
            copy.wait()
        body(*held, *results)

    return pl.pallas_call(
        loading,
        out_shape=[jax.ShapeDtypeStruct(shape, jnp.float32) for shape in outs],
        in_specs=[pl.BlockSpec(memory_space=pltpu.HBM)] * len(args),
        out_specs=[pl.BlockSpec(memory_space=pltpu.VMEM)] * len(outs),
        scratch_shapes=[pltpu.VMEM(arg.shape, arg.dtype) for arg in args]
        + [pltpu.SemaphoreType.DMA((len(args),))],
        cost_estimate=pl.CostEstimate(flops=3_000_000_000, bytes_accessed=0, transcendentals=0),
        compiler_params=pltpu.CompilerParams(vmem_limit_bytes=VMEM_BYTES),
    )(*args)


def one_hot(order):
    size = order.shape[1]
    rows = lax.broadcasted_iota(jnp.int32, (size, size), 0)
    return jnp.where(rows == order, 1.0, 0.0).astype(jnp.bfloat16)


def identity(size):
    shape = (size, size)
    return jnp.where(
        lax.broadcasted_iota(jnp.int32, shape, 0) == lax.broadcasted_iota(jnp.int32, shape, 1), 1.0, 0.0
    )


def stacked(everyone, low, count):
    return jnp.concatenate([everyone[group, low : low + count, :] for group in range(everyone.shape[0])], 0)


def start_body(sides, order, inverse_cols, bases, send, tree):
    levels, rank, leaf = bases.shape
    groups, _, piece = send.shape
    share = rank // groups
    tree[...] = dot_left_parts(sides[...], one_hot(order[...]), NN)
    applied = dot_right_parts(bases[...].reshape(levels * rank, leaf), inverse_cols[...], NN)
    for group in range(groups):
        for level in range(levels):
            low = level * rank + group * share
            send[group, level * share : (level + 1) * share, :] = applied[low : low + share]
        send[group, levels * share :, :] = tree[:, group * piece : (group + 1) * piece]


def gram_body(got, send, bases, gram):
    levels, rank, leaf = bases.shape
    groups, rows, piece = got.shape
    share = rank // groups
    own = rows - levels * share
    applied = jnp.concatenate([got[group, : levels * share, :] for group in range(groups)], 1)
    product = dot_left_parts(applied, bases[...].reshape(levels * rank, leaf), NT)
    at = 0
    for column in range(levels):
        count = (levels - column) * share
        gram[at : at + count, :] = product[column * share :, column * rank : (column + 1) * rank]
        at += count
    sides = stacked(got, levels * share, own)
    for level in range(levels):
        block = exact_dot(sides, stacked(send, level * share, share), NT)
        for group in range(groups):
            low = at + (group * levels + level) * own
            gram[low : low + own, :] = block[group * own : (group + 1) * own]


def first_body(everyone, mine, arrived, panel, weights, own_weights, inverse, side_upper):
    groups, _, rank = everyone.shape
    share = rank // groups
    own = side_upper.shape[0]
    far = jnp.concatenate([stacked(everyone, level * share, share) for level in range(1, 7)], 0)
    inverse[...] = inverse_of(stacked(everyone, 0, share) + identity(rank))
    side_row = lambda level: sum(
        everyone[group, 7 * share + level * own : 7 * share + (level + 1) * own, :] for group in range(groups)
    )
    side_upper[...] = side_row(0)
    upper = jnp.concatenate([mine[share : 7 * share, :] + arrived[share : 7 * share, :], side_upper[...]], 0)
    own_weights[...] = exact_dot(upper, inverse[...], NN)
    update = exact_dot(own_weights[...], far[:rank], NT)
    panel[: 6 * share, :] = mine[7 * share : 13 * share, :] + arrived[7 * share : 13 * share, :] - update[: 6 * share]
    panel[6 * share :, :] = side_row(1) - update[6 * share :]
    weights[...] = far


def first_rest_body(everyone, mine, arrived, far, own_weights, rest):
    groups, _, rank = everyone.shape
    share = rank // groups
    own = own_weights.shape[0] - 6 * share
    side_row = lambda level: sum(
        everyone[group, 7 * share + level * own : 7 * share + (level + 1) * own, :] for group in range(groups)
    )
    at = 0
    source = 13 * share
    for column in range(2, 7):
        count = (7 - column) * share
        update = exact_dot(own_weights[(column - 1) * share :, :], far[(column - 1) * rank : column * rank, :], NT)
        rest[at : at + count, :] = (
            mine[source : source + count, :] + arrived[source : source + count, :] - update[:count]
        )
        rest[at + count : at + count + own, :] = side_row(column) - update[count:]
        source += count
        at += count + own


def level_body(everyone, mine, arrived, later, later_arrived, panel, far, own_weights, inverse):
    groups, rows, rank = everyone.shape
    share = rank // groups
    above = rows // share - 1
    far[...] = jnp.concatenate([stacked(everyone, level * share, share) for level in range(1, above + 1)], 0)
    inverse[...] = inverse_of(stacked(everyone, 0, share) + identity(rank))
    own_weights[...] = exact_dot(mine[share:, :] + arrived[share:, :], inverse[...], NN)
    count = panel.shape[0]
    panel[...] = later[:count, :] + later_arrived[:count, :] - exact_dot(own_weights[...], far[:rank, :], NT)


def level_rest_body(later, later_arrived, far, own_weights, rest):
    rank = far.shape[1]
    share = rank // 4
    at = 0
    source = own_weights.shape[0]
    for column in range(1, far.shape[0] // rank):
        count = own_weights.shape[0] - column * share
        update = exact_dot(own_weights[column * share :, :], far[column * rank : (column + 1) * rank, :], NT)
        rest[at : at + count, :] = (
            later[source : source + count, :] + later_arrived[source : source + count, :] - update
        )
        source += count
        at += count


def spread_body(everyone, fifth, far, weights):
    groups, _, rank = everyone.shape
    share = rank // groups
    own = fifth.shape[0] - 3 * rank
    own = own // groups
    blocks = [stacked(everyone, level * share, share) for level in range(4)]
    inverse = inverse_of(blocks[0] + identity(rank))
    far[: 3 * rank, :] = jnp.concatenate(blocks[1:], 0)
    far[3 * rank :, :] = stacked(everyone, 4 * share, own)
    weights[...] = exact_dot(far[...], inverse, NN)
    update = exact_dot(weights[...], far[:rank, :], NT)
    at = 4 * share + own
    for level in range(3):
        fifth[level * rank : (level + 1) * rank, :] = (
            stacked(everyone, at + level * share, share) - update[level * rank : (level + 1) * rank]
        )
    fifth[3 * rank :, :] = stacked(everyone, at + 3 * share, own) - update[3 * rank :]


def spread_rest_body(everyone, far, weights, sixth, seventh):
    groups, _, rank = everyone.shape
    share = rank // groups
    own = (far.shape[0] - 3 * rank) // groups
    source = 7 * share + 2 * own
    for column, panel in ((1, sixth), (2, seventh)):
        update = exact_dot(weights[column * rank :, :], far[column * rank : (column + 1) * rank, :], NT)
        at = 0
        for level in range(column, 3):
            panel[at : at + rank, :] = stacked(everyone, source, share) - update[at : at + rank]
            at += rank
            source += share
        panel[at:, :] = stacked(everyone, source, own) - update[at:]
        source += own


def factor_body(mine, arrived, upper, weights):
    rank = mine.shape[1]
    upper[...] = mine[rank:, :] + arrived[rank:, :]
    inverse = inverse_of(mine[:rank, :] + arrived[:rank, :] + identity(rank))
    weights[...] = exact_dot(upper[...], inverse, NN)


def next_body(later, later_arrived, upper, weights, panel):
    rank = upper.shape[1]
    panel[...] = later[...] + later_arrived[...] - exact_dot(weights[...], upper[:rank, :], NT)


def rest_body(later, later_arrived, upper, weights, rest):
    rank = upper.shape[1]
    rest[...] = later[...] + later_arrived[...] - exact_dot(weights[rank:, :], upper[rank : 2 * rank, :], NT)


def last_panel_body(place, later, later_arrived, upper, weights, panel):
    rank = upper.shape[1]
    own = panel.shape[0] - rank
    rows = pl.ds(pl.multiple_of(rank + place[0] * own, own), own)
    left = jnp.concatenate([weights[:rank, :], weights[rows, :]], 0)
    update = exact_dot(left, upper[:rank, :], NT)
    panel[:rank, :] = later[:rank, :] + later_arrived[:rank, :] - update[:rank]
    panel[rank:, :] = later[rows, :] + later_arrived[rows, :] - update[rank:]


def carry_first_body(send, far, inverse, carried, gone):
    groups = send.shape[0]
    share = inverse.shape[0] // groups
    applied = [stacked(send, level * share, share) for level in range(7)]
    gone[...] = applied[0]
    weights = exact_dot(far[...], inverse[...], NN)
    carried[...] = jnp.concatenate(applied[1:], 0) - exact_dot(weights, applied[0], NN)


def carry_body(before, far, inverse, carried, gone):
    rank = inverse.shape[0]
    gone[...] = before[:rank, :]
    weights = exact_dot(far[...], inverse[...], NN)
    carried[...] = before[rank:, :] - exact_dot(weights, before[:rank, :], NN)


def carry_sides_body(tree, inverse_cols, everyone, i1, i2, i3, g1, g2, g3, before, weights, carried):
    groups, _, rank = everyone.shape
    sides = tree.shape[0]
    own = sides // groups
    source = everyone.shape[1] - 3 * own
    found = exact_dot(tree[...], inverse_cols[...], NN)
    for level, inverse, gone in ((0, i1, g1), (1, i2, g2), (2, i3, g3)):
        side_weights = exact_dot(stacked(everyone, source + level * own, own), inverse[...], NN)
        found = found - exact_dot(side_weights, gone[...], NN)
    update = exact_dot(weights[...], before[:rank, :], NN)
    carried[: 3 * rank, :] = before[rank:, :] - update[: 3 * rank]
    carried[3 * rank :, :] = found - update[3 * rank :]


def carry_on_body(before, weights, carried):
    rank = weights.shape[1]
    carried[...] = before[rank:, :] - exact_dot(weights[...], before[:rank, :], NN)


def carry_last_body(before, weights, send):
    groups, rows, _ = send.shape
    rank = weights.shape[1]
    own = rows - rank
    carried = before[rank:, :] - exact_dot(weights[...], before[:rank, :], NN)
    for group in range(groups):
        send[group, :rank, :] = carried[:rank]
        send[group, rank:, :] = carried[rank + group * own : rank + (group + 1) * own]


def finish_body(mine, arrived, got, order, out):
    rank = mine.shape[1]
    groups = got.shape[0]
    inverse = inverse_of(mine[:rank, :] + arrived[:rank, :] + identity(rank))
    top = exact_dot(mine[rank:, :] + arrived[rank:, :], inverse, NN)
    slope = jnp.concatenate([got[group, :rank, :] for group in range(groups)], 1)
    base = jnp.concatenate([got[group, rank:, :] for group in range(groups)], 1)
    out[...] = dot_left_parts(base - exact_dot(top, slope, NN), one_hot(order[...]), NT)


def to_all(block, axis):
    count = lax.axis_size(axis)
    return lax.all_to_all(jnp.broadcast_to(block[None], (count,) + block.shape), axis, 0, 0)


def route(height):
    pairs = []
    for leaf in range(128):
        if height in (4, 7):
            low = 1 if height == 4 else 4
            ring = (leaf >> low) & 7
            pairs.append((leaf, leaf & ~(7 << low) | ((ring ^ 6) << low)))
        else:
            pairs.append((leaf, leaf ^ (1 << (height - 1))))
    return pairs


def local(right_sides, leaf_inverse, bases, ordering):
    own, leaf = right_sides.shape
    piece = leaf_inverse.shape[1]
    levels, rank, _ = bases.shape
    groups = lax.axis_size("rhs")
    share = rank // groups
    sides = own * groups
    square = (rank, rank)
    swap = lambda block, height: lax.ppermute(block, "leaf", route(height))

    send, tree = run_loading(
        start_body,
        [(groups, levels * share + own, piece), (own, leaf)],
        right_sides,
        ordering,
        leaf_inverse,
        bases,
    )
    got = lax.all_to_all(send, "rhs", 0, 0)
    rows = 28 * share
    (gram,) = run(gram_body, [(rows + groups * levels * own, rank)], got, send, bases)
    other = swap(gram, 1)
    total = gram + other
    shared = jnp.broadcast_to(total[: 7 * share][None], (groups, 7 * share, rank))
    parts = total[rows:].reshape(groups, levels * own, rank)
    everyone = lax.all_to_all(jnp.concatenate([shared, parts], 1), "rhs", 0, 0)

    panel, far1, own_weights, inverse1, side1 = run(
        first_body,
        [(6 * share + own, rank), (6 * rank, rank), (6 * share + own, rank), square, (own, rank)],
        everyone,
        gram,
        other,
    )
    arrived = swap(panel, 2)
    (later,) = run(
        first_rest_body, [(15 * share + 5 * own, rank)], everyone, gram, other, far1, own_weights
    )
    tree, later = lax.optimization_barrier((tree, later))
    spread_tree = lax.dynamic_update_slice(
        jnp.zeros((sides, leaf), jnp.float32), tree, (lax.axis_index("rhs") * own, 0)
    )
    whole_tree = lax.psum(spread_tree, "rhs")
    carried, gone = run(carry_first_body, [(6 * rank, piece), (rank, piece)], send, far1, inverse1)
    inverses, gones, side_uppers = [inverse1], [gone], [side1]
    for height in (2, 3):
        above = 7 - height
        later_arrived = swap(later, height)
        near = panel[: (above + 1) * share] + arrived[: (above + 1) * share]
        near, later = lax.optimization_barrier((near, later))
        everyone = to_all(near, "rhs")
        side_uppers.append(panel[(above + 1) * share :] + arrived[(above + 1) * share :])
        next_panel, level_far, own_weights, inverse = run(
            level_body,
            [(above * share + own, rank), (above * rank, rank), (above * share + own, rank), square],
            everyone,
            panel,
            arrived,
            later,
            later_arrived,
        )
        arrived = swap(next_panel, height + 1)
        rest_rows = above * (above - 1) // 2 * share + (above - 1) * own
        (later,) = run(
            level_rest_body, [(rest_rows, rank)], later, later_arrived, level_far, own_weights
        )
        panel = next_panel
        carried, gone = run(
            carry_body, [(above * rank, piece), (rank, piece)], carried, level_far, inverse
        )
        inverses.append(inverse)
        gones.append(gone)

    later_arrived = swap(later, 4)
    everyone = to_all(
        jnp.concatenate([panel + arrived, later + later_arrived] + side_uppers, 0), "rhs"
    )
    heights = lambda count: (count * rank + sides, rank)
    fifth, upper, weights = run(spread_body, [heights(3)] * 3, everyone)
    arrived = swap(fifth, 5)
    sixth, seventh = run(spread_rest_body, [heights(2), heights(1)], everyone, upper, weights)
    sixth_arrived = swap(sixth, 5)
    seventh_arrived = swap(seventh, 5)
    (carried,) = run(
        carry_sides_body,
        [(3 * rank + sides, piece)],
        whole_tree,
        leaf_inverse,
        everyone,
        *inverses,
        *gones,
        carried,
        weights,
    )
    upper, weights = run(factor_body, [heights(2)] * 2, fifth, arrived)
    (sixth,) = run(next_body, [heights(2)], sixth, sixth_arrived, upper, weights)
    arrived = swap(sixth, 6)
    (seventh,) = run(rest_body, [heights(1)], seventh, seventh_arrived, upper, weights)
    seventh_arrived = swap(seventh, 6)
    (carried,) = run(carry_on_body, [(2 * rank + sides, piece)], carried, weights)
    upper, weights = run(factor_body, [heights(1)] * 2, sixth, arrived)
    place = lax.axis_index("rhs").reshape(1)
    (seventh,) = run(
        last_panel_body, [(rank + own, rank)], seventh, seventh_arrived, upper, weights, place=place
    )
    arrived = swap(seventh, 7)
    carried, seventh = lax.optimization_barrier((carried, seventh))
    (send,) = run(carry_last_body, [(groups, rank + own, piece)], carried, weights)
    got = lax.all_to_all(send, "rhs", 0, 0)
    (result,) = run(finish_body, [(own, leaf)], seventh, arrived, got, ordering)
    return result


def solution(mesh):
    placed = (P("rhs", "leaf"), P("leaf", "rhs"), P(None, None, "leaf"), P("leaf", None))
    return jax.shard_map(
        local, mesh=mesh, in_specs=placed, out_specs=P("rhs", "leaf"), check_vma=False
    )
```

```python
import functools

import jax
import jax.numpy as jnp
from jax import lax
from jax.experimental import pallas as pl
from jax.experimental.pallas import tpu as pltpu
from jax.sharding import PartitionSpec as P

HIGHEST = lax.Precision.HIGHEST
VMEM_BYTES = 24 * 1024 * 1024
START_BYTES = 60 * 1024 * 1024
NN = (((1,), (0,)), ((), ()))
NT = (((1,), (1,)), ((), ()))


def exact_dot(left, right, dims):
    return lax.dot_general(left, right, dims, precision=HIGHEST, preferred_element_type=jnp.float32)


def short_dot(left, right, dims):
    return lax.dot_general(left, right, dims, preferred_element_type=jnp.float32)


def three_parts(values):
    high = values.astype(jnp.bfloat16)
    rest = values - high.astype(jnp.float32)
    middle = rest.astype(jnp.bfloat16)
    low = (rest - middle.astype(jnp.float32)).astype(jnp.bfloat16)
    return high, middle, low


def dot_left_parts(left, right16, dims):
    high, middle, low = three_parts(left)
    return short_dot(low, right16, dims) + short_dot(middle, right16, dims) + short_dot(high, right16, dims)


def dot_right_parts(left16, right, dims):
    high, middle, low = three_parts(right)
    return short_dot(left16, low, dims) + short_dot(left16, middle, dims) + short_dot(left16, high, dims)


def two_parts(values):
    high = values.astype(jnp.bfloat16)
    return high, (values - high.astype(jnp.float32)).astype(jnp.bfloat16)


def close_dot(left, right):
    left_high, left_low = two_parts(left)
    right_high, right_low = two_parts(right)
    small = short_dot(left_high, right_low, NN) + short_dot(left_low, right_high, NN)
    return small + short_dot(left_high, right_high, NN)


def inverse_of(capacity):
    eye = identity(capacity.shape[0])
    bound = jnp.max(jnp.sum(jnp.abs(capacity), axis=1, keepdims=True), axis=0, keepdims=True)
    scale = 2.0 / (1.0 + bound)
    begin = 2.0 * scale * eye - scale * scale * capacity
    guess = begin
    short = capacity.astype(jnp.bfloat16)
    for _ in range(4):
        guess16 = guess.astype(jnp.bfloat16)
        factor = 2.0 * eye - short_dot(short, guess16, NN)
        guess = short_dot(guess16, factor.astype(jnp.bfloat16), NN)

    def improve(inverse):
        residual = eye - exact_dot(capacity, inverse, NN)
        size2 = jnp.sum(jnp.sum(residual * residual, axis=1, keepdims=True), axis=0, keepdims=True)
        return inverse + close_dot(inverse, residual), size2

    better, size2 = improve(guess)
    better = jnp.where(size2 < 0.25, better, begin)
    better, size2 = improve(better)

    def unfinished(state):
        return (state[1] < 80) & jnp.logical_not(state[2] < 1e-6)

    def again(state):
        inverse, size2 = improve(state[0])
        return inverse, state[1] + 1, size2[0, 0]

    return lax.while_loop(unfinished, again, (better, 0, size2[0, 0]))[0]


def shape_of(out):
    return out if isinstance(out, jax.ShapeDtypeStruct) else jax.ShapeDtypeStruct(out, jnp.float32)


def run(body, outs, *args, place=None):
    vmem = pl.BlockSpec(memory_space=pltpu.VMEM)
    scalars = [] if place is None else [place]
    return pl.pallas_call(
        body,
        out_shape=[shape_of(out) for out in outs],
        in_specs=[pl.BlockSpec(memory_space=pltpu.SMEM)] * len(scalars) + [vmem] * len(args),
        out_specs=[vmem] * len(outs),
        cost_estimate=pl.CostEstimate(flops=1_000_000_000, bytes_accessed=0, transcendentals=0),
        compiler_params=pltpu.CompilerParams(vmem_limit_bytes=VMEM_BYTES),
    )(*scalars, *args)


def run_loading(body, outs, *args):
    def loading(*refs):
        count = len(args)
        sources, rest = refs[:count], refs[count:]
        results, held, done = rest[: len(outs)], rest[len(outs) : -1], rest[-1]
        copies = [
            pltpu.make_async_copy(source, target, done.at[place])
            for place, (source, target) in enumerate(zip(sources, held))
        ]
        for copy in copies:
            copy.start()
        for copy in copies:
            copy.wait()
        body(*held, *results)

    return pl.pallas_call(
        loading,
        out_shape=[shape_of(out) for out in outs],
        in_specs=[pl.BlockSpec(memory_space=pltpu.HBM)] * len(args),
        out_specs=[pl.BlockSpec(memory_space=pltpu.VMEM)] * len(outs),
        scratch_shapes=[pltpu.VMEM(arg.shape, arg.dtype) for arg in args]
        + [pltpu.SemaphoreType.DMA((len(args),))],
        cost_estimate=pl.CostEstimate(flops=1_000_000_000, bytes_accessed=0, transcendentals=0),
        compiler_params=pltpu.CompilerParams(vmem_limit_bytes=START_BYTES),
    )(*args)


def one_hot(order):
    size = order.shape[1]
    rows = lax.broadcasted_iota(jnp.int32, (size, size), 0)
    return jnp.where(rows == order, 1.0, 0.0).astype(jnp.bfloat16)


def identity(size):
    shape = (size, size)
    return jnp.where(
        lax.broadcasted_iota(jnp.int32, shape, 0) == lax.broadcasted_iota(jnp.int32, shape, 1), 1.0, 0.0
    )


def stacked(everyone, low, count):
    return jnp.concatenate([everyone[group, low : low + count, :] for group in range(everyone.shape[0])], 0)


def start_body(sides, order, inverse_cols, bases, send, hot):
    levels, rank, leaf = bases.shape
    groups, _, piece = send.shape
    share = rank // groups
    own = sides.shape[0]
    hot[...] = one_hot(order[...])
    tree = dot_left_parts(sides[...], hot[...], NN)
    applied = dot_right_parts(bases[...].reshape(levels * rank, leaf), inverse_cols[...], NN)
    for group in range(groups):
        for level in range(levels):
            low = level * rank + group * share
            send[group, level * share : (level + 1) * share, :] = applied[low : low + share]
        for part in range(groups):
            low = levels * share + part * own
            send[group, low : low + own, :] = tree[:, part * piece : (part + 1) * piece]


def gram_body(place, got, send, bases, gram, tree):
    levels, rank, leaf = bases.shape
    groups, rows, piece = got.shape
    share = rank // groups
    v_rows = levels * share
    own = (rows - v_rows) // groups
    applied = jnp.concatenate([got[group, :v_rows, :] for group in range(groups)], 1)
    product = dot_left_parts(applied, bases[...].reshape(levels * rank, leaf), NT)
    at = 0
    for column in range(levels):
        count = (levels - column) * share
        gram[at : at + count, :] = product[column * share :, column * rank : (column + 1) * rank]
        at += count
    mine = pl.ds(pl.multiple_of(v_rows + place[0] * own, own), own)
    sides = jnp.concatenate([got[group, mine, :] for group in range(groups)], 0)
    for level in range(levels):
        block = exact_dot(sides, stacked(send, level * share, share), NT)
        for group in range(groups):
            low = at + (group * levels + level) * own
            gram[low : low + own, :] = block[group * own : (group + 1) * own]
    for group in range(groups):
        tree[group * own : (group + 1) * own, :] = jnp.concatenate(
            [got[group, v_rows + part * own : v_rows + (part + 1) * own, :] for part in range(groups)], 1
        )


def first_body(everyone, mine, arrived, panel, weights, own_weights, inverse, side_upper):
    groups, _, rank = everyone.shape
    share = rank // groups
    own = side_upper.shape[0]
    far = jnp.concatenate([stacked(everyone, level * share, share) for level in range(1, 7)], 0)
    inverse[...] = inverse_of(stacked(everyone, 0, share) + identity(rank))
    side_row = lambda level: sum(
        everyone[group, 7 * share + level * own : 7 * share + (level + 1) * own, :] for group in range(groups)
    )
    side_upper[...] = side_row(0)
    upper = jnp.concatenate([mine[share : 7 * share, :] + arrived[share : 7 * share, :], side_upper[...]], 0)
    own_weights[...] = exact_dot(upper, inverse[...], NN)
    update = exact_dot(own_weights[...], far[:rank], NT)
    panel[: 6 * share, :] = mine[7 * share : 13 * share, :] + arrived[7 * share : 13 * share, :] - update[: 6 * share]
    panel[6 * share :, :] = side_row(1) - update[6 * share :]
    weights[...] = far


def first_rest_body(everyone, mine, arrived, far, own_weights, rest):
    groups, _, rank = everyone.shape
    share = rank // groups
    own = own_weights.shape[0] - 6 * share
    side_row = lambda level: sum(
        everyone[group, 7 * share + level * own : 7 * share + (level + 1) * own, :] for group in range(groups)
    )
    at = 0
    source = 13 * share
    for column in range(2, 7):
        count = (7 - column) * share
        update = exact_dot(own_weights[(column - 1) * share :, :], far[(column - 1) * rank : column * rank, :], NT)
        rest[at : at + count, :] = (
            mine[source : source + count, :] + arrived[source : source + count, :] - update[:count]
        )
        rest[at + count : at + count + own, :] = side_row(column) - update[count:]
        source += count
        at += count + own


def level_body(above, everyone, mine, arrived, later, later_arrived, panel, far, own_weights, inverse):
    groups, _, rank = everyone.shape
    share = rank // groups
    far[...] = jnp.concatenate([stacked(everyone, level * share, share) for level in range(1, above + 1)], 0)
    inverse[...] = inverse_of(stacked(everyone, 0, share) + identity(rank))
    own_weights[...] = exact_dot(mine[share:, :] + arrived[share:, :], inverse[...], NN)
    count = panel.shape[0]
    panel[...] = later[:count, :] + later_arrived[:count, :] - exact_dot(own_weights[...], far[:rank, :], NT)


def level_rest_body(later, later_arrived, far, own_weights, rest):
    rank = far.shape[1]
    share = rank // 4
    at = 0
    source = own_weights.shape[0]
    for column in range(1, far.shape[0] // rank):
        count = own_weights.shape[0] - column * share
        update = exact_dot(own_weights[column * share :, :], far[column * rank : (column + 1) * rank, :], NT)
        rest[at : at + count, :] = (
            later[source : source + count, :] + later_arrived[source : source + count, :] - update
        )
        source += count
        at += count


def spread_body(everyone, fifth, far, weights):
    groups, _, rank = everyone.shape
    share = rank // groups
    own = fifth.shape[0] - 3 * rank
    own = own // groups
    blocks = [stacked(everyone, level * share, share) for level in range(4)]
    inverse = inverse_of(blocks[0] + identity(rank))
    far[: 3 * rank, :] = jnp.concatenate(blocks[1:], 0)
    far[3 * rank :, :] = stacked(everyone, 4 * share, own)
    weights[...] = exact_dot(far[...], inverse, NN)
    update = exact_dot(weights[...], far[:rank, :], NT)
    at = 4 * share + own
    for level in range(3):
        fifth[level * rank : (level + 1) * rank, :] = (
            stacked(everyone, at + level * share, share) - update[level * rank : (level + 1) * rank]
        )
    fifth[3 * rank :, :] = stacked(everyone, at + 3 * share, own) - update[3 * rank :]


def spread_rest_body(column, everyone, far, weights, panel):
    groups, _, rank = everyone.shape
    share = rank // groups
    own = (far.shape[0] - 3 * rank) // groups
    source = (7 if column == 1 else 9) * share + (2 if column == 1 else 3) * own
    update = exact_dot(weights[column * rank :, :], far[column * rank : (column + 1) * rank, :], NT)
    at = 0
    for level in range(column, 3):
        panel[at : at + rank, :] = stacked(everyone, source, share) - update[at : at + rank]
        at += rank
        source += share
    panel[at:, :] = stacked(everyone, source, own) - update[at:]


def factor_body(mine, arrived, upper, weights):
    rank = mine.shape[1]
    upper[...] = mine[rank:, :] + arrived[rank:, :]
    inverse = inverse_of(mine[:rank, :] + arrived[:rank, :] + identity(rank))
    weights[...] = exact_dot(upper[...], inverse, NN)


def next_body(later, later_arrived, upper, weights, panel):
    rank = upper.shape[1]
    panel[...] = later[...] + later_arrived[...] - exact_dot(weights[...], upper[:rank, :], NT)


def rest_body(later, later_arrived, upper, weights, rest):
    rank = upper.shape[1]
    rest[...] = later[...] + later_arrived[...] - exact_dot(weights[rank:, :], upper[rank : 2 * rank, :], NT)


def last_panel_body(place, later, later_arrived, upper, weights, panel):
    rank = upper.shape[1]
    own = panel.shape[0] - rank
    rows = pl.ds(pl.multiple_of(rank + place[0] * own, own), own)
    left = jnp.concatenate([weights[:rank, :], weights[rows, :]], 0)
    update = exact_dot(left, upper[:rank, :], NT)
    panel[:rank, :] = later[:rank, :] + later_arrived[:rank, :] - update[:rank]
    panel[rank:, :] = later[rows, :] + later_arrived[rows, :] - update[rank:]


def carry_step(applied, sides, far, side_far, inverse):
    rank = inverse.shape[0]
    gone = applied[:rank]
    sides = sides - exact_dot(exact_dot(side_far, inverse, NN), gone, NN)
    return applied[rank:] - exact_dot(exact_dot(far, inverse, NN), gone, NN), sides


def carry_first_body(send, tree, inverse_cols, far1, inverse1, everyone, far2, inverse2, carried):
    groups = everyone.shape[0]
    share = inverse1.shape[0] // groups
    own = tree.shape[0] // groups
    applied = jnp.concatenate([stacked(send, level * share, share) for level in range(7)], 0)
    sides = exact_dot(tree[...], inverse_cols[...], NN)
    applied, sides = carry_step(applied, sides, far1[...], stacked(everyone, 6 * share + own, own), inverse1[...])
    applied, sides = carry_step(applied, sides, far2[...], stacked(everyone, 6 * share, own), inverse2[...])
    carried[...] = jnp.concatenate([applied, sides], 0)


def carry_body(above, before, everyone, far, inverse, carried):
    groups, _, rank = everyone.shape
    share = rank // groups
    count = (above + 1) * rank
    own = (before.shape[0] - count) // groups
    applied, sides = carry_step(
        before[:count, :], before[count:, :], far[...], stacked(everyone, (above + 1) * share, own), inverse[...]
    )
    carried[...] = jnp.concatenate([applied, sides], 0)


def carry_on_body(before, weights, carried):
    rank = weights.shape[1]
    carried[...] = before[rank:, :] - exact_dot(weights[...], before[:rank, :], NN)


def carry_last_body(before, weights, send):
    groups, rows, _ = send.shape
    rank = weights.shape[1]
    own = rows - rank
    carried = before[rank:, :] - exact_dot(weights[...], before[:rank, :], NN)
    for group in range(groups):
        send[group, :rank, :] = carried[:rank]
        send[group, rank:, :] = carried[rank + group * own : rank + (group + 1) * own]


def finish_body(mine, arrived, got, hot, out):
    rank = mine.shape[1]
    groups = got.shape[0]
    inverse = inverse_of(mine[:rank, :] + arrived[:rank, :] + identity(rank))
    top = exact_dot(mine[rank:, :] + arrived[rank:, :], inverse, NN)
    slope = jnp.concatenate([got[group, :rank, :] for group in range(groups)], 1)
    base = jnp.concatenate([got[group, rank:, :] for group in range(groups)], 1)
    out[...] = dot_left_parts(base - exact_dot(top, slope, NN), hot[...], NT)


def to_all(block, axis):
    count = lax.axis_size(axis)
    return lax.all_to_all(jnp.broadcast_to(block[None], (count,) + block.shape), axis, 0, 0)


def route(height):
    pairs = []
    for leaf in range(128):
        if height in (4, 7):
            low = 1 if height == 4 else 4
            ring = (leaf >> low) & 7
            pairs.append((leaf, leaf & ~(7 << low) | ((ring ^ 6) << low)))
        else:
            pairs.append((leaf, leaf ^ (1 << (height - 1))))
    return pairs


def local(right_sides, leaf_inverse, bases, ordering):
    own, leaf = right_sides.shape
    piece = leaf_inverse.shape[1]
    levels, rank, _ = bases.shape
    groups = lax.axis_size("rhs")
    share = rank // groups
    sides = own * groups
    square = (rank, rank)
    swap = lambda block, height: lax.ppermute(block, "leaf", route(height))

    place = lax.axis_index("rhs").reshape(1)
    send, hot = run_loading(
        start_body,
        [
            (groups, levels * share + sides, piece),
            jax.ShapeDtypeStruct((leaf, leaf), jnp.bfloat16),
        ],
        right_sides,
        ordering,
        leaf_inverse,
        bases,
    )
    got = lax.all_to_all(send, "rhs", 0, 0)
    rows = 28 * share
    gram, tree = run(
        gram_body, [(rows + groups * levels * own, rank), (sides, leaf)], got, send, bases, place=place
    )
    other = swap(gram, 1)
    total = gram + other
    shared = jnp.broadcast_to(total[: 7 * share][None], (groups, 7 * share, rank))
    parts = total[rows:].reshape(groups, levels * own, rank)
    everyone = lax.all_to_all(jnp.concatenate([shared, parts], 1), "rhs", 0, 0)

    panel, far1, own_weights, inverse1, side1 = run(
        first_body,
        [(6 * share + own, rank), (6 * rank, rank), (6 * share + own, rank), square, (own, rank)],
        everyone,
        gram,
        other,
    )
    arrived = swap(panel, 2)
    (later,) = run(
        first_rest_body, [(15 * share + 5 * own, rank)], everyone, gram, other, far1, own_weights
    )
    for height in (2, 3):
        above = 7 - height
        later_arrived = swap(later, height)
        near = panel + arrived
        if height == 2:
            near = jnp.concatenate([near, side1], 0)
        near, later = lax.optimization_barrier((near, later))
        everyone = to_all(near, "rhs")
        next_panel, far, own_weights, inverse = run(
            functools.partial(level_body, above),
            [(above * share + own, rank), (above * rank, rank), (above * share + own, rank), square],
            everyone,
            panel,
            arrived,
            later,
            later_arrived,
        )
        arrived = swap(next_panel, height + 1)
        rest_rows = above * (above - 1) // 2 * share + (above - 1) * own
        (later,) = run(level_rest_body, [(rest_rows, rank)], later, later_arrived, far, own_weights)
        panel = next_panel
        if height == 2:
            (carried,) = run(
                carry_first_body,
                [(5 * rank + sides, piece)],
                send,
                tree,
                leaf_inverse,
                far1,
                inverse1,
                everyone,
                far,
                inverse,
            )
        else:
            (carried,) = run(
                functools.partial(carry_body, above),
                [(4 * rank + sides, piece)],
                carried,
                everyone,
                far,
                inverse,
            )

    later_arrived = swap(later, 4)
    everyone = to_all(jnp.concatenate([panel + arrived, later + later_arrived], 0), "rhs")
    heights = lambda count: (count * rank + sides, rank)
    fifth, upper, weights = run(spread_body, [heights(3)] * 3, everyone)
    arrived = swap(fifth, 5)
    (sixth,) = run(functools.partial(spread_rest_body, 1), [heights(2)], everyone, upper, weights)
    sixth_arrived = swap(sixth, 5)
    everyone, sixth = lax.optimization_barrier((everyone, sixth))
    (seventh,) = run(functools.partial(spread_rest_body, 2), [heights(1)], everyone, upper, weights)
    seventh_arrived = swap(seventh, 5)
    (carried,) = run(carry_on_body, [(3 * rank + sides, piece)], carried, weights)
    upper, weights = run(factor_body, [heights(2)] * 2, fifth, arrived)
    (sixth,) = run(next_body, [heights(2)], sixth, sixth_arrived, upper, weights)
    arrived = swap(sixth, 6)
    sixth, seventh = lax.optimization_barrier((sixth, seventh))
    (seventh,) = run(rest_body, [heights(1)], seventh, seventh_arrived, upper, weights)
    seventh_arrived = swap(seventh, 6)
    (carried,) = run(carry_on_body, [(2 * rank + sides, piece)], carried, weights)
    upper, weights = run(factor_body, [heights(1)] * 2, sixth, arrived)
    (seventh,) = run(
        last_panel_body, [(rank + own, rank)], seventh, seventh_arrived, upper, weights, place=place
    )
    arrived = swap(seventh, 7)
    carried, seventh = lax.optimization_barrier((carried, seventh))
    (send,) = run(carry_last_body, [(groups, rank + own, piece)], carried, weights)
    got = lax.all_to_all(send, "rhs", 0, 0)
    (result,) = run(finish_body, [(own, leaf)], seventh, arrived, got, hot)
    return result


def solution(mesh):
    placed = (P("rhs", "leaf"), P("leaf", "rhs"), P(None, None, "leaf"), P("leaf", None))
    return jax.shard_map(
        local, mesh=mesh, in_specs=placed, out_specs=P("rhs", "leaf"), check_vma=False
    )
```

```python
import functools

import jax
import jax.numpy as jnp
from jax import lax
from jax.experimental import pallas as pl
from jax.experimental.pallas import tpu as pltpu
from jax.sharding import PartitionSpec as P

HIGHEST = lax.Precision.HIGHEST
VMEM_BYTES = 24 * 1024 * 1024
START_BYTES = 60 * 1024 * 1024
NN = (((1,), (0,)), ((), ()))
NT = (((1,), (1,)), ((), ()))


def exact_dot(left, right, dims):
    return lax.dot_general(left, right, dims, precision=HIGHEST, preferred_element_type=jnp.float32)


def short_dot(left, right, dims):
    return lax.dot_general(left, right, dims, preferred_element_type=jnp.float32)


def three_parts(values):
    high = values.astype(jnp.bfloat16)
    rest = values - high.astype(jnp.float32)
    middle = rest.astype(jnp.bfloat16)
    low = (rest - middle.astype(jnp.float32)).astype(jnp.bfloat16)
    return high, middle, low


def dot_left_parts(left, right16, dims):
    high, middle, low = three_parts(left)
    return short_dot(low, right16, dims) + short_dot(middle, right16, dims) + short_dot(high, right16, dims)


def dot_right_parts(left16, right, dims):
    high, middle, low = three_parts(right)
    return short_dot(left16, low, dims) + short_dot(left16, middle, dims) + short_dot(left16, high, dims)


def two_parts(values):
    high = values.astype(jnp.bfloat16)
    return high, (values - high.astype(jnp.float32)).astype(jnp.bfloat16)


def close_dot(left, right):
    left_high, left_low = two_parts(left)
    right_high, right_low = two_parts(right)
    small = short_dot(left_high, right_low, NN) + short_dot(left_low, right_high, NN)
    return small + short_dot(left_high, right_high, NN)


def inverse_of(capacity):
    eye = identity(capacity.shape[0])
    bound = jnp.max(jnp.sum(jnp.abs(capacity), axis=1, keepdims=True), axis=0, keepdims=True)
    scale = 2.0 / (1.0 + bound)
    power = eye - scale * capacity
    series = eye + power
    begin = scale * series
    for _ in range(4):
        power = close_dot(power, power)
        series = series + close_dot(series, power)

    def improve(inverse):
        residual = eye - exact_dot(capacity, inverse, NN)
        size2 = jnp.sum(jnp.sum(residual * residual, axis=1, keepdims=True), axis=0, keepdims=True)
        return inverse + close_dot(inverse, residual), size2

    better, size2 = improve(scale * series)
    better = jnp.where(size2 < 0.25, better, begin)

    def unfinished(state):
        return (state[1] < 80) & jnp.logical_not(state[2] < 1e-6)

    def again(state):
        inverse, size2 = improve(state[0])
        return inverse, state[1] + 1, size2[0, 0]

    return lax.while_loop(unfinished, again, (better, 0, size2[0, 0]))[0]


def shape_of(out):
    return out if isinstance(out, jax.ShapeDtypeStruct) else jax.ShapeDtypeStruct(out, jnp.float32)


def run(body, outs, *args, place=None):
    vmem = pl.BlockSpec(memory_space=pltpu.VMEM)
    scalars = [] if place is None else [place]
    return pl.pallas_call(
        body,
        out_shape=[shape_of(out) for out in outs],
        in_specs=[pl.BlockSpec(memory_space=pltpu.SMEM)] * len(scalars) + [vmem] * len(args),
        out_specs=[vmem] * len(outs),
        cost_estimate=pl.CostEstimate(flops=1_000_000_000, bytes_accessed=0, transcendentals=0),
        compiler_params=pltpu.CompilerParams(vmem_limit_bytes=VMEM_BYTES),
    )(*scalars, *args)


def run_loading(body, outs, *args):
    parts = [arg.shape[0] if arg.ndim == 3 else 1 for arg in args]
    first = [sum(parts[:index]) for index in range(len(parts))]

    def loading(*refs):
        count = len(args)
        sources, rest = refs[:count], refs[count:]
        results, held, done = rest[: len(outs)], rest[len(outs) : -1], rest[-1]

        def copy(index, part):
            source, target = sources[index], held[index]
            if parts[index] > 1:
                source, target = source.at[part], target.at[part]
            return pltpu.make_async_copy(source, target, done.at[first[index] + part])

        for index in range(count):
            for part in range(parts[index]):
                copy(index, part).start()
        body(lambda index, part=0: copy(index, part).wait(), *held, *results)

    return pl.pallas_call(
        loading,
        out_shape=[shape_of(out) for out in outs],
        in_specs=[pl.BlockSpec(memory_space=pltpu.HBM)] * len(args),
        out_specs=[pl.BlockSpec(memory_space=pltpu.VMEM)] * len(outs),
        scratch_shapes=[pltpu.VMEM(arg.shape, arg.dtype) for arg in args]
        + [pltpu.SemaphoreType.DMA((sum(parts),))],
        cost_estimate=pl.CostEstimate(flops=1_000_000_000, bytes_accessed=0, transcendentals=0),
        compiler_params=pltpu.CompilerParams(vmem_limit_bytes=START_BYTES),
    )(*args)


def one_hot(order):
    size = order.shape[1]
    rows = lax.broadcasted_iota(jnp.int32, (size, size), 0)
    return jnp.where(rows == order, 1.0, 0.0).astype(jnp.bfloat16)


def identity(size):
    shape = (size, size)
    return jnp.where(
        lax.broadcasted_iota(jnp.int32, shape, 0) == lax.broadcasted_iota(jnp.int32, shape, 1), 1.0, 0.0
    )


def stacked(everyone, low, count):
    return jnp.concatenate([everyone[group, low : low + count, :] for group in range(everyone.shape[0])], 0)


def start_body(wait, order, sides, inverse_cols, bases, send, hot):
    levels, rank, leaf = bases.shape
    groups, _, piece = send.shape
    share = rank // groups
    own = sides.shape[0]
    wait(0)
    hot[...] = one_hot(order[...])
    wait(1)
    tree = dot_left_parts(sides[...], hot[...], NN)
    for group in range(groups):
        for part in range(groups):
            low = levels * share + part * own
            send[group, low : low + own, :] = tree[:, part * piece : (part + 1) * piece]
    wait(2)
    high, middle, low_part = three_parts(inverse_cols[...])
    for level in range(levels):
        wait(3, level)
        rows = bases[level]
        applied = short_dot(rows, low_part, NN) + short_dot(rows, middle, NN) + short_dot(rows, high, NN)
        for group in range(groups):
            send[group, level * share : (level + 1) * share, :] = applied[group * share : (group + 1) * share]


def gram_body(place, got, send, bases, gram, tree):
    levels, rank, leaf = bases.shape
    groups, rows, piece = got.shape
    share = rank // groups
    v_rows = levels * share
    own = (rows - v_rows) // groups
    applied = jnp.concatenate([got[group, :v_rows, :] for group in range(groups)], 1)
    product = dot_left_parts(applied, bases[...].reshape(levels * rank, leaf), NT)
    at = 0
    for column in range(levels):
        count = (levels - column) * share
        gram[at : at + count, :] = product[column * share :, column * rank : (column + 1) * rank]
        at += count
    mine = pl.ds(pl.multiple_of(v_rows + place[0] * own, own), own)
    sides = jnp.concatenate([got[group, mine, :] for group in range(groups)], 0)
    for level in range(levels):
        block = exact_dot(sides, stacked(send, level * share, share), NT)
        for group in range(groups):
            low = at + (group * levels + level) * own
            gram[low : low + own, :] = block[group * own : (group + 1) * own]
    for group in range(groups):
        tree[group * own : (group + 1) * own, :] = jnp.concatenate(
            [got[group, v_rows + part * own : v_rows + (part + 1) * own, :] for part in range(groups)], 1
        )


def first_body(everyone, mine, arrived, panel, weights, own_weights, inverse, side_upper):
    groups, _, rank = everyone.shape
    share = rank // groups
    own = side_upper.shape[0]
    far = jnp.concatenate([stacked(everyone, level * share, share) for level in range(1, 7)], 0)
    inverse[...] = inverse_of(stacked(everyone, 0, share) + identity(rank))
    side_row = lambda level: sum(
        everyone[group, 7 * share + level * own : 7 * share + (level + 1) * own, :] for group in range(groups)
    )
    side_upper[...] = side_row(0)
    upper = jnp.concatenate([mine[share : 7 * share, :] + arrived[share : 7 * share, :], side_upper[...]], 0)
    own_weights[...] = exact_dot(upper, inverse[...], NN)
    update = exact_dot(own_weights[...], far[:rank], NT)
    panel[: 6 * share, :] = mine[7 * share : 13 * share, :] + arrived[7 * share : 13 * share, :] - update[: 6 * share]
    panel[6 * share :, :] = side_row(1) - update[6 * share :]
    weights[...] = far


def first_rest_body(everyone, mine, arrived, far, own_weights, rest):
    groups, _, rank = everyone.shape
    share = rank // groups
    own = own_weights.shape[0] - 6 * share
    side_row = lambda level: sum(
        everyone[group, 7 * share + level * own : 7 * share + (level + 1) * own, :] for group in range(groups)
    )
    at = 0
    source = 13 * share
    for column in range(2, 7):
        count = (7 - column) * share
        update = exact_dot(own_weights[(column - 1) * share :, :], far[(column - 1) * rank : column * rank, :], NT)
        rest[at : at + count, :] = (
            mine[source : source + count, :] + arrived[source : source + count, :] - update[:count]
        )
        rest[at + count : at + count + own, :] = side_row(column) - update[count:]
        source += count
        at += count + own


def level_body(above, place, everyone, later, later_arrived, panel, far, own_weights, inverse):
    groups, _, rank = everyone.shape
    share = rank // groups
    far[...] = jnp.concatenate([stacked(everyone, level * share, share) for level in range(1, above + 1)], 0)
    inverse[...] = inverse_of(stacked(everyone, 0, share) + identity(rank))
    own_upper = everyone[place[0], share : share + own_weights.shape[0], :]
    own_weights[...] = exact_dot(own_upper, inverse[...], NN)
    count = panel.shape[0]
    panel[...] = later[:count, :] + later_arrived[:count, :] - exact_dot(own_weights[...], far[:rank, :], NT)


def level_all_body(above, place, everyone, later, later_arrived, panels, far, own_weights, inverse):
    groups, _, rank = everyone.shape
    share = rank // groups
    far[...] = jnp.concatenate([stacked(everyone, level * share, share) for level in range(1, above + 1)], 0)
    inverse[...] = inverse_of(stacked(everyone, 0, share) + identity(rank))
    own_upper = everyone[place[0], share : share + own_weights.shape[0], :]
    own_weights[...] = exact_dot(own_upper, inverse[...], NN)
    at = 0
    for column in range(above):
        count = own_weights.shape[0] - column * share
        update = exact_dot(own_weights[column * share :, :], far[column * rank : (column + 1) * rank, :], NT)
        panels[at : at + count, :] = later[at : at + count, :] + later_arrived[at : at + count, :] - update
        at += count


def level_rest_body(later, later_arrived, far, own_weights, rest):
    rank = far.shape[1]
    share = rank // 4
    at = 0
    source = own_weights.shape[0]
    for column in range(1, far.shape[0] // rank):
        count = own_weights.shape[0] - column * share
        update = exact_dot(own_weights[column * share :, :], far[column * rank : (column + 1) * rank, :], NT)
        rest[at : at + count, :] = (
            later[source : source + count, :] + later_arrived[source : source + count, :] - update
        )
        source += count
        at += count


def spread_body(everyone, fifth, far, weights):
    groups, _, rank = everyone.shape
    share = rank // groups
    own = fifth.shape[0] - 3 * rank
    own = own // groups
    blocks = [stacked(everyone, level * share, share) for level in range(4)]
    inverse = inverse_of(blocks[0] + identity(rank))
    far[: 3 * rank, :] = jnp.concatenate(blocks[1:], 0)
    far[3 * rank :, :] = stacked(everyone, 4 * share, own)
    weights[...] = exact_dot(far[...], inverse, NN)
    update = exact_dot(weights[...], far[:rank, :], NT)
    at = 4 * share + own
    for level in range(3):
        fifth[level * rank : (level + 1) * rank, :] = (
            stacked(everyone, at + level * share, share) - update[level * rank : (level + 1) * rank]
        )
    fifth[3 * rank :, :] = stacked(everyone, at + 3 * share, own) - update[3 * rank :]


def spread_rest_body(column, everyone, far, weights, panel):
    groups, _, rank = everyone.shape
    share = rank // groups
    own = (far.shape[0] - 3 * rank) // groups
    source = (7 if column == 1 else 9) * share + (2 if column == 1 else 3) * own
    update = exact_dot(weights[column * rank :, :], far[column * rank : (column + 1) * rank, :], NT)
    at = 0
    for level in range(column, 3):
        panel[at : at + rank, :] = stacked(everyone, source, share) - update[at : at + rank]
        at += rank
        source += share
    panel[at:, :] = stacked(everyone, source, own) - update[at:]


def factor_body(mine, arrived, upper, weights):
    rank = mine.shape[1]
    upper[...] = mine[rank:, :] + arrived[rank:, :]
    inverse = inverse_of(mine[:rank, :] + arrived[:rank, :] + identity(rank))
    weights[...] = exact_dot(upper[...], inverse, NN)


def next_body(later, later_arrived, upper, weights, panel):
    rank = upper.shape[1]
    panel[...] = later[...] + later_arrived[...] - exact_dot(weights[...], upper[:rank, :], NT)


def rest_body(later, later_arrived, upper, weights, rest):
    rank = upper.shape[1]
    rest[...] = later[...] + later_arrived[...] - exact_dot(weights[rank:, :], upper[rank : 2 * rank, :], NT)


def last_panel_body(place, later, later_arrived, upper, weights, panel):
    rank = upper.shape[1]
    own = panel.shape[0] - rank
    rows = pl.ds(pl.multiple_of(rank + place[0] * own, own), own)
    left = jnp.concatenate([weights[:rank, :], weights[rows, :]], 0)
    update = exact_dot(left, upper[:rank, :], NT)
    panel[:rank, :] = later[:rank, :] + later_arrived[:rank, :] - update[:rank]
    panel[rank:, :] = later[rows, :] + later_arrived[rows, :] - update[rank:]


def carry_step(applied, sides, far, side_far, inverse):
    rank = inverse.shape[0]
    gone = applied[:rank]
    sides = sides - exact_dot(exact_dot(side_far, inverse, NN), gone, NN)
    return applied[rank:] - exact_dot(exact_dot(far, inverse, NN), gone, NN), sides


def base_body(tree, inverse_cols, base):
    base[...] = exact_dot(tree[...], inverse_cols[...], NN)


def carry_first_body(send, base, far1, inverse1, everyone, far2, inverse2, carried):
    groups = everyone.shape[0]
    share = inverse1.shape[0] // groups
    own = base.shape[0] // groups
    applied = jnp.concatenate([stacked(send, level * share, share) for level in range(7)], 0)
    sides = base[...]
    applied, sides = carry_step(applied, sides, far1[...], stacked(everyone, 6 * share + own, own), inverse1[...])
    applied, sides = carry_step(applied, sides, far2[...], stacked(everyone, 6 * share, own), inverse2[...])
    carried[...] = jnp.concatenate([applied, sides], 0)


def carry_body(above, before, everyone, far, inverse, carried):
    groups, _, rank = everyone.shape
    share = rank // groups
    count = (above + 1) * rank
    own = (before.shape[0] - count) // groups
    applied, sides = carry_step(
        before[:count, :], before[count:, :], far[...], stacked(everyone, (above + 1) * share, own), inverse[...]
    )
    carried[...] = jnp.concatenate([applied, sides], 0)


def carry_on_body(before, weights, carried):
    rank = weights.shape[1]
    carried[...] = before[rank:, :] - exact_dot(weights[...], before[:rank, :], NN)


def carry_last_body(before, weights, send):
    groups, rows, _ = send.shape
    rank = weights.shape[1]
    own = rows - rank
    carried = before[rank:, :] - exact_dot(weights[...], before[:rank, :], NN)
    for group in range(groups):
        send[group, :rank, :] = carried[:rank]
        send[group, rank:, :] = carried[rank + group * own : rank + (group + 1) * own]


def finish_body(mine, arrived, got, hot, out):
    rank = mine.shape[1]
    groups = got.shape[0]
    inverse = inverse_of(mine[:rank, :] + arrived[:rank, :] + identity(rank))
    top = exact_dot(mine[rank:, :] + arrived[rank:, :], inverse, NN)
    slope = jnp.concatenate([got[group, :rank, :] for group in range(groups)], 1)
    base = jnp.concatenate([got[group, rank:, :] for group in range(groups)], 1)
    out[...] = dot_left_parts(base - exact_dot(top, slope, NN), hot[...], NT)


def add_body(*refs):
    send = refs[-1]
    mine, arrived, others = refs[0], refs[1], refs[2:-1]
    count = mine.shape[0]
    total = mine[...] + arrived[...]
    for group in range(send.shape[0]):
        send[group, :count, :] = total
        for other in others:
            send[group, count:, :] = other[...]


def sum_to_all(mine, arrived, *others):
    groups = lax.axis_size("rhs")
    rows = sum(block.shape[0] for block in (mine,) + others)
    (send,) = run(add_body, [(groups, rows, mine.shape[1])], mine, arrived, *others)
    return lax.all_to_all(send, "rhs", 0, 0)


def route(height):
    pairs = []
    for leaf in range(128):
        if height in (4, 7):
            low = 1 if height == 4 else 4
            ring = (leaf >> low) & 7
            pairs.append((leaf, leaf & ~(7 << low) | ((ring ^ 6) << low)))
        else:
            pairs.append((leaf, leaf ^ (1 << (height - 1))))
    return pairs


def local(right_sides, leaf_inverse, bases, ordering):
    own, leaf = right_sides.shape
    piece = leaf_inverse.shape[1]
    levels, rank, _ = bases.shape
    groups = lax.axis_size("rhs")
    share = rank // groups
    sides = own * groups
    square = (rank, rank)
    swap = lambda block, height: lax.ppermute(block, "leaf", route(height))

    place = lax.axis_index("rhs").reshape(1)
    send, hot = run_loading(
        start_body,
        [
            (groups, levels * share + sides, piece),
            jax.ShapeDtypeStruct((leaf, leaf), jnp.bfloat16),
        ],
        ordering,
        right_sides,
        leaf_inverse,
        bases,
    )
    got = lax.all_to_all(send, "rhs", 0, 0)
    rows = 28 * share
    gram, tree = run(
        gram_body, [(rows + groups * levels * own, rank), (sides, leaf)], got, send, bases, place=place
    )
    other = swap(gram, 1)
    total = gram + other
    shared = jnp.broadcast_to(total[: 7 * share][None], (groups, 7 * share, rank))
    parts = total[rows:].reshape(groups, levels * own, rank)
    everyone = lax.all_to_all(jnp.concatenate([shared, parts], 1), "rhs", 0, 0)

    panel, far1, own_weights, inverse1, side1 = run(
        first_body,
        [(6 * share + own, rank), (6 * rank, rank), (6 * share + own, rank), square, (own, rank)],
        everyone,
        gram,
        other,
    )
    arrived = swap(panel, 2)
    (later,) = run(
        first_rest_body, [(15 * share + 5 * own, rank)], everyone, gram, other, far1, own_weights
    )
    for height in (2, 3):
        above = 7 - height
        later_arrived = swap(later, height)
        arrived, later = lax.optimization_barrier((arrived, later))
        everyone = sum_to_all(panel, arrived, side1) if height == 2 else sum_to_all(panel, arrived)
        if height == 2:
            (base,) = run(base_body, [(sides, piece)], tree, leaf_inverse)
            everyone, base = lax.optimization_barrier((everyone, base))
        else:
            everyone, carried = lax.optimization_barrier((everyone, carried))
        if height == 2:
            next_panel, far, own_weights, inverse = run(
                functools.partial(level_body, above),
                [(above * share + own, rank), (above * rank, rank), (above * share + own, rank), square],
                everyone,
                later,
                later_arrived,
                place=place,
            )
            arrived = swap(next_panel, 3)
            rest_rows = above * (above - 1) // 2 * share + (above - 1) * own
            (later,) = run(level_rest_body, [(rest_rows, rank)], later, later_arrived, far, own_weights)
            panel = next_panel
            (carried,) = run(
                carry_first_body,
                [(5 * rank + sides, piece)],
                send,
                base,
                far1,
                inverse1,
                everyone,
                far,
                inverse,
            )
        else:
            panels, far, _, inverse = run(
                functools.partial(level_all_body, above),
                [
                    (above * (above + 1) // 2 * share + above * own, rank),
                    (above * rank, rank),
                    (above * share + own, rank),
                    square,
                ],
                everyone,
                later,
                later_arrived,
                place=place,
            )
            panels_arrived = swap(panels, 4)
            (carried,) = run(
                functools.partial(carry_body, above),
                [(4 * rank + sides, piece)],
                carried,
                everyone,
                far,
                inverse,
            )
    panels_arrived, carried = lax.optimization_barrier((panels_arrived, carried))
    everyone = sum_to_all(panels, panels_arrived)
    heights = lambda count: (count * rank + sides, rank)
    fifth, upper, weights = run(spread_body, [heights(3)] * 3, everyone)
    arrived = swap(fifth, 5)
    (sixth,) = run(functools.partial(spread_rest_body, 1), [heights(2)], everyone, upper, weights)
    sixth_arrived = swap(sixth, 5)
    everyone, sixth = lax.optimization_barrier((everyone, sixth))
    (seventh,) = run(functools.partial(spread_rest_body, 2), [heights(1)], everyone, upper, weights)
    seventh_arrived = swap(seventh, 5)
    (carried,) = run(carry_on_body, [(3 * rank + sides, piece)], carried, weights)
    upper, weights = run(factor_body, [heights(2)] * 2, fifth, arrived)
    (sixth,) = run(next_body, [heights(2)], sixth, sixth_arrived, upper, weights)
    arrived = swap(sixth, 6)
    sixth, seventh = lax.optimization_barrier((sixth, seventh))
    (seventh,) = run(rest_body, [heights(1)], seventh, seventh_arrived, upper, weights)
    seventh_arrived = swap(seventh, 6)
    (carried,) = run(carry_on_body, [(2 * rank + sides, piece)], carried, weights)
    upper, weights = run(factor_body, [heights(1)] * 2, sixth, arrived)
    (seventh,) = run(
        last_panel_body, [(rank + own, rank)], seventh, seventh_arrived, upper, weights, place=place
    )
    arrived = swap(seventh, 7)
    carried, seventh = lax.optimization_barrier((carried, seventh))
    (send,) = run(carry_last_body, [(groups, rank + own, piece)], carried, weights)
    got = lax.all_to_all(send, "rhs", 0, 0)
    (result,) = run(finish_body, [(own, leaf)], seventh, arrived, got, hot)
    return result


def solution(mesh):
    placed = (P("rhs", "leaf"), P("leaf", "rhs"), P(None, None, "leaf"), P("leaf", None))
    return jax.shard_map(
        local, mesh=mesh, in_specs=placed, out_specs=P("rhs", "leaf"), check_vma=False
    )
```

```python
import functools

import jax
import jax.numpy as jnp
from jax import lax
from jax.experimental import pallas as pl
from jax.experimental.pallas import tpu as pltpu
from jax.sharding import PartitionSpec as P

HIGHEST = lax.Precision.HIGHEST
VMEM_BYTES = 24 * 1024 * 1024
START_BYTES = 60 * 1024 * 1024
NN = (((1,), (0,)), ((), ()))
NT = (((1,), (1,)), ((), ()))


def exact_dot(left, right, dims):
    return lax.dot_general(left, right, dims, precision=HIGHEST, preferred_element_type=jnp.float32)


def short_dot(left, right, dims):
    return lax.dot_general(left, right, dims, preferred_element_type=jnp.float32)


def three_parts(values):
    high = values.astype(jnp.bfloat16)
    rest = values - high.astype(jnp.float32)
    middle = rest.astype(jnp.bfloat16)
    low = (rest - middle.astype(jnp.float32)).astype(jnp.bfloat16)
    return high, middle, low


def dot_left_parts(left, right16, dims):
    high, middle, low = three_parts(left)
    return short_dot(low, right16, dims) + short_dot(middle, right16, dims) + short_dot(high, right16, dims)


def dot_right_parts(left16, right, dims):
    high, middle, low = three_parts(right)
    return short_dot(left16, low, dims) + short_dot(left16, middle, dims) + short_dot(left16, high, dims)


def two_parts(values):
    high = values.astype(jnp.bfloat16)
    return high, (values - high.astype(jnp.float32)).astype(jnp.bfloat16)


def close_dot(left, right):
    left_high, left_low = two_parts(left)
    right_high, right_low = two_parts(right)
    small = short_dot(left_high, right_low, NN) + short_dot(left_low, right_high, NN)
    return small + short_dot(left_high, right_high, NN)


def inverse_of(capacity):
    eye = identity(capacity.shape[0])
    bound = jnp.max(jnp.sum(jnp.abs(capacity), axis=1, keepdims=True), axis=0, keepdims=True)
    scale = 2.0 / (1.0 + bound)
    power = eye - scale * capacity
    series = eye + power
    begin = scale * series
    for _ in range(4):
        power = close_dot(power, power)
        series = series + close_dot(series, power)

    def improve(inverse):
        residual = eye - exact_dot(capacity, inverse, NN)
        size2 = jnp.sum(jnp.sum(residual * residual, axis=1, keepdims=True), axis=0, keepdims=True)
        return inverse + close_dot(inverse, residual), size2

    better, size2 = improve(scale * series)
    better = jnp.where(size2 < 0.25, better, begin)

    def unfinished(state):
        return (state[1] < 80) & jnp.logical_not(state[2] < 1e-6)

    def again(state):
        inverse, size2 = improve(state[0])
        return inverse, state[1] + 1, size2[0, 0]

    return lax.while_loop(unfinished, again, (better, 0, size2[0, 0]))[0]


def shape_of(out):
    return out if isinstance(out, jax.ShapeDtypeStruct) else jax.ShapeDtypeStruct(out, jnp.float32)


def run(body, outs, *args, place=None):
    vmem = pl.BlockSpec(memory_space=pltpu.VMEM)
    scalars = [] if place is None else [place]
    return pl.pallas_call(
        body,
        out_shape=[shape_of(out) for out in outs],
        in_specs=[pl.BlockSpec(memory_space=pltpu.SMEM)] * len(scalars) + [vmem] * len(args),
        out_specs=[vmem] * len(outs),
        cost_estimate=pl.CostEstimate(flops=1_000_000_000, bytes_accessed=0, transcendentals=0),
        compiler_params=pltpu.CompilerParams(vmem_limit_bytes=VMEM_BYTES),
    )(*scalars, *args)


def run_loading(body, outs, *args, place=None):
    parts = [arg.shape[0] if arg.ndim == 3 else 1 for arg in args]
    first = [sum(parts[:index]) for index in range(len(parts))]

    scalars = [] if place is None else [place]

    def loading(*refs):
        count = len(args)
        given, refs = refs[: len(scalars)], refs[len(scalars) :]
        sources, rest = refs[:count], refs[count:]
        results, held, done = rest[: len(outs)], rest[len(outs) : -1], rest[-1]

        def copy(index, part):
            source, target = sources[index], held[index]
            if parts[index] > 1:
                source, target = source.at[part], target.at[part]
            return pltpu.make_async_copy(source, target, done.at[first[index] + part])

        for index in range(count):
            for part in range(parts[index]):
                copy(index, part).start()
        body(lambda index, part=0: copy(index, part).wait(), *given, *held, *results)

    return pl.pallas_call(
        loading,
        out_shape=[shape_of(out) for out in outs],
        in_specs=[pl.BlockSpec(memory_space=pltpu.SMEM)] * len(scalars)
        + [pl.BlockSpec(memory_space=pltpu.HBM)] * len(args),
        out_specs=[pl.BlockSpec(memory_space=pltpu.VMEM)] * len(outs),
        scratch_shapes=[pltpu.VMEM(arg.shape, arg.dtype) for arg in args]
        + [pltpu.SemaphoreType.DMA((sum(parts),))],
        cost_estimate=pl.CostEstimate(flops=1_000_000_000, bytes_accessed=0, transcendentals=0),
        compiler_params=pltpu.CompilerParams(vmem_limit_bytes=START_BYTES),
    )(*scalars, *args)


def one_hot(order):
    size = order.shape[1]
    rows = lax.broadcasted_iota(jnp.int32, (size, size), 0)
    return jnp.where(rows == order, 1.0, 0.0).astype(jnp.bfloat16)


def identity(size):
    shape = (size, size)
    return jnp.where(
        lax.broadcasted_iota(jnp.int32, shape, 0) == lax.broadcasted_iota(jnp.int32, shape, 1), 1.0, 0.0
    )


def stacked(everyone, low, count):
    return jnp.concatenate([everyone[group, low : low + count, :] for group in range(everyone.shape[0])], 0)


def start_body(wait, order, sides, inverse_cols, bases, send, hot):
    levels, rank, leaf = bases.shape
    groups, _, piece = send.shape
    share = rank // groups
    own = sides.shape[0]
    wait(0)
    hot[...] = one_hot(order[...])
    wait(1)
    tree = dot_left_parts(sides[...], hot[...], NN)
    for group in range(groups):
        for part in range(groups):
            low = levels * share + part * own
            send[group, low : low + own, :] = tree[:, part * piece : (part + 1) * piece]
    wait(2)
    high, middle, low_part = three_parts(inverse_cols[...])
    for level in range(levels):
        wait(3, level)
    rows = bases[...].reshape(levels * rank, leaf)
    applied = short_dot(rows, low_part, NN) + short_dot(rows, middle, NN) + short_dot(rows, high, NN)
    for group in range(groups):
        for level in range(levels):
            low = level * rank + group * share
            send[group, level * share : (level + 1) * share, :] = applied[low : low + share]


def gram_body(wait, place, got, bases, send, gram, tree):
    levels, rank, leaf = bases.shape
    groups, rows, piece = got.shape
    share = rank // groups
    v_rows = levels * share
    own = (rows - v_rows) // groups
    for group in range(groups):
        wait(0, group)
    applied = three_parts(jnp.concatenate([got[group, :v_rows, :] for group in range(groups)], 1))
    at = 0
    for column in range(levels):
        count = (levels - column) * share
        wait(1, column)
        high, middle, low = [part[column * share :] for part in applied]
        right = bases[column]
        gram[at : at + count, :] = (
            short_dot(low, right, NT) + short_dot(middle, right, NT) + short_dot(high, right, NT)
        )
        at += count
    for group in range(groups):
        wait(2, group)
    mine = pl.ds(pl.multiple_of(v_rows + place[0] * own, own), own)
    sides = jnp.concatenate([got[group, mine, :] for group in range(groups)], 0)
    for level in range(levels):
        block = exact_dot(sides, stacked(send, level * share, share), NT)
        for group in range(groups):
            low = at + (group * levels + level) * own
            gram[low : low + own, :] = block[group * own : (group + 1) * own]
    for group in range(groups):
        tree[group * own : (group + 1) * own, :] = jnp.concatenate(
            [got[group, v_rows + part * own : v_rows + (part + 1) * own, :] for part in range(groups)], 1
        )


def first_body(everyone, mine, arrived, panel, weights, own_weights, inverse, side_weights):
    groups, _, rank = everyone.shape
    share = rank // groups
    own = side_weights.shape[0]
    far = jnp.concatenate([stacked(everyone, level * share, share) for level in range(1, 7)], 0)
    inverse[...] = inverse_of(stacked(everyone, 0, share) + identity(rank))
    side_row = lambda level: sum(
        everyone[group, 7 * share + level * own : 7 * share + (level + 1) * own, :] for group in range(groups)
    )
    upper = jnp.concatenate([mine[share : 7 * share, :] + arrived[share : 7 * share, :], side_row(0)], 0)
    own_weights[...] = exact_dot(upper, inverse[...], NN)
    side_weights[...] = own_weights[6 * share :, :]
    update = exact_dot(own_weights[...], far[:rank], NT)
    panel[: 6 * share, :] = mine[7 * share : 13 * share, :] + arrived[7 * share : 13 * share, :] - update[: 6 * share]
    panel[6 * share :, :] = side_row(1) - update[6 * share :]
    weights[...] = far


def first_rest_body(everyone, mine, arrived, far, own_weights, inverse, rest, far_weights):
    groups, _, rank = everyone.shape
    share = rank // groups
    own = own_weights.shape[0] - 6 * share
    side_row = lambda level: sum(
        everyone[group, 7 * share + level * own : 7 * share + (level + 1) * own, :] for group in range(groups)
    )
    far_weights[...] = exact_dot(far[...], inverse[...], NN)
    at = 0
    source = 13 * share
    for column in range(2, 7):
        count = (7 - column) * share
        update = exact_dot(own_weights[(column - 1) * share :, :], far[(column - 1) * rank : column * rank, :], NT)
        rest[at : at + count, :] = (
            mine[source : source + count, :] + arrived[source : source + count, :] - update[:count]
        )
        rest[at + count : at + count + own, :] = side_row(column) - update[count:]
        source += count
        at += count + own


def level_body(above, place, everyone, later, later_arrived, panel, far, own_weights, inverse):
    groups, _, rank = everyone.shape
    share = rank // groups
    far[...] = jnp.concatenate([stacked(everyone, level * share, share) for level in range(1, above + 1)], 0)
    inverse[...] = inverse_of(stacked(everyone, 0, share) + identity(rank))
    own_upper = everyone[place[0], share : share + own_weights.shape[0], :]
    own_weights[...] = exact_dot(own_upper, inverse[...], NN)
    count = panel.shape[0]
    panel[...] = later[:count, :] + later_arrived[:count, :] - exact_dot(own_weights[...], far[:rank, :], NT)


def level_all_body(above, place, everyone, later, later_arrived, panels, far, own_weights, inverse):
    groups, _, rank = everyone.shape
    share = rank // groups
    far[...] = jnp.concatenate([stacked(everyone, level * share, share) for level in range(1, above + 1)], 0)
    inverse[...] = inverse_of(stacked(everyone, 0, share) + identity(rank))
    own_upper = everyone[place[0], share : share + own_weights.shape[0], :]
    own_weights[...] = exact_dot(own_upper, inverse[...], NN)
    at = 0
    for column in range(above):
        count = own_weights.shape[0] - column * share
        update = exact_dot(own_weights[column * share :, :], far[column * rank : (column + 1) * rank, :], NT)
        panels[at : at + count, :] = later[at : at + count, :] + later_arrived[at : at + count, :] - update
        at += count


def level_rest_body(everyone, later, later_arrived, far, own_weights, inverse, rest, far_weights, side_weights):
    groups, _, rank = everyone.shape
    share = rank // groups
    above = far.shape[0] // rank
    own = own_weights.shape[0] - above * share
    sides = groups * own
    low = (above + 1) * share
    far_weights[: above * rank, :] = exact_dot(far[...], inverse[...], NN)
    far_weights[above * rank :, :] = exact_dot(stacked(everyone, low, own), inverse[...], NN)
    side_weights[...] = stacked(everyone, low + own, own)
    at = 0
    source = own_weights.shape[0]
    for column in range(1, far.shape[0] // rank):
        count = own_weights.shape[0] - column * share
        update = exact_dot(own_weights[column * share :, :], far[column * rank : (column + 1) * rank, :], NT)
        rest[at : at + count, :] = (
            later[source : source + count, :] + later_arrived[source : source + count, :] - update
        )
        source += count
        at += count


def spread_body(everyone, fifth, far, weights):
    groups, _, rank = everyone.shape
    share = rank // groups
    own = fifth.shape[0] - 3 * rank
    own = own // groups
    blocks = [stacked(everyone, level * share, share) for level in range(4)]
    inverse = inverse_of(blocks[0] + identity(rank))
    far[: 3 * rank, :] = jnp.concatenate(blocks[1:], 0)
    far[3 * rank :, :] = stacked(everyone, 4 * share, own)
    weights[...] = exact_dot(far[...], inverse, NN)
    update = exact_dot(weights[...], far[:rank, :], NT)
    at = 4 * share + own
    for level in range(3):
        fifth[level * rank : (level + 1) * rank, :] = (
            stacked(everyone, at + level * share, share) - update[level * rank : (level + 1) * rank]
        )
    fifth[3 * rank :, :] = stacked(everyone, at + 3 * share, own) - update[3 * rank :]


def spread_rest_body(column, everyone, far, weights, panel):
    groups, _, rank = everyone.shape
    share = rank // groups
    own = (far.shape[0] - 3 * rank) // groups
    source = (7 if column == 1 else 9) * share + (2 if column == 1 else 3) * own
    update = exact_dot(weights[column * rank :, :], far[column * rank : (column + 1) * rank, :], NT)
    at = 0
    for level in range(column, 3):
        panel[at : at + rank, :] = stacked(everyone, source, share) - update[at : at + rank]
        at += rank
        source += share
    panel[at:, :] = stacked(everyone, source, own) - update[at:]


def factor_body(mine, arrived, upper, weights):
    rank = mine.shape[1]
    upper[...] = mine[rank:, :] + arrived[rank:, :]
    inverse = inverse_of(mine[:rank, :] + arrived[:rank, :] + identity(rank))
    weights[...] = exact_dot(upper[...], inverse, NN)


def next_body(later, later_arrived, upper, weights, panel):
    rank = upper.shape[1]
    panel[...] = later[...] + later_arrived[...] - exact_dot(weights[...], upper[:rank, :], NT)


def rest_body(later, later_arrived, upper, weights, rest):
    rank = upper.shape[1]
    rest[...] = later[...] + later_arrived[...] - exact_dot(weights[rank:, :], upper[rank : 2 * rank, :], NT)


def last_panel_body(place, later, later_arrived, upper, weights, panel):
    rank = upper.shape[1]
    own = panel.shape[0] - rank
    rows = pl.ds(pl.multiple_of(rank + place[0] * own, own), own)
    left = jnp.concatenate([weights[:rank, :], weights[rows, :]], 0)
    update = exact_dot(left, upper[:rank, :], NT)
    panel[:rank, :] = later[:rank, :] + later_arrived[:rank, :] - update[:rank]
    panel[rank:, :] = later[rows, :] + later_arrived[rows, :] - update[rank:]


def carry_step(applied, sides, far, side_far, inverse):
    rank = inverse.shape[0]
    gone = applied[:rank]
    sides = sides - exact_dot(exact_dot(side_far, inverse, NN), gone, NN)
    return applied[rank:] - exact_dot(exact_dot(far, inverse, NN), gone, NN), sides


def base_body(tree, inverse_cols, base):
    base[...] = exact_dot(tree[...], inverse_cols[...], NN)


def carry_first_body(send, base, far_weights1, side_weights1, weights2, carried):
    groups = send.shape[0]
    rank = weights2.shape[1]
    share = rank // groups
    applied = [stacked(send, level * share, share) for level in range(7)]
    rest = jnp.concatenate(applied[1:], 0) - exact_dot(far_weights1[...], applied[0], NN)
    sides = base[...] - exact_dot(side_weights1[...], applied[0], NN)
    update = exact_dot(weights2[...], rest[:rank], NN)
    carried[: 5 * rank, :] = rest[rank:] - update[: 5 * rank]
    carried[5 * rank :, :] = sides - update[5 * rank :]


def carry_body(above, before, everyone, far, inverse, carried):
    groups, _, rank = everyone.shape
    share = rank // groups
    count = (above + 1) * rank
    own = (before.shape[0] - count) // groups
    applied, sides = carry_step(
        before[:count, :], before[count:, :], far[...], stacked(everyone, (above + 1) * share, own), inverse[...]
    )
    carried[...] = jnp.concatenate([applied, sides], 0)


def carry_on_body(before, weights, carried):
    rank = weights.shape[1]
    carried[...] = before[rank:, :] - exact_dot(weights[...], before[:rank, :], NN)


def carry_last_body(before, weights, send):
    groups, rows, _ = send.shape
    rank = weights.shape[1]
    own = rows - rank
    carried = before[rank:, :] - exact_dot(weights[...], before[:rank, :], NN)
    for group in range(groups):
        send[group, :rank, :] = carried[:rank]
        send[group, rank:, :] = carried[rank + group * own : rank + (group + 1) * own]


def finish_body(mine, arrived, got, hot, out):
    rank = mine.shape[1]
    groups = got.shape[0]
    inverse = inverse_of(mine[:rank, :] + arrived[:rank, :] + identity(rank))
    top = exact_dot(mine[rank:, :] + arrived[rank:, :], inverse, NN)
    slope = jnp.concatenate([got[group, :rank, :] for group in range(groups)], 1)
    base = jnp.concatenate([got[group, rank:, :] for group in range(groups)], 1)
    out[...] = dot_left_parts(base - exact_dot(top, slope, NN), hot[...], NT)


def add_body(*refs):
    send = refs[-1]
    mine, arrived, others = refs[0], refs[1], refs[2:-1]
    count = mine.shape[0]
    total = mine[...] + arrived[...]
    for group in range(send.shape[0]):
        send[group, :count, :] = total
        for other in others:
            send[group, count:, :] = other[...]


def sum_to_all(mine, arrived, *others):
    groups = lax.axis_size("rhs")
    rows = sum(block.shape[0] for block in (mine,) + others)
    (send,) = run(add_body, [(groups, rows, mine.shape[1])], mine, arrived, *others)
    return lax.all_to_all(send, "rhs", 0, 0)


def route(height):
    pairs = []
    for leaf in range(128):
        if height in (4, 7):
            low = 1 if height == 4 else 4
            ring = (leaf >> low) & 7
            pairs.append((leaf, leaf & ~(7 << low) | ((ring ^ 6) << low)))
        else:
            pairs.append((leaf, leaf ^ (1 << (height - 1))))
    return pairs


def local(right_sides, leaf_inverse, bases, ordering):
    own, leaf = right_sides.shape
    piece = leaf_inverse.shape[1]
    levels, rank, _ = bases.shape
    groups = lax.axis_size("rhs")
    share = rank // groups
    sides = own * groups
    square = (rank, rank)
    swap = lambda block, height: lax.ppermute(block, "leaf", route(height))

    place = lax.axis_index("rhs").reshape(1)
    send, hot = run_loading(
        start_body,
        [
            (groups, levels * share + sides, piece),
            jax.ShapeDtypeStruct((leaf, leaf), jnp.bfloat16),
        ],
        ordering,
        right_sides,
        leaf_inverse,
        bases,
    )
    got = lax.all_to_all(send, "rhs", 0, 0)
    rows = 28 * share
    gram, tree = run_loading(
        gram_body, [(rows + groups * levels * own, rank), (sides, leaf)], got, bases, send, place=place
    )
    other = swap(gram, 1)
    total = gram + other
    shared = jnp.broadcast_to(total[: 7 * share][None], (groups, 7 * share, rank))
    parts = total[rows:].reshape(groups, levels * own, rank)
    everyone = lax.all_to_all(jnp.concatenate([shared, parts], 1), "rhs", 0, 0)

    panel, far1, own_weights, inverse1, side1 = run(
        first_body,
        [(6 * share + own, rank), (6 * rank, rank), (6 * share + own, rank), square, (own, rank)],
        everyone,
        gram,
        other,
    )
    arrived = swap(panel, 2)
    later, far_weights1 = run(
        first_rest_body,
        [(15 * share + 5 * own, rank), (6 * rank, rank)],
        everyone,
        gram,
        other,
        far1,
        own_weights,
        inverse1,
    )
    for height in (2, 3):
        above = 7 - height
        later_arrived = swap(later, height)
        arrived, later = lax.optimization_barrier((arrived, later))
        everyone = sum_to_all(panel, arrived, side1) if height == 2 else sum_to_all(panel, arrived)
        if height == 2:
            (base,) = run(base_body, [(sides, piece)], tree, leaf_inverse)
            everyone, base = lax.optimization_barrier((everyone, base))
        else:
            everyone, carried = lax.optimization_barrier((everyone, carried))
        if height == 2:
            next_panel, far, own_weights, inverse = run(
                functools.partial(level_body, above),
                [(above * share + own, rank), (above * rank, rank), (above * share + own, rank), square],
                everyone,
                later,
                later_arrived,
                place=place,
            )
            arrived = swap(next_panel, 3)
            rest_rows = above * (above - 1) // 2 * share + (above - 1) * own
            later, far_weights2, side_weights1 = run(
                level_rest_body,
                [(rest_rows, rank), (above * rank + sides, rank), (sides, rank)],
                everyone,
                later,
                later_arrived,
                far,
                own_weights,
                inverse,
            )
            panel = next_panel
            (carried,) = run(
                carry_first_body,
                [(5 * rank + sides, piece)],
                send,
                base,
                far_weights1,
                side_weights1,
                far_weights2,
            )
        else:
            panels, far, _, inverse = run(
                functools.partial(level_all_body, above),
                [
                    (above * (above + 1) // 2 * share + above * own, rank),
                    (above * rank, rank),
                    (above * share + own, rank),
                    square,
                ],
                everyone,
                later,
                later_arrived,
                place=place,
            )
            panels_arrived = swap(panels, 4)
            (carried,) = run(
                functools.partial(carry_body, above),
                [(4 * rank + sides, piece)],
                carried,
                everyone,
                far,
                inverse,
            )
    panels_arrived, carried = lax.optimization_barrier((panels_arrived, carried))
    everyone = sum_to_all(panels, panels_arrived)
    heights = lambda count: (count * rank + sides, rank)
    fifth, upper, weights = run(spread_body, [heights(3)] * 3, everyone)
    arrived = swap(fifth, 5)
    (sixth,) = run(functools.partial(spread_rest_body, 1), [heights(2)], everyone, upper, weights)
    sixth_arrived = swap(sixth, 5)
    everyone, sixth = lax.optimization_barrier((everyone, sixth))
    (seventh,) = run(functools.partial(spread_rest_body, 2), [heights(1)], everyone, upper, weights)
    seventh_arrived = swap(seventh, 5)
    (carried,) = run(carry_on_body, [(3 * rank + sides, piece)], carried, weights)
    upper, weights = run(factor_body, [heights(2)] * 2, fifth, arrived)
    (sixth,) = run(next_body, [heights(2)], sixth, sixth_arrived, upper, weights)
    arrived = swap(sixth, 6)
    sixth, seventh = lax.optimization_barrier((sixth, seventh))
    (seventh,) = run(rest_body, [heights(1)], seventh, seventh_arrived, upper, weights)
    seventh_arrived = swap(seventh, 6)
    (carried,) = run(carry_on_body, [(2 * rank + sides, piece)], carried, weights)
    upper, weights = run(factor_body, [heights(1)] * 2, sixth, arrived)
    (seventh,) = run(
        last_panel_body, [(rank + own, rank)], seventh, seventh_arrived, upper, weights, place=place
    )
    arrived = swap(seventh, 7)
    carried, seventh = lax.optimization_barrier((carried, seventh))
    (send,) = run(carry_last_body, [(groups, rank + own, piece)], carried, weights)
    got = lax.all_to_all(send, "rhs", 0, 0)
    (result,) = run(finish_body, [(own, leaf)], seventh, arrived, got, hot)
    return result


def solution(mesh):
    placed = (P("rhs", "leaf"), P("leaf", "rhs"), P(None, None, "leaf"), P("leaf", None))
    return jax.shard_map(
        local, mesh=mesh, in_specs=placed, out_specs=P("rhs", "leaf"), check_vma=False
    )
```

```python
import functools

import jax
import jax.numpy as jnp
from jax import lax
from jax.experimental import pallas as pl
from jax.experimental.pallas import tpu as pltpu
from jax.sharding import PartitionSpec as P

HIGHEST = lax.Precision.HIGHEST
VMEM_BYTES = 24 * 1024 * 1024
START_BYTES = 60 * 1024 * 1024
NN = (((1,), (0,)), ((), ()))
NT = (((1,), (1,)), ((), ()))


def exact_dot(left, right, dims):
    return lax.dot_general(left, right, dims, precision=HIGHEST, preferred_element_type=jnp.float32)


def short_dot(left, right, dims):
    return lax.dot_general(left, right, dims, preferred_element_type=jnp.float32)


def three_parts(values):
    high = values.astype(jnp.bfloat16)
    rest = values - high.astype(jnp.float32)
    middle = rest.astype(jnp.bfloat16)
    low = (rest - middle.astype(jnp.float32)).astype(jnp.bfloat16)
    return high, middle, low


def dot_left_parts(left, right16, dims):
    high, middle, low = three_parts(left)
    return short_dot(low, right16, dims) + short_dot(middle, right16, dims) + short_dot(high, right16, dims)


def dot_right_parts(left16, right, dims):
    high, middle, low = three_parts(right)
    return short_dot(left16, low, dims) + short_dot(left16, middle, dims) + short_dot(left16, high, dims)


def two_parts(values):
    high = values.astype(jnp.bfloat16)
    return high, (values - high.astype(jnp.float32)).astype(jnp.bfloat16)


def close_dot(left, right):
    left_high, left_low = two_parts(left)
    right_high, right_low = two_parts(right)
    small = short_dot(left_high, right_low, NN) + short_dot(left_low, right_high, NN)
    return small + short_dot(left_high, right_high, NN)


def inverse_of(capacity):
    eye = identity(capacity.shape[0])
    bound = jnp.max(jnp.sum(jnp.abs(capacity), axis=1, keepdims=True), axis=0, keepdims=True)
    scale = 2.0 / (1.0 + bound)
    power = eye - scale * capacity
    series = eye + power
    begin = scale * series
    for _ in range(4):
        power = close_dot(power, power)
        series = series + close_dot(series, power)

    def improve(inverse):
        residual = eye - exact_dot(capacity, inverse, NN)
        size2 = jnp.sum(jnp.sum(residual * residual, axis=1, keepdims=True), axis=0, keepdims=True)
        return inverse + close_dot(inverse, residual), size2

    better, size2 = improve(scale * series)
    better = jnp.where(size2 < 0.25, better, begin)

    def unfinished(state):
        return (state[1] < 80) & jnp.logical_not(state[2] < 1e-6)

    def again(state):
        inverse, size2 = improve(state[0])
        return inverse, state[1] + 1, size2[0, 0]

    return lax.while_loop(unfinished, again, (better, 0, size2[0, 0]))[0]


def shape_of(out):
    return out if isinstance(out, jax.ShapeDtypeStruct) else jax.ShapeDtypeStruct(out, jnp.float32)


def run(body, outs, *args, place=None):
    vmem = pl.BlockSpec(memory_space=pltpu.VMEM)
    scalars = [] if place is None else [place]
    return pl.pallas_call(
        body,
        out_shape=[shape_of(out) for out in outs],
        in_specs=[pl.BlockSpec(memory_space=pltpu.SMEM)] * len(scalars) + [vmem] * len(args),
        out_specs=[vmem] * len(outs),
        cost_estimate=pl.CostEstimate(flops=1_000_000_000, bytes_accessed=0, transcendentals=0),
        compiler_params=pltpu.CompilerParams(vmem_limit_bytes=VMEM_BYTES),
    )(*scalars, *args)


def run_loading(body, outs, *args, place=None):
    parts = [arg.shape[0] if arg.ndim == 3 else 1 for arg in args]
    first = [sum(parts[:index]) for index in range(len(parts))]

    scalars = [] if place is None else [place]

    def loading(*refs):
        count = len(args)
        given, refs = refs[: len(scalars)], refs[len(scalars) :]
        sources, rest = refs[:count], refs[count:]
        results, held, done = rest[: len(outs)], rest[len(outs) : -1], rest[-1]

        def copy(index, part):
            source, target = sources[index], held[index]
            if parts[index] > 1:
                source, target = source.at[part], target.at[part]
            return pltpu.make_async_copy(source, target, done.at[first[index] + part])

        for index in range(count):
            for part in range(parts[index]):
                copy(index, part).start()
        body(lambda index, part=0: copy(index, part).wait(), *given, *held, *results)

    return pl.pallas_call(
        loading,
        out_shape=[shape_of(out) for out in outs],
        in_specs=[pl.BlockSpec(memory_space=pltpu.SMEM)] * len(scalars)
        + [pl.BlockSpec(memory_space=pltpu.HBM)] * len(args),
        out_specs=[pl.BlockSpec(memory_space=pltpu.VMEM)] * len(outs),
        scratch_shapes=[pltpu.VMEM(arg.shape, arg.dtype) for arg in args]
        + [pltpu.SemaphoreType.DMA((sum(parts),))],
        cost_estimate=pl.CostEstimate(flops=1_000_000_000, bytes_accessed=0, transcendentals=0),
        compiler_params=pltpu.CompilerParams(vmem_limit_bytes=START_BYTES),
    )(*scalars, *args)


def one_hot(order):
    size = order.shape[1]
    rows = lax.broadcasted_iota(jnp.int32, (size, size), 0)
    return jnp.where(rows == order, 1.0, 0.0).astype(jnp.bfloat16)


def identity(size):
    shape = (size, size)
    return jnp.where(
        lax.broadcasted_iota(jnp.int32, shape, 0) == lax.broadcasted_iota(jnp.int32, shape, 1), 1.0, 0.0
    )


def stacked(everyone, low, count):
    return jnp.concatenate([everyone[group, low : low + count, :] for group in range(everyone.shape[0])], 0)


def start_body(wait, order, sides, inverse_cols, bases, send, hot, tree):
    levels, rank, leaf = bases.shape
    groups, _, piece = send.shape
    share = rank // groups
    own = sides.shape[0]
    wait(0)
    hot[...] = one_hot(order[...])
    wait(1)
    ordered = dot_left_parts(sides[...], hot[...], NN)
    for group in range(groups):
        send[group, levels * share :, :] = ordered[:, group * piece : (group + 1) * piece]
    for part in range(leaf // rank):
        tree[part * own : (part + 1) * own, :] = ordered[:, part * rank : (part + 1) * rank]
    wait(2)
    high, middle, low_part = three_parts(inverse_cols[...])
    for level in range(levels):
        wait(3, level)
    rows = bases[...].reshape(levels * rank, leaf)
    applied = short_dot(rows, low_part, NN) + short_dot(rows, middle, NN) + short_dot(rows, high, NN)
    for group in range(groups):
        for level in range(levels):
            low = level * rank + group * share
            send[group, level * share : (level + 1) * share, :] = applied[low : low + share]


def gram_body(got, send, bases, gram):
    levels, rank, leaf = bases.shape
    groups, rows, piece = got.shape
    share = rank // groups
    own = rows - levels * share
    applied = three_parts(jnp.concatenate([got[group, : levels * share, :] for group in range(groups)], 1))
    at = 0
    for column in range(levels):
        count = (levels - column) * share
        high, middle, low = [part[column * share :] for part in applied]
        right = bases[column]
        gram[at : at + count, :] = (
            short_dot(low, right, NT) + short_dot(middle, right, NT) + short_dot(high, right, NT)
        )
        at += count
    sides = stacked(got, levels * share, own)
    for level in range(levels):
        block = exact_dot(sides, stacked(send, level * share, share), NT)
        for group in range(groups):
            low = at + (group * levels + level) * own
            gram[low : low + own, :] = block[group * own : (group + 1) * own]


def first_body(everyone, mine, arrived, panel, weights, own_weights, inverse, side_weights):
    groups, _, rank = everyone.shape
    share = rank // groups
    own = side_weights.shape[0]
    far = jnp.concatenate([stacked(everyone, level * share, share) for level in range(1, 7)], 0)
    inverse[...] = inverse_of(stacked(everyone, 0, share) + identity(rank))
    side_row = lambda level: sum(
        everyone[group, 7 * share + level * own : 7 * share + (level + 1) * own, :] for group in range(groups)
    )
    upper = jnp.concatenate([mine[share : 7 * share, :] + arrived[share : 7 * share, :], side_row(0)], 0)
    own_weights[...] = exact_dot(upper, inverse[...], NN)
    side_weights[...] = own_weights[6 * share :, :]
    update = exact_dot(own_weights[...], far[:rank], NT)
    panel[: 6 * share, :] = mine[7 * share : 13 * share, :] + arrived[7 * share : 13 * share, :] - update[: 6 * share]
    panel[6 * share :, :] = side_row(1) - update[6 * share :]
    weights[...] = far


def first_rest_body(everyone, mine, arrived, far, own_weights, inverse, rest, far_weights):
    groups, _, rank = everyone.shape
    share = rank // groups
    own = own_weights.shape[0] - 6 * share
    side_row = lambda level: sum(
        everyone[group, 7 * share + level * own : 7 * share + (level + 1) * own, :] for group in range(groups)
    )
    far_weights[...] = exact_dot(far[...], inverse[...], NN)
    at = 0
    source = 13 * share
    for column in range(2, 7):
        count = (7 - column) * share
        update = exact_dot(own_weights[(column - 1) * share :, :], far[(column - 1) * rank : column * rank, :], NT)
        rest[at : at + count, :] = (
            mine[source : source + count, :] + arrived[source : source + count, :] - update[:count]
        )
        rest[at + count : at + count + own, :] = side_row(column) - update[count:]
        source += count
        at += count + own


def level_body(above, place, everyone, later, later_arrived, panel, far, own_weights, inverse):
    groups, _, rank = everyone.shape
    share = rank // groups
    far[...] = jnp.concatenate([stacked(everyone, level * share, share) for level in range(1, above + 1)], 0)
    inverse[...] = inverse_of(stacked(everyone, 0, share) + identity(rank))
    own_upper = everyone[place[0], share : share + own_weights.shape[0], :]
    own_weights[...] = exact_dot(own_upper, inverse[...], NN)
    count = panel.shape[0]
    panel[...] = later[:count, :] + later_arrived[:count, :] - exact_dot(own_weights[...], far[:rank, :], NT)


def level_factor_body(above, place, everyone, far, own_weights, inverse):
    groups, _, rank = everyone.shape
    share = rank // groups
    far[...] = jnp.concatenate([stacked(everyone, level * share, share) for level in range(1, above + 1)], 0)
    inverse[...] = inverse_of(stacked(everyone, 0, share) + identity(rank))
    own_upper = everyone[place[0], share : share + own_weights.shape[0], :]
    own_weights[...] = exact_dot(own_upper, inverse[...], NN)


def level_all_body(above, later, later_arrived, far, own_weights, panels):
    rank = far.shape[1]
    share = rank // 4
    at = 0
    for column in range(above):
        count = own_weights.shape[0] - column * share
        update = exact_dot(own_weights[column * share :, :], far[column * rank : (column + 1) * rank, :], NT)
        panels[at : at + count, :] = later[at : at + count, :] + later_arrived[at : at + count, :] - update
        at += count


def level_rest_body(everyone, later, later_arrived, far, own_weights, inverse, rest, far_weights, side_weights):
    groups, _, rank = everyone.shape
    share = rank // groups
    above = far.shape[0] // rank
    own = own_weights.shape[0] - above * share
    sides = groups * own
    low = (above + 1) * share
    far_weights[...] = exact_dot(far[...], inverse[...], NN)
    side_weights[:sides, :] = stacked(everyone, low + own, own)
    side_weights[sides:, :] = exact_dot(stacked(everyone, low, own), inverse[...], NN)
    at = 0
    source = own_weights.shape[0]
    for column in range(1, far.shape[0] // rank):
        count = own_weights.shape[0] - column * share
        update = exact_dot(own_weights[column * share :, :], far[column * rank : (column + 1) * rank, :], NT)
        rest[at : at + count, :] = (
            later[source : source + count, :] + later_arrived[source : source + count, :] - update
        )
        source += count
        at += count


def spread_body(everyone, fifth, far, weights):
    groups, _, rank = everyone.shape
    share = rank // groups
    own = fifth.shape[0] - 3 * rank
    own = own // groups
    blocks = [stacked(everyone, level * share, share) for level in range(4)]
    inverse = inverse_of(blocks[0] + identity(rank))
    far[: 3 * rank, :] = jnp.concatenate(blocks[1:], 0)
    far[3 * rank :, :] = stacked(everyone, 4 * share, own)
    weights[...] = exact_dot(far[...], inverse, NN)
    update = exact_dot(weights[...], far[:rank, :], NT)
    at = 4 * share + own
    for level in range(3):
        fifth[level * rank : (level + 1) * rank, :] = (
            stacked(everyone, at + level * share, share) - update[level * rank : (level + 1) * rank]
        )
    fifth[3 * rank :, :] = stacked(everyone, at + 3 * share, own) - update[3 * rank :]


def spread_rest_body(column, everyone, far, weights, panel):
    groups, _, rank = everyone.shape
    share = rank // groups
    own = (far.shape[0] - 3 * rank) // groups
    source = (7 if column == 1 else 9) * share + (2 if column == 1 else 3) * own
    update = exact_dot(weights[column * rank :, :], far[column * rank : (column + 1) * rank, :], NT)
    at = 0
    for level in range(column, 3):
        panel[at : at + rank, :] = stacked(everyone, source, share) - update[at : at + rank]
        at += rank
        source += share
    panel[at:, :] = stacked(everyone, source, own) - update[at:]


def factor_body(mine, arrived, upper, weights):
    rank = mine.shape[1]
    upper[...] = mine[rank:, :] + arrived[rank:, :]
    inverse = inverse_of(mine[:rank, :] + arrived[:rank, :] + identity(rank))
    weights[...] = exact_dot(upper[...], inverse, NN)


def next_body(later, later_arrived, upper, weights, panel):
    rank = upper.shape[1]
    panel[...] = later[...] + later_arrived[...] - exact_dot(weights[...], upper[:rank, :], NT)


def rest_body(later, later_arrived, upper, weights, rest):
    rank = upper.shape[1]
    rest[...] = later[...] + later_arrived[...] - exact_dot(weights[rank:, :], upper[rank : 2 * rank, :], NT)


def last_panel_body(place, later, later_arrived, upper, weights, panel):
    rank = upper.shape[1]
    own = panel.shape[0] - rank
    rows = pl.ds(pl.multiple_of(rank + place[0] * own, own), own)
    left = jnp.concatenate([weights[:rank, :], weights[rows, :]], 0)
    update = exact_dot(left, upper[:rank, :], NT)
    panel[:rank, :] = later[:rank, :] + later_arrived[:rank, :] - update[:rank]
    panel[rank:, :] = later[rows, :] + later_arrived[rows, :] - update[rank:]


def carry_step(applied, sides, far, side_far, inverse):
    rank = inverse.shape[0]
    gone = applied[:rank]
    sides = sides - exact_dot(exact_dot(side_far, inverse, NN), gone, NN)
    return applied[rank:] - exact_dot(exact_dot(far, inverse, NN), gone, NN), sides


def carry_first_body(send, weights1, weights2, carried, gone):
    groups = send.shape[0]
    rank = weights2.shape[1]
    share = rank // groups
    applied = [stacked(send, level * share, share) for level in range(7)]
    rest = jnp.concatenate(applied[1:], 0) - exact_dot(weights1[...], applied[0], NN)
    carried[...] = rest[rank:] - exact_dot(weights2[...], rest[:rank], NN)
    gone[:rank, :] = applied[0]
    gone[rank:, :] = rest[:rank]


def carry_body(above, before, gone, side_weights, everyone, far, inverse, inverse_cols, carried):
    groups, rows, rank = everyone.shape
    share = rank // groups
    low = (above + 1) * share
    sides = side_weights.shape[0] // 2
    own = sides // groups
    parts = (rows - low - own) // own
    tree = jnp.concatenate(
        [stacked(everyone, low + own + part * own, own) for part in range(parts)], 1
    )
    found = exact_dot(tree, inverse_cols[...], NN)
    for place in range(2):
        weights = side_weights[place * sides : (place + 1) * sides, :]
        found = found - exact_dot(weights, gone[place * rank : (place + 1) * rank, :], NN)
    applied, found = carry_step(before[...], found, far[...], stacked(everyone, low, own), inverse[...])
    carried[: above * rank, :] = applied
    carried[above * rank :, :] = found


def carry_on_body(before, weights, carried):
    rank = weights.shape[1]
    carried[...] = before[rank:, :] - exact_dot(weights[...], before[:rank, :], NN)


def carry_last_body(before, weights, send):
    groups, rows, _ = send.shape
    rank = weights.shape[1]
    own = rows - rank
    carried = before[rank:, :] - exact_dot(weights[...], before[:rank, :], NN)
    for group in range(groups):
        send[group, :rank, :] = carried[:rank]
        send[group, rank:, :] = carried[rank + group * own : rank + (group + 1) * own]


def finish_body(mine, arrived, got, hot, out):
    rank = mine.shape[1]
    groups = got.shape[0]
    inverse = inverse_of(mine[:rank, :] + arrived[:rank, :] + identity(rank))
    top = exact_dot(mine[rank:, :] + arrived[rank:, :], inverse, NN)
    slope = jnp.concatenate([got[group, :rank, :] for group in range(groups)], 1)
    base = jnp.concatenate([got[group, rank:, :] for group in range(groups)], 1)
    out[...] = dot_left_parts(base - exact_dot(top, slope, NN), hot[...], NT)


def add_body(*refs):
    send = refs[-1]
    mine, arrived, others = refs[0], refs[1], refs[2:-1]
    count = mine.shape[0]
    total = mine[...] + arrived[...]
    for group in range(send.shape[0]):
        send[group, :count, :] = total
        for other in others:
            send[group, count : count + other.shape[0], :] = other[...]


def sum_to_all(mine, arrived, *others):
    groups = lax.axis_size("rhs")
    rows = sum(block.shape[0] for block in (mine,) + others)
    (send,) = run(add_body, [(groups, rows, mine.shape[1])], mine, arrived, *others)
    return lax.all_to_all(send, "rhs", 0, 0)


def route(height):
    pairs = []
    for leaf in range(128):
        if height in (4, 7):
            low = 1 if height == 4 else 4
            ring = (leaf >> low) & 7
            pairs.append((leaf, leaf & ~(7 << low) | ((ring ^ 6) << low)))
        else:
            pairs.append((leaf, leaf ^ (1 << (height - 1))))
    return pairs


def local(right_sides, leaf_inverse, bases, ordering):
    own, leaf = right_sides.shape
    piece = leaf_inverse.shape[1]
    levels, rank, _ = bases.shape
    groups = lax.axis_size("rhs")
    share = rank // groups
    sides = own * groups
    square = (rank, rank)
    swap = lambda block, height: lax.ppermute(block, "leaf", route(height))

    place = lax.axis_index("rhs").reshape(1)
    send, hot, tree = run_loading(
        start_body,
        [
            (groups, levels * share + own, piece),
            jax.ShapeDtypeStruct((leaf, leaf), jnp.bfloat16),
            (leaf // rank * own, rank),
        ],
        ordering,
        right_sides,
        leaf_inverse,
        bases,
    )
    got = lax.all_to_all(send, "rhs", 0, 0)
    rows = 28 * share
    (gram,) = run(gram_body, [(rows + groups * levels * own, rank)], got, send, bases)
    other = swap(gram, 1)
    total = gram + other
    shared = jnp.broadcast_to(total[: 7 * share][None], (groups, 7 * share, rank))
    parts = total[rows:].reshape(groups, levels * own, rank)
    everyone = lax.all_to_all(jnp.concatenate([shared, parts], 1), "rhs", 0, 0)

    panel, far1, own_weights, inverse1, side1 = run(
        first_body,
        [(6 * share + own, rank), (6 * rank, rank), (6 * share + own, rank), square, (own, rank)],
        everyone,
        gram,
        other,
    )
    arrived = swap(panel, 2)
    later, far_weights1 = run(
        first_rest_body,
        [(15 * share + 5 * own, rank), (6 * rank, rank)],
        everyone,
        gram,
        other,
        far1,
        own_weights,
        inverse1,
    )
    for height in (2, 3):
        above = 7 - height
        later_arrived = swap(later, height)
        arrived, later = lax.optimization_barrier((arrived, later))
        everyone = sum_to_all(panel, arrived, side1) if height == 2 else sum_to_all(panel, arrived, tree)
        if height == 3:
            everyone, carried = lax.optimization_barrier((everyone, carried))
        if height == 2:
            next_panel, far, own_weights, inverse = run(
                functools.partial(level_body, above),
                [(above * share + own, rank), (above * rank, rank), (above * share + own, rank), square],
                everyone,
                later,
                later_arrived,
                place=place,
            )
            arrived = swap(next_panel, 3)
            rest_rows = above * (above - 1) // 2 * share + (above - 1) * own
            later, far_weights2, side_weights = run(
                level_rest_body,
                [(rest_rows, rank), (above * rank, rank), (2 * sides, rank)],
                everyone,
                later,
                later_arrived,
                far,
                own_weights,
                inverse,
            )
            panel = next_panel
            carried, gone = run(
                carry_first_body,
                [(5 * rank, piece), (2 * rank, piece)],
                send,
                far_weights1,
                far_weights2,
            )
        else:
            far, own_weights, inverse = run(
                functools.partial(level_factor_body, above),
                [(above * rank, rank), (above * share + own, rank), square],
                everyone,
                place=place,
            )
            (panels,) = run(
                functools.partial(level_all_body, above),
                [(above * (above + 1) // 2 * share + above * own, rank)],
                later,
                later_arrived,
                far,
                own_weights,
            )
            panels_arrived = swap(panels, 4)
            (carried,) = run(
                functools.partial(carry_body, above),
                [(4 * rank + sides, piece)],
                carried,
                gone,
                side_weights,
                everyone,
                far,
                inverse,
                leaf_inverse,
            )
    panels_arrived, carried = lax.optimization_barrier((panels_arrived, carried))
    everyone = sum_to_all(panels, panels_arrived)
    heights = lambda count: (count * rank + sides, rank)
    fifth, upper, weights = run(spread_body, [heights(3)] * 3, everyone)
    arrived = swap(fifth, 5)
    (sixth,) = run(functools.partial(spread_rest_body, 1), [heights(2)], everyone, upper, weights)
    sixth_arrived = swap(sixth, 5)
    everyone, sixth = lax.optimization_barrier((everyone, sixth))
    (seventh,) = run(functools.partial(spread_rest_body, 2), [heights(1)], everyone, upper, weights)
    seventh_arrived = swap(seventh, 5)
    (carried,) = run(carry_on_body, [(3 * rank + sides, piece)], carried, weights)
    upper, weights = run(factor_body, [heights(2)] * 2, fifth, arrived)
    (sixth,) = run(next_body, [heights(2)], sixth, sixth_arrived, upper, weights)
    arrived = swap(sixth, 6)
    sixth, seventh = lax.optimization_barrier((sixth, seventh))
    (seventh,) = run(rest_body, [heights(1)], seventh, seventh_arrived, upper, weights)
    seventh_arrived = swap(seventh, 6)
    (carried,) = run(carry_on_body, [(2 * rank + sides, piece)], carried, weights)
    upper, weights = run(factor_body, [heights(1)] * 2, sixth, arrived)
    (seventh,) = run(
        last_panel_body, [(rank + own, rank)], seventh, seventh_arrived, upper, weights, place=place
    )
    arrived = swap(seventh, 7)
    carried, seventh = lax.optimization_barrier((carried, seventh))
    (send,) = run(carry_last_body, [(groups, rank + own, piece)], carried, weights)
    got = lax.all_to_all(send, "rhs", 0, 0)
    (result,) = run(finish_body, [(own, leaf)], seventh, arrived, got, hot)
    return result


def solution(mesh):
    placed = (P("rhs", "leaf"), P("leaf", "rhs"), P(None, None, "leaf"), P("leaf", None))
    return jax.shard_map(
        local, mesh=mesh, in_specs=placed, out_specs=P("rhs", "leaf"), check_vma=False
    )
```

```python
import functools

import jax
import jax.numpy as jnp
from jax import lax
from jax.experimental import pallas as pl
from jax.experimental.pallas import tpu as pltpu
from jax.sharding import PartitionSpec as P

HIGHEST = lax.Precision.HIGHEST
VMEM_BYTES = 24 * 1024 * 1024
START_BYTES = 60 * 1024 * 1024
NN = (((1,), (0,)), ((), ()))
NT = (((1,), (1,)), ((), ()))


def exact_dot(left, right, dims):
    return lax.dot_general(left, right, dims, precision=HIGHEST, preferred_element_type=jnp.float32)


def short_dot(left, right, dims):
    return lax.dot_general(left, right, dims, preferred_element_type=jnp.float32)


def three_parts(values):
    high = values.astype(jnp.bfloat16)
    rest = values - high.astype(jnp.float32)
    middle = rest.astype(jnp.bfloat16)
    low = (rest - middle.astype(jnp.float32)).astype(jnp.bfloat16)
    return high, middle, low


def dot_left_parts(left, right16, dims):
    high, middle, low = three_parts(left)
    return short_dot(low, right16, dims) + short_dot(middle, right16, dims) + short_dot(high, right16, dims)


def dot_right_parts(left16, right, dims):
    high, middle, low = three_parts(right)
    return short_dot(left16, low, dims) + short_dot(left16, middle, dims) + short_dot(left16, high, dims)


def two_parts(values):
    high = values.astype(jnp.bfloat16)
    return high, (values - high.astype(jnp.float32)).astype(jnp.bfloat16)


def close_dot(left, right):
    left_high, left_low = two_parts(left)
    right_high, right_low = two_parts(right)
    small = short_dot(left_high, right_low, NN) + short_dot(left_low, right_high, NN)
    return small + short_dot(left_high, right_high, NN)


def inverse_of(capacity):
    eye = identity(capacity.shape[0])
    bound = jnp.max(jnp.sum(jnp.abs(capacity), axis=1, keepdims=True), axis=0, keepdims=True)
    scale = 2.0 / (1.0 + bound)
    power = eye - scale * capacity
    series = eye + power
    begin = scale * series
    for _ in range(4):
        power = close_dot(power, power)
        series = series + close_dot(series, power)

    def improve(inverse):
        residual = eye - exact_dot(capacity, inverse, NN)
        size2 = jnp.sum(jnp.sum(residual * residual, axis=1, keepdims=True), axis=0, keepdims=True)
        return inverse + close_dot(inverse, residual), size2

    better, size2 = improve(scale * series)
    better = jnp.where(size2 < 0.25, better, begin)

    def unfinished(state):
        return (state[1] < 80) & jnp.logical_not(state[2] < 1e-6)

    def again(state):
        inverse, size2 = improve(state[0])
        return inverse, state[1] + 1, size2[0, 0]

    return lax.while_loop(unfinished, again, (better, 0, size2[0, 0]))[0]


def shape_of(out):
    return out if isinstance(out, jax.ShapeDtypeStruct) else jax.ShapeDtypeStruct(out, jnp.float32)


def run(body, outs, *args, place=None):
    vmem = pl.BlockSpec(memory_space=pltpu.VMEM)
    scalars = [] if place is None else [place]
    return pl.pallas_call(
        body,
        out_shape=[shape_of(out) for out in outs],
        in_specs=[pl.BlockSpec(memory_space=pltpu.SMEM)] * len(scalars) + [vmem] * len(args),
        out_specs=[vmem] * len(outs),
        cost_estimate=pl.CostEstimate(flops=1_000_000_000, bytes_accessed=0, transcendentals=0),
        compiler_params=pltpu.CompilerParams(vmem_limit_bytes=VMEM_BYTES),
    )(*scalars, *args)


def run_loading(body, outs, *args, place=None):
    parts = [arg.shape[0] if arg.ndim == 3 else 1 for arg in args]
    first = [sum(parts[:index]) for index in range(len(parts))]

    scalars = [] if place is None else [place]

    def loading(*refs):
        count = len(args)
        given, refs = refs[: len(scalars)], refs[len(scalars) :]
        sources, rest = refs[:count], refs[count:]
        results, held, done = rest[: len(outs)], rest[len(outs) : -1], rest[-1]

        def copy(index, part):
            source, target = sources[index], held[index]
            if parts[index] > 1:
                source, target = source.at[part], target.at[part]
            return pltpu.make_async_copy(source, target, done.at[first[index] + part])

        for index in range(count):
            for part in range(parts[index]):
                copy(index, part).start()
        body(lambda index, part=0: copy(index, part).wait(), *given, *held, *results)

    return pl.pallas_call(
        loading,
        out_shape=[shape_of(out) for out in outs],
        in_specs=[pl.BlockSpec(memory_space=pltpu.SMEM)] * len(scalars)
        + [pl.BlockSpec(memory_space=pltpu.HBM)] * len(args),
        out_specs=[pl.BlockSpec(memory_space=pltpu.VMEM)] * len(outs),
        scratch_shapes=[pltpu.VMEM(arg.shape, arg.dtype) for arg in args]
        + [pltpu.SemaphoreType.DMA((sum(parts),))],
        cost_estimate=pl.CostEstimate(flops=1_000_000_000, bytes_accessed=0, transcendentals=0),
        compiler_params=pltpu.CompilerParams(vmem_limit_bytes=START_BYTES),
    )(*scalars, *args)


def one_hot(order):
    size = order.shape[1]
    rows = lax.broadcasted_iota(jnp.int32, (size, size), 0)
    return jnp.where(rows == order, 1.0, 0.0).astype(jnp.bfloat16)


def identity(size):
    shape = (size, size)
    return jnp.where(
        lax.broadcasted_iota(jnp.int32, shape, 0) == lax.broadcasted_iota(jnp.int32, shape, 1), 1.0, 0.0
    )


def stacked(everyone, low, count):
    return jnp.concatenate([everyone[group, low : low + count, :] for group in range(everyone.shape[0])], 0)


def start_body(wait, order, sides, inverse_cols, bases, send, hot, tree):
    levels, rank, leaf = bases.shape
    groups, _, piece = send.shape
    share = rank // groups
    own = sides.shape[0]
    wait(0)
    hot[...] = one_hot(order[...])
    wait(1)
    ordered = dot_left_parts(sides[...], hot[...], NN)
    for group in range(groups):
        send[group, levels * share :, :] = ordered[:, group * piece : (group + 1) * piece]
    for part in range(leaf // rank):
        tree[part * own : (part + 1) * own, :] = ordered[:, part * rank : (part + 1) * rank]
    wait(2)
    high, middle, low_part = three_parts(inverse_cols[...])
    for level in range(levels):
        wait(3, level)
    rows = bases[...].reshape(levels * rank, leaf)
    applied = short_dot(rows, low_part, NN) + short_dot(rows, middle, NN) + short_dot(rows, high, NN)
    for group in range(groups):
        for level in range(levels):
            low = level * rank + group * share
            send[group, level * share : (level + 1) * share, :] = applied[low : low + share]


def gram_body(got, send, bases, gram):
    levels, rank, leaf = bases.shape
    groups, rows, piece = got.shape
    share = rank // groups
    own = rows - levels * share
    applied = three_parts(jnp.concatenate([got[group, : levels * share, :] for group in range(groups)], 1))
    at = 0
    for column in range(levels):
        count = (levels - column) * share
        high, middle, low = [part[column * share :] for part in applied]
        right = bases[column]
        gram[at : at + count, :] = (
            short_dot(low, right, NT) + short_dot(middle, right, NT) + short_dot(high, right, NT)
        )
        at += count
    sides = stacked(got, levels * share, own)
    for level in range(levels):
        block = exact_dot(sides, stacked(send, level * share, share), NT)
        for group in range(groups):
            low = at + (group * levels + level) * own
            gram[low : low + own, :] = block[group * own : (group + 1) * own]


def first_body(everyone, mine, arrived, panel, weights, own_weights, inverse, side_weights):
    groups, _, rank = everyone.shape
    share = rank // groups
    own = side_weights.shape[0]
    far = jnp.concatenate([stacked(everyone, level * share, share) for level in range(1, 7)], 0)
    inverse[...] = inverse_of(stacked(everyone, 0, share) + identity(rank))
    side_row = lambda level: sum(
        everyone[group, 7 * share + level * own : 7 * share + (level + 1) * own, :] for group in range(groups)
    )
    upper = jnp.concatenate([mine[share : 7 * share, :] + arrived[share : 7 * share, :], side_row(0)], 0)
    own_weights[...] = exact_dot(upper, inverse[...], NN)
    side_weights[...] = own_weights[6 * share :, :]
    update = exact_dot(own_weights[...], far[:rank], NT)
    panel[: 6 * share, :] = mine[7 * share : 13 * share, :] + arrived[7 * share : 13 * share, :] - update[: 6 * share]
    panel[6 * share :, :] = side_row(1) - update[6 * share :]
    weights[...] = far


def first_rest_body(everyone, mine, arrived, far, own_weights, inverse, rest, far_weights):
    groups, _, rank = everyone.shape
    share = rank // groups
    own = own_weights.shape[0] - 6 * share
    side_row = lambda level: sum(
        everyone[group, 7 * share + level * own : 7 * share + (level + 1) * own, :] for group in range(groups)
    )
    far_weights[...] = exact_dot(far[...], inverse[...], NN)
    at = 0
    source = 13 * share
    for column in range(2, 7):
        count = (7 - column) * share
        update = exact_dot(own_weights[(column - 1) * share :, :], far[(column - 1) * rank : column * rank, :], NT)
        rest[at : at + count, :] = (
            mine[source : source + count, :] + arrived[source : source + count, :] - update[:count]
        )
        rest[at + count : at + count + own, :] = side_row(column) - update[count:]
        source += count
        at += count + own


def level_panel_body(later, later_arrived, far, own_weights, panel):
    rank = far.shape[1]
    count = panel.shape[0]
    update = exact_dot(own_weights[...], far[:rank, :], NT)
    panel[...] = later[:count, :] + later_arrived[:count, :] - update


def level_factor_body(above, place, everyone, far, own_weights, inverse):
    groups, _, rank = everyone.shape
    share = rank // groups
    far[...] = jnp.concatenate([stacked(everyone, level * share, share) for level in range(1, above + 1)], 0)
    inverse[...] = inverse_of(stacked(everyone, 0, share) + identity(rank))
    own_upper = everyone[place[0], share : share + own_weights.shape[0], :]
    own_weights[...] = exact_dot(own_upper, inverse[...], NN)


def level_all_body(above, later, later_arrived, far, own_weights, panels):
    rank = far.shape[1]
    share = rank // 4
    at = 0
    for column in range(above):
        count = own_weights.shape[0] - column * share
        update = exact_dot(own_weights[column * share :, :], far[column * rank : (column + 1) * rank, :], NT)
        panels[at : at + count, :] = later[at : at + count, :] + later_arrived[at : at + count, :] - update
        at += count


def level_rest_body(everyone, later, later_arrived, far, own_weights, inverse, rest, far_weights, side_weights):
    groups, _, rank = everyone.shape
    share = rank // groups
    above = far.shape[0] // rank
    own = own_weights.shape[0] - above * share
    sides = groups * own
    low = (above + 1) * share
    far_weights[...] = exact_dot(far[...], inverse[...], NN)
    side_weights[:sides, :] = stacked(everyone, low + own, own)
    side_weights[sides:, :] = exact_dot(stacked(everyone, low, own), inverse[...], NN)
    at = 0
    source = own_weights.shape[0]
    for column in range(1, far.shape[0] // rank):
        count = own_weights.shape[0] - column * share
        update = exact_dot(own_weights[column * share :, :], far[column * rank : (column + 1) * rank, :], NT)
        rest[at : at + count, :] = (
            later[source : source + count, :] + later_arrived[source : source + count, :] - update
        )
        source += count
        at += count


def spread_body(everyone, fifth, far, weights):
    groups, _, rank = everyone.shape
    share = rank // groups
    own = fifth.shape[0] - 3 * rank
    own = own // groups
    blocks = [stacked(everyone, level * share, share) for level in range(4)]
    inverse = inverse_of(blocks[0] + identity(rank))
    far[: 3 * rank, :] = jnp.concatenate(blocks[1:], 0)
    far[3 * rank :, :] = stacked(everyone, 4 * share, own)
    weights[...] = exact_dot(far[...], inverse, NN)
    update = exact_dot(weights[...], far[:rank, :], NT)
    at = 4 * share + own
    for level in range(3):
        fifth[level * rank : (level + 1) * rank, :] = (
            stacked(everyone, at + level * share, share) - update[level * rank : (level + 1) * rank]
        )
    fifth[3 * rank :, :] = stacked(everyone, at + 3 * share, own) - update[3 * rank :]


def spread_rest_body(column, everyone, far, weights, panel):
    groups, _, rank = everyone.shape
    share = rank // groups
    own = (far.shape[0] - 3 * rank) // groups
    source = (7 if column == 1 else 9) * share + (2 if column == 1 else 3) * own
    update = exact_dot(weights[column * rank :, :], far[column * rank : (column + 1) * rank, :], NT)
    at = 0
    for level in range(column, 3):
        panel[at : at + rank, :] = stacked(everyone, source, share) - update[at : at + rank]
        at += rank
        source += share
    panel[at:, :] = stacked(everyone, source, own) - update[at:]


def factor_body(mine, arrived, upper, weights):
    rank = mine.shape[1]
    upper[...] = mine[rank:, :] + arrived[rank:, :]
    inverse = inverse_of(mine[:rank, :] + arrived[:rank, :] + identity(rank))
    weights[...] = exact_dot(upper[...], inverse, NN)


def next_body(later, later_arrived, upper, weights, panel):
    rank = upper.shape[1]
    panel[...] = later[...] + later_arrived[...] - exact_dot(weights[...], upper[:rank, :], NT)


def rest_body(later, later_arrived, upper, weights, rest):
    rank = upper.shape[1]
    rest[...] = later[...] + later_arrived[...] - exact_dot(weights[rank:, :], upper[rank : 2 * rank, :], NT)


def last_panel_body(place, later, later_arrived, upper, weights, panel):
    rank = upper.shape[1]
    own = panel.shape[0] - rank
    rows = pl.ds(pl.multiple_of(rank + place[0] * own, own), own)
    left = jnp.concatenate([weights[:rank, :], weights[rows, :]], 0)
    update = exact_dot(left, upper[:rank, :], NT)
    panel[:rank, :] = later[:rank, :] + later_arrived[:rank, :] - update[:rank]
    panel[rank:, :] = later[rows, :] + later_arrived[rows, :] - update[rank:]


def carry_step(applied, sides, far, side_far, inverse):
    rank = inverse.shape[0]
    gone = applied[:rank]
    sides = sides - exact_dot(exact_dot(side_far, inverse, NN), gone, NN)
    return applied[rank:] - exact_dot(exact_dot(far, inverse, NN), gone, NN), sides


def carry_first_body(send, weights1, weights2, carried, gone):
    groups = send.shape[0]
    rank = weights2.shape[1]
    share = rank // groups
    applied = [stacked(send, level * share, share) for level in range(7)]
    rest = jnp.concatenate(applied[1:], 0) - exact_dot(weights1[...], applied[0], NN)
    carried[...] = rest[rank:] - exact_dot(weights2[...], rest[:rank], NN)
    gone[:rank, :] = applied[0]
    gone[rank:, :] = rest[:rank]


def carry_body(above, before, gone, side_weights, everyone, far, inverse, inverse_cols, carried):
    groups, rows, rank = everyone.shape
    share = rank // groups
    low = (above + 1) * share
    sides = side_weights.shape[0] // 2
    own = sides // groups
    parts = (rows - low - own) // own
    tree = jnp.concatenate(
        [stacked(everyone, low + own + part * own, own) for part in range(parts)], 1
    )
    found = exact_dot(tree, inverse_cols[...], NN)
    for place in range(2):
        weights = side_weights[place * sides : (place + 1) * sides, :]
        found = found - exact_dot(weights, gone[place * rank : (place + 1) * rank, :], NN)
    applied, found = carry_step(before[...], found, far[...], stacked(everyone, low, own), inverse[...])
    carried[: above * rank, :] = applied
    carried[above * rank :, :] = found


def carry_on_body(before, weights, carried):
    rank = weights.shape[1]
    carried[...] = before[rank:, :] - exact_dot(weights[...], before[:rank, :], NN)


def carry_last_body(before, weights, send):
    groups, rows, _ = send.shape
    rank = weights.shape[1]
    own = rows - rank
    carried = before[rank:, :] - exact_dot(weights[...], before[:rank, :], NN)
    for group in range(groups):
        send[group, :rank, :] = carried[:rank]
        send[group, rank:, :] = carried[rank + group * own : rank + (group + 1) * own]


def finish_body(mine, arrived, got, hot, out):
    rank = mine.shape[1]
    groups = got.shape[0]
    inverse = inverse_of(mine[:rank, :] + arrived[:rank, :] + identity(rank))
    top = exact_dot(mine[rank:, :] + arrived[rank:, :], inverse, NN)
    slope = jnp.concatenate([got[group, :rank, :] for group in range(groups)], 1)
    base = jnp.concatenate([got[group, rank:, :] for group in range(groups)], 1)
    out[...] = dot_left_parts(base - exact_dot(top, slope, NN), hot[...], NT)


def add_body(*refs):
    send = refs[-1]
    mine, arrived, others = refs[0], refs[1], refs[2:-1]
    count = mine.shape[0]
    total = mine[...] + arrived[...]
    for group in range(send.shape[0]):
        send[group, :count, :] = total
        for other in others:
            send[group, count : count + other.shape[0], :] = other[...]


def sum_to_all(mine, arrived, *others):
    groups = lax.axis_size("rhs")
    rows = sum(block.shape[0] for block in (mine,) + others)
    (send,) = run(add_body, [(groups, rows, mine.shape[1])], mine, arrived, *others)
    return lax.all_to_all(send, "rhs", 0, 0)


def route(height):
    pairs = []
    for leaf in range(128):
        if height in (4, 7):
            low = 1 if height == 4 else 4
            ring = (leaf >> low) & 7
            pairs.append((leaf, leaf & ~(7 << low) | ((ring ^ 6) << low)))
        else:
            pairs.append((leaf, leaf ^ (1 << (height - 1))))
    return pairs


def local(right_sides, leaf_inverse, bases, ordering):
    own, leaf = right_sides.shape
    piece = leaf_inverse.shape[1]
    levels, rank, _ = bases.shape
    groups = lax.axis_size("rhs")
    share = rank // groups
    sides = own * groups
    square = (rank, rank)
    swap = lambda block, height: lax.ppermute(block, "leaf", route(height))

    place = lax.axis_index("rhs").reshape(1)
    send, hot, tree = run_loading(
        start_body,
        [
            (groups, levels * share + own, piece),
            jax.ShapeDtypeStruct((leaf, leaf), jnp.bfloat16),
            (leaf // rank * own, rank),
        ],
        ordering,
        right_sides,
        leaf_inverse,
        bases,
    )
    got = lax.all_to_all(send, "rhs", 0, 0)
    rows = 28 * share
    (gram,) = run(gram_body, [(rows + groups * levels * own, rank)], got, send, bases)
    other = swap(gram, 1)
    total = gram + other
    shared = jnp.broadcast_to(total[: 7 * share][None], (groups, 7 * share, rank))
    parts = total[rows:].reshape(groups, levels * own, rank)
    everyone = lax.all_to_all(jnp.concatenate([shared, parts], 1), "rhs", 0, 0)

    panel, far1, own_weights, inverse1, side1 = run(
        first_body,
        [(6 * share + own, rank), (6 * rank, rank), (6 * share + own, rank), square, (own, rank)],
        everyone,
        gram,
        other,
    )
    arrived = swap(panel, 2)
    later, far_weights1 = run(
        first_rest_body,
        [(15 * share + 5 * own, rank), (6 * rank, rank)],
        everyone,
        gram,
        other,
        far1,
        own_weights,
        inverse1,
    )
    for height in (2, 3):
        above = 7 - height
        later_arrived = swap(later, height)
        arrived, later = lax.optimization_barrier((arrived, later))
        everyone = sum_to_all(panel, arrived, side1) if height == 2 else sum_to_all(panel, arrived, tree)
        if height == 3:
            everyone, carried = lax.optimization_barrier((everyone, carried))
        far, own_weights, inverse = run(
            functools.partial(level_factor_body, above),
            [(above * rank, rank), (above * share + own, rank), square],
            everyone,
            place=place,
        )
        if height == 2:
            (next_panel,) = run(
                level_panel_body, [(above * share + own, rank)], later, later_arrived, far, own_weights
            )
            arrived = swap(next_panel, 3)
            rest_rows = above * (above - 1) // 2 * share + (above - 1) * own
            later, far_weights2, side_weights = run(
                level_rest_body,
                [(rest_rows, rank), (above * rank, rank), (2 * sides, rank)],
                everyone,
                later,
                later_arrived,
                far,
                own_weights,
                inverse,
            )
            panel = next_panel
            carried, gone = run(
                carry_first_body,
                [(5 * rank, piece), (2 * rank, piece)],
                send,
                far_weights1,
                far_weights2,
            )
        else:
            (panels,) = run(
                functools.partial(level_all_body, above),
                [(above * (above + 1) // 2 * share + above * own, rank)],
                later,
                later_arrived,
                far,
                own_weights,
            )
            panels_arrived = swap(panels, 4)
            (carried,) = run(
                functools.partial(carry_body, above),
                [(4 * rank + sides, piece)],
                carried,
                gone,
                side_weights,
                everyone,
                far,
                inverse,
                leaf_inverse,
            )
    panels_arrived, carried = lax.optimization_barrier((panels_arrived, carried))
    everyone = sum_to_all(panels, panels_arrived)
    heights = lambda count: (count * rank + sides, rank)
    fifth, upper, weights = run(spread_body, [heights(3)] * 3, everyone)
    arrived = swap(fifth, 5)
    (sixth,) = run(functools.partial(spread_rest_body, 1), [heights(2)], everyone, upper, weights)
    sixth_arrived = swap(sixth, 5)
    everyone, sixth = lax.optimization_barrier((everyone, sixth))
    (seventh,) = run(functools.partial(spread_rest_body, 2), [heights(1)], everyone, upper, weights)
    seventh_arrived = swap(seventh, 5)
    (carried,) = run(carry_on_body, [(3 * rank + sides, piece)], carried, weights)
    upper, weights = run(factor_body, [heights(2)] * 2, fifth, arrived)
    (sixth,) = run(next_body, [heights(2)], sixth, sixth_arrived, upper, weights)
    arrived = swap(sixth, 6)
    sixth, seventh = lax.optimization_barrier((sixth, seventh))
    (seventh,) = run(rest_body, [heights(1)], seventh, seventh_arrived, upper, weights)
    seventh_arrived = swap(seventh, 6)
    (carried,) = run(carry_on_body, [(2 * rank + sides, piece)], carried, weights)
    upper, weights = run(factor_body, [heights(1)] * 2, sixth, arrived)
    (seventh,) = run(
        last_panel_body, [(rank + own, rank)], seventh, seventh_arrived, upper, weights, place=place
    )
    arrived = swap(seventh, 7)
    (send,) = run(carry_last_body, [(groups, rank + own, piece)], carried, weights)
    send, seventh = lax.optimization_barrier((send, seventh))
    got = lax.all_to_all(send, "rhs", 0, 0)
    (result,) = run(finish_body, [(own, leaf)], seventh, arrived, got, hot)
    return result


def solution(mesh):
    placed = (P("rhs", "leaf"), P("leaf", "rhs"), P(None, None, "leaf"), P("leaf", None))
    return jax.shard_map(
        local, mesh=mesh, in_specs=placed, out_specs=P("rhs", "leaf"), check_vma=False
    )
```

```python
import functools

import jax
import jax.numpy as jnp
from jax import lax
from jax.experimental import pallas as pl
from jax.experimental.pallas import tpu as pltpu
from jax.sharding import PartitionSpec as P

HIGHEST = lax.Precision.HIGHEST
VMEM_BYTES = 24 * 1024 * 1024
START_BYTES = 60 * 1024 * 1024
NN = (((1,), (0,)), ((), ()))
NT = (((1,), (1,)), ((), ()))


def exact_dot(left, right, dims):
    return lax.dot_general(left, right, dims, precision=HIGHEST, preferred_element_type=jnp.float32)


def short_dot(left, right, dims):
    return lax.dot_general(left, right, dims, preferred_element_type=jnp.float32)


def three_parts(values):
    high = values.astype(jnp.bfloat16)
    rest = values - high.astype(jnp.float32)
    middle = rest.astype(jnp.bfloat16)
    low = (rest - middle.astype(jnp.float32)).astype(jnp.bfloat16)
    return high, middle, low


def dot_left_parts(left, right16, dims):
    high, middle, low = three_parts(left)
    return short_dot(low, right16, dims) + short_dot(middle, right16, dims) + short_dot(high, right16, dims)


def dot_right_parts(left16, right, dims):
    high, middle, low = three_parts(right)
    return short_dot(left16, low, dims) + short_dot(left16, middle, dims) + short_dot(left16, high, dims)


def two_parts(values):
    high = values.astype(jnp.bfloat16)
    return high, (values - high.astype(jnp.float32)).astype(jnp.bfloat16)


def close_dot(left, right):
    left_high, left_low = two_parts(left)
    right_high, right_low = two_parts(right)
    small = short_dot(left_high, right_low, NN) + short_dot(left_low, right_high, NN)
    return small + short_dot(left_high, right_high, NN)


def inverse_of(capacity):
    eye = identity(capacity.shape[0])
    bound = jnp.max(jnp.sum(jnp.abs(capacity), axis=1, keepdims=True), axis=0, keepdims=True)
    scale = 2.0 / (1.0 + bound)
    power = eye - scale * capacity
    series = eye + power
    begin = scale * series
    for _ in range(4):
        power = close_dot(power, power)
        series = series + close_dot(series, power)

    def improve(inverse):
        residual = eye - exact_dot(capacity, inverse, NN)
        size2 = jnp.sum(jnp.sum(residual * residual, axis=1, keepdims=True), axis=0, keepdims=True)
        return inverse + close_dot(inverse, residual), size2

    better, size2 = improve(scale * series)
    better = jnp.where(size2 < 0.25, better, begin)

    def unfinished(state):
        return (state[1] < 80) & jnp.logical_not(state[2] < 1e-6)

    def again(state):
        inverse, size2 = improve(state[0])
        return inverse, state[1] + 1, size2[0, 0]

    return lax.while_loop(unfinished, again, (better, 0, size2[0, 0]))[0]


def shape_of(out):
    return out if isinstance(out, jax.ShapeDtypeStruct) else jax.ShapeDtypeStruct(out, jnp.float32)


def run(body, outs, *args, place=None):
    vmem = pl.BlockSpec(memory_space=pltpu.VMEM)
    scalars = [] if place is None else [place]
    return pl.pallas_call(
        body,
        out_shape=[shape_of(out) for out in outs],
        in_specs=[pl.BlockSpec(memory_space=pltpu.SMEM)] * len(scalars) + [vmem] * len(args),
        out_specs=[vmem] * len(outs),
        cost_estimate=pl.CostEstimate(flops=1_000_000_000, bytes_accessed=0, transcendentals=0),
        compiler_params=pltpu.CompilerParams(vmem_limit_bytes=VMEM_BYTES),
    )(*scalars, *args)


def run_loading(body, outs, *args, place=None):
    parts = [arg.shape[0] if arg.ndim == 3 else 1 for arg in args]
    first = [sum(parts[:index]) for index in range(len(parts))]

    scalars = [] if place is None else [place]

    def loading(*refs):
        count = len(args)
        given, refs = refs[: len(scalars)], refs[len(scalars) :]
        sources, rest = refs[:count], refs[count:]
        results, held, done = rest[: len(outs)], rest[len(outs) : -1], rest[-1]

        def copy(index, part):
            source, target = sources[index], held[index]
            if parts[index] > 1:
                source, target = source.at[part], target.at[part]
            return pltpu.make_async_copy(source, target, done.at[first[index] + part])

        for index in range(count):
            for part in range(parts[index]):
                copy(index, part).start()
        body(lambda index, part=0: copy(index, part).wait(), *given, *held, *results)

    return pl.pallas_call(
        loading,
        out_shape=[shape_of(out) for out in outs],
        in_specs=[pl.BlockSpec(memory_space=pltpu.SMEM)] * len(scalars)
        + [pl.BlockSpec(memory_space=pltpu.HBM)] * len(args),
        out_specs=[pl.BlockSpec(memory_space=pltpu.VMEM)] * len(outs),
        scratch_shapes=[pltpu.VMEM(arg.shape, arg.dtype) for arg in args]
        + [pltpu.SemaphoreType.DMA((sum(parts),))],
        cost_estimate=pl.CostEstimate(flops=1_000_000_000, bytes_accessed=0, transcendentals=0),
        compiler_params=pltpu.CompilerParams(vmem_limit_bytes=START_BYTES),
    )(*scalars, *args)


def one_hot(order):
    size = order.shape[1]
    rows = lax.broadcasted_iota(jnp.int32, (size, size), 0)
    return jnp.where(rows == order, 1.0, 0.0).astype(jnp.bfloat16)


def identity(size):
    shape = (size, size)
    return jnp.where(
        lax.broadcasted_iota(jnp.int32, shape, 0) == lax.broadcasted_iota(jnp.int32, shape, 1), 1.0, 0.0
    )


def stacked(everyone, low, count):
    return jnp.concatenate([everyone[group, low : low + count, :] for group in range(everyone.shape[0])], 0)


def start_body(wait, order, sides, inverse_cols, bases, send, tree):
    levels, rank, leaf = bases.shape
    groups, _, piece = send.shape
    share = rank // groups
    own = sides.shape[0]
    wait(0)
    hot = one_hot(order[...])
    wait(1)
    ordered = dot_left_parts(sides[...], hot, NN)
    for group in range(groups):
        send[group, levels * share :, :] = ordered[:, group * piece : (group + 1) * piece]
    for part in range(leaf // rank):
        tree[part * own : (part + 1) * own, :] = ordered[:, part * rank : (part + 1) * rank]
    wait(2)
    high, middle, low_part = three_parts(inverse_cols[...])
    for level in range(levels):
        wait(3, level)
    rows = bases[...].reshape(levels * rank, leaf)
    applied = short_dot(rows, low_part, NN) + short_dot(rows, middle, NN) + short_dot(rows, high, NN)
    for group in range(groups):
        for level in range(levels):
            low = level * rank + group * share
            send[group, level * share : (level + 1) * share, :] = applied[low : low + share]


def places_body(order, hot):
    columns = lax.broadcasted_iota(jnp.int32, hot.shape, 1)
    hot[...] = jnp.where(columns == order[...], 1.0, 0.0).astype(jnp.bfloat16)


def gram_body(got, send, bases, gram):
    levels, rank, leaf = bases.shape
    groups, rows, piece = got.shape
    share = rank // groups
    own = rows - levels * share
    applied = three_parts(jnp.concatenate([got[group, : levels * share, :] for group in range(groups)], 1))
    at = 0
    for column in range(levels):
        count = (levels - column) * share
        high, middle, low = [part[column * share :] for part in applied]
        right = bases[column]
        gram[at : at + count, :] = (
            short_dot(low, right, NT) + short_dot(middle, right, NT) + short_dot(high, right, NT)
        )
        at += count
    sides = stacked(got, levels * share, own)
    for level in range(levels):
        block = exact_dot(sides, stacked(send, level * share, share), NT)
        for group in range(groups):
            low = at + (group * levels + level) * own
            gram[low : low + own, :] = block[group * own : (group + 1) * own]


def first_body(everyone, mine, arrived, panel, weights, own_weights, inverse, side_weights):
    groups, _, rank = everyone.shape
    share = rank // groups
    own = side_weights.shape[0]
    far = jnp.concatenate([stacked(everyone, level * share, share) for level in range(1, 7)], 0)
    inverse[...] = inverse_of(stacked(everyone, 0, share) + identity(rank))
    side_row = lambda level: sum(
        everyone[group, 7 * share + level * own : 7 * share + (level + 1) * own, :] for group in range(groups)
    )
    upper = jnp.concatenate([mine[share : 7 * share, :] + arrived[share : 7 * share, :], side_row(0)], 0)
    own_weights[...] = exact_dot(upper, inverse[...], NN)
    side_weights[...] = own_weights[6 * share :, :]
    update = exact_dot(own_weights[...], far[:rank], NT)
    panel[: 6 * share, :] = mine[7 * share : 13 * share, :] + arrived[7 * share : 13 * share, :] - update[: 6 * share]
    panel[6 * share :, :] = side_row(1) - update[6 * share :]
    weights[...] = far


def first_rest_body(everyone, mine, arrived, far, own_weights, inverse, rest, far_weights):
    groups, _, rank = everyone.shape
    share = rank // groups
    own = own_weights.shape[0] - 6 * share
    side_row = lambda level: sum(
        everyone[group, 7 * share + level * own : 7 * share + (level + 1) * own, :] for group in range(groups)
    )
    far_weights[...] = exact_dot(far[...], inverse[...], NN)
    at = 0
    source = 13 * share
    for column in range(2, 7):
        count = (7 - column) * share
        update = exact_dot(own_weights[(column - 1) * share :, :], far[(column - 1) * rank : column * rank, :], NT)
        rest[at : at + count, :] = (
            mine[source : source + count, :] + arrived[source : source + count, :] - update[:count]
        )
        rest[at + count : at + count + own, :] = side_row(column) - update[count:]
        source += count
        at += count + own


def level_panel_body(later, later_arrived, far, own_weights, panel):
    rank = far.shape[1]
    count = panel.shape[0]
    update = exact_dot(own_weights[...], far[:rank, :], NT)
    panel[...] = later[:count, :] + later_arrived[:count, :] - update


def level_factor_body(above, place, everyone, far, own_weights, inverse):
    groups, _, rank = everyone.shape
    share = rank // groups
    far[...] = jnp.concatenate([stacked(everyone, level * share, share) for level in range(1, above + 1)], 0)
    inverse[...] = inverse_of(stacked(everyone, 0, share) + identity(rank))
    own_upper = everyone[place[0], share : share + own_weights.shape[0], :]
    own_weights[...] = exact_dot(own_upper, inverse[...], NN)


def level_all_body(above, later, later_arrived, far, own_weights, panels):
    rank = far.shape[1]
    share = rank // 4
    at = 0
    for column in range(above):
        count = own_weights.shape[0] - column * share
        update = exact_dot(own_weights[column * share :, :], far[column * rank : (column + 1) * rank, :], NT)
        panels[at : at + count, :] = later[at : at + count, :] + later_arrived[at : at + count, :] - update
        at += count


def level_rest_body(everyone, later, later_arrived, far, own_weights, inverse, rest, far_weights, side_weights):
    groups, _, rank = everyone.shape
    share = rank // groups
    above = far.shape[0] // rank
    own = own_weights.shape[0] - above * share
    sides = groups * own
    low = (above + 1) * share
    far_weights[...] = exact_dot(far[...], inverse[...], NN)
    side_weights[:sides, :] = stacked(everyone, low + own, own)
    side_weights[sides:, :] = exact_dot(stacked(everyone, low, own), inverse[...], NN)
    at = 0
    source = own_weights.shape[0]
    for column in range(1, far.shape[0] // rank):
        count = own_weights.shape[0] - column * share
        update = exact_dot(own_weights[column * share :, :], far[column * rank : (column + 1) * rank, :], NT)
        rest[at : at + count, :] = (
            later[source : source + count, :] + later_arrived[source : source + count, :] - update
        )
        source += count
        at += count


def spread_body(everyone, fifth, far, weights):
    groups, _, rank = everyone.shape
    share = rank // groups
    own = fifth.shape[0] - 3 * rank
    own = own // groups
    blocks = [stacked(everyone, level * share, share) for level in range(4)]
    inverse = inverse_of(blocks[0] + identity(rank))
    far[: 3 * rank, :] = jnp.concatenate(blocks[1:], 0)
    far[3 * rank :, :] = stacked(everyone, 4 * share, own)
    weights[...] = exact_dot(far[...], inverse, NN)
    update = exact_dot(weights[...], far[:rank, :], NT)
    at = 4 * share + own
    for level in range(3):
        fifth[level * rank : (level + 1) * rank, :] = (
            stacked(everyone, at + level * share, share) - update[level * rank : (level + 1) * rank]
        )
    fifth[3 * rank :, :] = stacked(everyone, at + 3 * share, own) - update[3 * rank :]


def spread_rest_body(column, everyone, far, weights, panel):
    groups, _, rank = everyone.shape
    share = rank // groups
    own = (far.shape[0] - 3 * rank) // groups
    source = (7 if column == 1 else 9) * share + (2 if column == 1 else 3) * own
    update = exact_dot(weights[column * rank :, :], far[column * rank : (column + 1) * rank, :], NT)
    at = 0
    for level in range(column, 3):
        panel[at : at + rank, :] = stacked(everyone, source, share) - update[at : at + rank]
        at += rank
        source += share
    panel[at:, :] = stacked(everyone, source, own) - update[at:]


def factor_body(mine, arrived, upper, weights):
    rank = mine.shape[1]
    upper[...] = mine[rank:, :] + arrived[rank:, :]
    inverse = inverse_of(mine[:rank, :] + arrived[:rank, :] + identity(rank))
    weights[...] = exact_dot(upper[...], inverse, NN)


def next_body(later, later_arrived, upper, weights, panel):
    rank = upper.shape[1]
    panel[...] = later[...] + later_arrived[...] - exact_dot(weights[...], upper[:rank, :], NT)


def rest_body(later, later_arrived, upper, weights, rest):
    rank = upper.shape[1]
    rest[...] = later[...] + later_arrived[...] - exact_dot(weights[rank:, :], upper[rank : 2 * rank, :], NT)


def last_panel_body(place, later, later_arrived, upper, weights, panel):
    rank = upper.shape[1]
    own = panel.shape[0] - rank
    rows = pl.ds(pl.multiple_of(rank + place[0] * own, own), own)
    left = jnp.concatenate([weights[:rank, :], weights[rows, :]], 0)
    update = exact_dot(left, upper[:rank, :], NT)
    panel[:rank, :] = later[:rank, :] + later_arrived[:rank, :] - update[:rank]
    panel[rank:, :] = later[rows, :] + later_arrived[rows, :] - update[rank:]


def carry_step(applied, sides, far, side_far, inverse):
    rank = inverse.shape[0]
    gone = applied[:rank]
    sides = sides - exact_dot(exact_dot(side_far, inverse, NN), gone, NN)
    return applied[rank:] - exact_dot(exact_dot(far, inverse, NN), gone, NN), sides


def carry_first_body(send, weights1, weights2, carried, gone):
    groups = send.shape[0]
    rank = weights2.shape[1]
    share = rank // groups
    applied = [stacked(send, level * share, share) for level in range(7)]
    rest = jnp.concatenate(applied[1:], 0) - exact_dot(weights1[...], applied[0], NN)
    carried[...] = rest[rank:] - exact_dot(weights2[...], rest[:rank], NN)
    gone[:rank, :] = applied[0]
    gone[rank:, :] = rest[:rank]


def carry_body(above, before, gone, side_weights, everyone, far, inverse, inverse_cols, carried):
    groups, rows, rank = everyone.shape
    share = rank // groups
    low = (above + 1) * share
    sides = side_weights.shape[0] // 2
    own = sides // groups
    parts = (rows - low - own) // own
    tree = jnp.concatenate(
        [stacked(everyone, low + own + part * own, own) for part in range(parts)], 1
    )
    found = exact_dot(tree, inverse_cols[...], NN)
    for place in range(2):
        weights = side_weights[place * sides : (place + 1) * sides, :]
        found = found - exact_dot(weights, gone[place * rank : (place + 1) * rank, :], NN)
    applied, found = carry_step(before[...], found, far[...], stacked(everyone, low, own), inverse[...])
    carried[: above * rank, :] = applied
    carried[above * rank :, :] = found


def carry_on_body(before, weights, carried):
    rank = weights.shape[1]
    carried[...] = before[rank:, :] - exact_dot(weights[...], before[:rank, :], NN)


def carry_last_body(before, weights, send):
    groups, rows, _ = send.shape
    rank = weights.shape[1]
    own = rows - rank
    carried = before[rank:, :] - exact_dot(weights[...], before[:rank, :], NN)
    for group in range(groups):
        send[group, :rank, :] = carried[:rank]
        send[group, rank:, :] = carried[rank + group * own : rank + (group + 1) * own]


def finish_body(mine, arrived, got, hot, out):
    rank = mine.shape[1]
    groups = got.shape[0]
    inverse = inverse_of(mine[:rank, :] + arrived[:rank, :] + identity(rank))
    top = exact_dot(mine[rank:, :] + arrived[rank:, :], inverse, NN)
    slope = jnp.concatenate([got[group, :rank, :] for group in range(groups)], 1)
    base = jnp.concatenate([got[group, rank:, :] for group in range(groups)], 1)
    out[...] = dot_left_parts(base - exact_dot(top, slope, NN), hot[...], NN)


def add_body(*refs):
    send = refs[-1]
    mine, arrived, others = refs[0], refs[1], refs[2:-1]
    count = mine.shape[0]
    total = mine[...] + arrived[...]
    for group in range(send.shape[0]):
        send[group, :count, :] = total
        for other in others:
            send[group, count : count + other.shape[0], :] = other[...]


def sum_to_all(mine, arrived, *others):
    groups = lax.axis_size("rhs")
    rows = sum(block.shape[0] for block in (mine,) + others)
    (send,) = run(add_body, [(groups, rows, mine.shape[1])], mine, arrived, *others)
    return lax.all_to_all(send, "rhs", 0, 0)


def route(height):
    pairs = []
    for leaf in range(128):
        if height in (4, 7):
            low = 1 if height == 4 else 4
            ring = (leaf >> low) & 7
            pairs.append((leaf, leaf & ~(7 << low) | ((ring ^ 6) << low)))
        else:
            pairs.append((leaf, leaf ^ (1 << (height - 1))))
    return pairs


def local(right_sides, leaf_inverse, bases, ordering):
    own, leaf = right_sides.shape
    piece = leaf_inverse.shape[1]
    levels, rank, _ = bases.shape
    groups = lax.axis_size("rhs")
    share = rank // groups
    sides = own * groups
    square = (rank, rank)
    swap = lambda block, height: lax.ppermute(block, "leaf", route(height))

    place = lax.axis_index("rhs").reshape(1)
    send, tree = run_loading(
        start_body,
        [
            (groups, levels * share + own, piece),
            (leaf // rank * own, rank),
        ],
        ordering,
        right_sides,
        leaf_inverse,
        bases,
    )
    got = lax.all_to_all(send, "rhs", 0, 0)
    rows = 28 * share
    (gram,) = run(gram_body, [(rows + groups * levels * own, rank)], got, send, bases)
    other = swap(gram, 1)
    total = gram + other
    shared = jnp.broadcast_to(total[: 7 * share][None], (groups, 7 * share, rank))
    parts = total[rows:].reshape(groups, levels * own, rank)
    everyone = lax.all_to_all(jnp.concatenate([shared, parts], 1), "rhs", 0, 0)

    panel, far1, own_weights, inverse1, side1 = run(
        first_body,
        [(6 * share + own, rank), (6 * rank, rank), (6 * share + own, rank), square, (own, rank)],
        everyone,
        gram,
        other,
    )
    arrived = swap(panel, 2)
    later, far_weights1 = run(
        first_rest_body,
        [(15 * share + 5 * own, rank), (6 * rank, rank)],
        everyone,
        gram,
        other,
        far1,
        own_weights,
        inverse1,
    )
    for height in (2, 3):
        above = 7 - height
        later_arrived = swap(later, height)
        arrived, later = lax.optimization_barrier((arrived, later))
        everyone = sum_to_all(panel, arrived, side1) if height == 2 else sum_to_all(panel, arrived, tree)
        if height == 3:
            everyone, carried = lax.optimization_barrier((everyone, carried))
        far, own_weights, inverse = run(
            functools.partial(level_factor_body, above),
            [(above * rank, rank), (above * share + own, rank), square],
            everyone,
            place=place,
        )
        if height == 2:
            (next_panel,) = run(
                level_panel_body, [(above * share + own, rank)], later, later_arrived, far, own_weights
            )
            arrived = swap(next_panel, 3)
            rest_rows = above * (above - 1) // 2 * share + (above - 1) * own
            later, far_weights2, side_weights = run(
                level_rest_body,
                [(rest_rows, rank), (above * rank, rank), (2 * sides, rank)],
                everyone,
                later,
                later_arrived,
                far,
                own_weights,
                inverse,
            )
            panel = next_panel
            carried, gone = run(
                carry_first_body,
                [(5 * rank, piece), (2 * rank, piece)],
                send,
                far_weights1,
                far_weights2,
            )
        else:
            (panels,) = run(
                functools.partial(level_all_body, above),
                [(above * (above + 1) // 2 * share + above * own, rank)],
                later,
                later_arrived,
                far,
                own_weights,
            )
            panels_arrived = swap(panels, 4)
            (carried,) = run(
                functools.partial(carry_body, above),
                [(4 * rank + sides, piece)],
                carried,
                gone,
                side_weights,
                everyone,
                far,
                inverse,
                leaf_inverse,
            )
    panels_arrived, carried = lax.optimization_barrier((panels_arrived, carried))
    everyone = sum_to_all(panels, panels_arrived)
    heights = lambda count: (count * rank + sides, rank)
    fifth, upper, weights = run(spread_body, [heights(3)] * 3, everyone)
    arrived = swap(fifth, 5)
    (sixth,) = run(functools.partial(spread_rest_body, 1), [heights(2)], everyone, upper, weights)
    sixth_arrived = swap(sixth, 5)
    everyone, sixth = lax.optimization_barrier((everyone, sixth))
    (seventh,) = run(functools.partial(spread_rest_body, 2), [heights(1)], everyone, upper, weights)
    seventh_arrived = swap(seventh, 5)
    (carried,) = run(carry_on_body, [(3 * rank + sides, piece)], carried, weights)
    upper, weights = run(factor_body, [heights(2)] * 2, fifth, arrived)
    (sixth,) = run(next_body, [heights(2)], sixth, sixth_arrived, upper, weights)
    arrived = swap(sixth, 6)
    sixth, seventh = lax.optimization_barrier((sixth, seventh))
    (seventh,) = run(rest_body, [heights(1)], seventh, seventh_arrived, upper, weights)
    seventh_arrived = swap(seventh, 6)
    (carried,) = run(carry_on_body, [(2 * rank + sides, piece)], carried, weights)
    upper, weights = run(factor_body, [heights(1)] * 2, sixth, arrived)
    (seventh,) = run(
        last_panel_body, [(rank + own, rank)], seventh, seventh_arrived, upper, weights, place=place
    )
    arrived = swap(seventh, 7)
    (send,) = run(carry_last_body, [(groups, rank + own, piece)], carried, weights)
    send, seventh = lax.optimization_barrier((send, seventh))
    got = lax.all_to_all(send, "rhs", 0, 0)
    late_order, carried = lax.optimization_barrier((ordering, carried))
    (hot,) = run(
        places_body, [jax.ShapeDtypeStruct((leaf, leaf), jnp.bfloat16)], late_order.reshape(leaf, 1)
    )
    (result,) = run(finish_body, [(own, leaf)], seventh, arrived, got, hot)
    return result


def solution(mesh):
    placed = (P("rhs", "leaf"), P("leaf", "rhs"), P(None, None, "leaf"), P("leaf", None))
    return jax.shard_map(
        local, mesh=mesh, in_specs=placed, out_specs=P("rhs", "leaf"), check_vma=False
    )
```

```python
import functools

import jax
import jax.numpy as jnp
from jax import lax
from jax.experimental import pallas as pl
from jax.experimental.pallas import tpu as pltpu
from jax.sharding import PartitionSpec as P

HIGHEST = lax.Precision.HIGHEST
VMEM_BYTES = 24 * 1024 * 1024
START_BYTES = 60 * 1024 * 1024
NN = (((1,), (0,)), ((), ()))
NT = (((1,), (1,)), ((), ()))


def exact_dot(left, right, dims):
    return lax.dot_general(left, right, dims, precision=HIGHEST, preferred_element_type=jnp.float32)


def short_dot(left, right, dims):
    return lax.dot_general(left, right, dims, preferred_element_type=jnp.float32)


def three_parts(values):
    high = values.astype(jnp.bfloat16)
    rest = values - high.astype(jnp.float32)
    middle = rest.astype(jnp.bfloat16)
    low = (rest - middle.astype(jnp.float32)).astype(jnp.bfloat16)
    return high, middle, low


def dot_left_parts(left, right16, dims):
    high, middle, low = three_parts(left)
    return short_dot(low, right16, dims) + short_dot(middle, right16, dims) + short_dot(high, right16, dims)


def dot_right_parts(left16, right, dims):
    high, middle, low = three_parts(right)
    return short_dot(left16, low, dims) + short_dot(left16, middle, dims) + short_dot(left16, high, dims)


def two_parts(values):
    high = values.astype(jnp.bfloat16)
    return high, (values - high.astype(jnp.float32)).astype(jnp.bfloat16)


def close_dot(left, right):
    left_high, left_low = two_parts(left)
    right_high, right_low = two_parts(right)
    small = short_dot(left_high, right_low, NN) + short_dot(left_low, right_high, NN)
    return small + short_dot(left_high, right_high, NN)


def inverse_of(capacity):
    eye = identity(capacity.shape[0])
    bound = jnp.max(jnp.sum(jnp.abs(capacity), axis=1, keepdims=True), axis=0, keepdims=True)
    scale = 2.0 / (1.0 + bound)
    power = eye - scale * capacity
    series = eye + power
    begin = scale * series
    for _ in range(4):
        power = close_dot(power, power)
        series = series + close_dot(series, power)

    def improve(inverse):
        residual = eye - exact_dot(capacity, inverse, NN)
        size2 = jnp.sum(jnp.sum(residual * residual, axis=1, keepdims=True), axis=0, keepdims=True)
        return inverse + close_dot(inverse, residual), size2

    better, size2 = improve(scale * series)
    better = jnp.where(size2 < 0.25, better, begin)

    def unfinished(state):
        return (state[1] < 80) & jnp.logical_not(state[2] < 1e-6)

    def again(state):
        inverse, size2 = improve(state[0])
        return inverse, state[1] + 1, size2[0, 0]

    return lax.while_loop(unfinished, again, (better, 0, size2[0, 0]))[0]


def shape_of(out):
    return out if isinstance(out, jax.ShapeDtypeStruct) else jax.ShapeDtypeStruct(out, jnp.float32)


def run(body, outs, *args, place=None):
    vmem = pl.BlockSpec(memory_space=pltpu.VMEM)
    scalars = [] if place is None else [place]
    return pl.pallas_call(
        body,
        out_shape=[shape_of(out) for out in outs],
        in_specs=[pl.BlockSpec(memory_space=pltpu.SMEM)] * len(scalars) + [vmem] * len(args),
        out_specs=[vmem] * len(outs),
        cost_estimate=pl.CostEstimate(flops=1_000_000_000, bytes_accessed=0, transcendentals=0),
        compiler_params=pltpu.CompilerParams(vmem_limit_bytes=VMEM_BYTES),
    )(*scalars, *args)


def run_loading(body, outs, *args, place=None):
    parts = [arg.shape[0] if arg.ndim == 3 else 1 for arg in args]
    first = [sum(parts[:index]) for index in range(len(parts))]

    scalars = [] if place is None else [place]

    def loading(*refs):
        count = len(args)
        given, refs = refs[: len(scalars)], refs[len(scalars) :]
        sources, rest = refs[:count], refs[count:]
        results, held, done = rest[: len(outs)], rest[len(outs) : -1], rest[-1]

        def copy(index, part):
            source, target = sources[index], held[index]
            if parts[index] > 1:
                source, target = source.at[part], target.at[part]
            return pltpu.make_async_copy(source, target, done.at[first[index] + part])

        for index in range(count):
            for part in range(parts[index]):
                copy(index, part).start()
        body(lambda index, part=0: copy(index, part).wait(), *given, *held, *results)

    return pl.pallas_call(
        loading,
        out_shape=[shape_of(out) for out in outs],
        in_specs=[pl.BlockSpec(memory_space=pltpu.SMEM)] * len(scalars)
        + [pl.BlockSpec(memory_space=pltpu.HBM)] * len(args),
        out_specs=[pl.BlockSpec(memory_space=pltpu.VMEM)] * len(outs),
        scratch_shapes=[pltpu.VMEM(arg.shape, arg.dtype) for arg in args]
        + [pltpu.SemaphoreType.DMA((sum(parts),))],
        cost_estimate=pl.CostEstimate(flops=1_000_000_000, bytes_accessed=0, transcendentals=0),
        compiler_params=pltpu.CompilerParams(vmem_limit_bytes=START_BYTES),
    )(*scalars, *args)


def one_hot(order):
    size = order.shape[1]
    rows = lax.broadcasted_iota(jnp.int32, (size, size), 0)
    return jnp.where(rows == order, 1.0, 0.0).astype(jnp.bfloat16)


def identity(size):
    shape = (size, size)
    return jnp.where(
        lax.broadcasted_iota(jnp.int32, shape, 0) == lax.broadcasted_iota(jnp.int32, shape, 1), 1.0, 0.0
    )


def stacked(everyone, low, count):
    return jnp.concatenate([everyone[group, low : low + count, :] for group in range(everyone.shape[0])], 0)


def start_body(wait, order, sides, inverse_cols, bases, send, tree):
    levels, rank, leaf = bases.shape
    groups, _, piece = send.shape
    share = rank // groups
    own = sides.shape[0]
    wait(0)
    hot = one_hot(order[...])
    wait(1)
    ordered = dot_left_parts(sides[...], hot, NN)
    for group in range(groups):
        send[group, levels * share :, :] = ordered[:, group * piece : (group + 1) * piece]
    for part in range(leaf // rank):
        tree[part * own : (part + 1) * own, :] = ordered[:, part * rank : (part + 1) * rank]
    wait(2)
    high, middle, low_part = three_parts(inverse_cols[...])
    for level in range(levels):
        wait(3, level)
    rows = bases[...].reshape(levels * rank, leaf)
    applied = short_dot(rows, low_part, NN) + short_dot(rows, middle, NN) + short_dot(rows, high, NN)
    for group in range(groups):
        for level in range(levels):
            low = level * rank + group * share
            send[group, level * share : (level + 1) * share, :] = applied[low : low + share]


def places_body(order, hot):
    columns = lax.broadcasted_iota(jnp.int32, hot.shape, 1)
    hot[...] = jnp.where(columns == order[...], 1.0, 0.0).astype(jnp.bfloat16)


def gram_body(got, send, bases, gram):
    levels, rank, leaf = bases.shape
    groups, rows, piece = got.shape
    share = rank // groups
    own = rows - levels * share
    applied = three_parts(jnp.concatenate([got[group, : levels * share, :] for group in range(groups)], 1))
    at = 0
    for column in range(levels):
        count = (levels - column) * share
        high, middle, low = [part[column * share :] for part in applied]
        right = bases[column]
        gram[at : at + count, :] = (
            short_dot(low, right, NT) + short_dot(middle, right, NT) + short_dot(high, right, NT)
        )
        at += count
    sides = stacked(got, levels * share, own)
    for level in range(levels):
        block = exact_dot(sides, stacked(send, level * share, share), NT)
        for group in range(groups):
            low = at + (group * levels + level) * own
            gram[low : low + own, :] = block[group * own : (group + 1) * own]


def first_body(everyone, mine, arrived, panel, weights, own_weights, inverse, side_weights):
    groups, _, rank = everyone.shape
    share = rank // groups
    own = side_weights.shape[0]
    far = jnp.concatenate([stacked(everyone, level * share, share) for level in range(1, 7)], 0)
    inverse[...] = inverse_of(stacked(everyone, 0, share) + identity(rank))
    side_row = lambda level: sum(
        everyone[group, 7 * share + level * own : 7 * share + (level + 1) * own, :] for group in range(groups)
    )
    upper = jnp.concatenate([mine[share : 7 * share, :] + arrived[share : 7 * share, :], side_row(0)], 0)
    own_weights[...] = exact_dot(upper, inverse[...], NN)
    side_weights[...] = own_weights[6 * share :, :]
    update = exact_dot(own_weights[...], far[:rank], NT)
    panel[: 6 * share, :] = mine[7 * share : 13 * share, :] + arrived[7 * share : 13 * share, :] - update[: 6 * share]
    panel[6 * share :, :] = side_row(1) - update[6 * share :]
    weights[...] = far


def first_rest_body(everyone, mine, arrived, far, own_weights, inverse, rest, far_weights):
    groups, _, rank = everyone.shape
    share = rank // groups
    own = own_weights.shape[0] - 6 * share
    side_row = lambda level: sum(
        everyone[group, 7 * share + level * own : 7 * share + (level + 1) * own, :] for group in range(groups)
    )
    far_weights[...] = exact_dot(far[...], inverse[...], NN)
    at = 0
    source = 13 * share
    for column in range(2, 7):
        count = (7 - column) * share
        update = exact_dot(own_weights[(column - 1) * share :, :], far[(column - 1) * rank : column * rank, :], NT)
        rest[at : at + count, :] = (
            mine[source : source + count, :] + arrived[source : source + count, :] - update[:count]
        )
        rest[at + count : at + count + own, :] = side_row(column) - update[count:]
        source += count
        at += count + own


def level_panel_body(later, later_arrived, far, own_weights, panel):
    rank = far.shape[1]
    count = panel.shape[0]
    update = exact_dot(own_weights[...], far[:rank, :], NT)
    panel[...] = later[:count, :] + later_arrived[:count, :] - update


def level_factor_body(above, place, everyone, far, own_weights, inverse):
    groups, _, rank = everyone.shape
    share = rank // groups
    far[...] = jnp.concatenate([stacked(everyone, level * share, share) for level in range(1, above + 1)], 0)
    inverse[...] = inverse_of(stacked(everyone, 0, share) + identity(rank))
    own_upper = everyone[place[0], share : share + own_weights.shape[0], :]
    own_weights[...] = exact_dot(own_upper, inverse[...], NN)


def level_all_body(above, later, later_arrived, far, own_weights, panels):
    rank = far.shape[1]
    share = rank // 4
    at = 0
    for column in range(above):
        count = own_weights.shape[0] - column * share
        update = exact_dot(own_weights[column * share :, :], far[column * rank : (column + 1) * rank, :], NT)
        panels[at : at + count, :] = later[at : at + count, :] + later_arrived[at : at + count, :] - update
        at += count


def level_rest_body(everyone, later, later_arrived, far, own_weights, inverse, rest, far_weights, side_weights):
    groups, _, rank = everyone.shape
    share = rank // groups
    above = far.shape[0] // rank
    own = own_weights.shape[0] - above * share
    sides = groups * own
    low = (above + 1) * share
    far_weights[...] = exact_dot(far[...], inverse[...], NN)
    side_weights[:sides, :] = stacked(everyone, low + own, own)
    side_weights[sides:, :] = exact_dot(stacked(everyone, low, own), inverse[...], NN)
    at = 0
    source = own_weights.shape[0]
    for column in range(1, far.shape[0] // rank):
        count = own_weights.shape[0] - column * share
        update = exact_dot(own_weights[column * share :, :], far[column * rank : (column + 1) * rank, :], NT)
        rest[at : at + count, :] = (
            later[source : source + count, :] + later_arrived[source : source + count, :] - update
        )
        source += count
        at += count


def spread_body(everyone, fifth, far, weights):
    groups, _, rank = everyone.shape
    share = rank // groups
    own = fifth.shape[0] - 3 * rank
    own = own // groups
    blocks = [stacked(everyone, level * share, share) for level in range(4)]
    inverse = inverse_of(blocks[0] + identity(rank))
    far[: 3 * rank, :] = jnp.concatenate(blocks[1:], 0)
    far[3 * rank :, :] = stacked(everyone, 4 * share, own)
    weights[...] = exact_dot(far[...], inverse, NN)
    update = exact_dot(weights[...], far[:rank, :], NT)
    at = 4 * share + own
    for level in range(3):
        fifth[level * rank : (level + 1) * rank, :] = (
            stacked(everyone, at + level * share, share) - update[level * rank : (level + 1) * rank]
        )
    fifth[3 * rank :, :] = stacked(everyone, at + 3 * share, own) - update[3 * rank :]


def spread_rest_body(column, everyone, far, weights, panel):
    groups, _, rank = everyone.shape
    share = rank // groups
    own = (far.shape[0] - 3 * rank) // groups
    source = (7 if column == 1 else 9) * share + (2 if column == 1 else 3) * own
    update = exact_dot(weights[column * rank :, :], far[column * rank : (column + 1) * rank, :], NT)
    at = 0
    for level in range(column, 3):
        panel[at : at + rank, :] = stacked(everyone, source, share) - update[at : at + rank]
        at += rank
        source += share
    panel[at:, :] = stacked(everyone, source, own) - update[at:]


def factor_body(mine, arrived, upper, weights):
    rank = mine.shape[1]
    upper[...] = mine[rank:, :] + arrived[rank:, :]
    inverse = inverse_of(mine[:rank, :] + arrived[:rank, :] + identity(rank))
    weights[...] = exact_dot(upper[...], inverse, NN)


def next_body(later, later_arrived, upper, weights, panel):
    rank = upper.shape[1]
    panel[...] = later[...] + later_arrived[...] - exact_dot(weights[...], upper[:rank, :], NT)


def rest_body(later, later_arrived, upper, weights, rest):
    rank = upper.shape[1]
    rest[...] = later[...] + later_arrived[...] - exact_dot(weights[rank:, :], upper[rank : 2 * rank, :], NT)


def last_panel_body(place, later, later_arrived, upper, weights, panel):
    rank = upper.shape[1]
    own = panel.shape[0] - rank
    rows = pl.ds(pl.multiple_of(rank + place[0] * own, own), own)
    left = jnp.concatenate([weights[:rank, :], weights[rows, :]], 0)
    update = exact_dot(left, upper[:rank, :], NT)
    panel[:rank, :] = later[:rank, :] + later_arrived[:rank, :] - update[:rank]
    panel[rank:, :] = later[rows, :] + later_arrived[rows, :] - update[rank:]


def carry_step(applied, sides, far, side_far, inverse):
    rank = inverse.shape[0]
    gone = applied[:rank]
    sides = sides - exact_dot(exact_dot(side_far, inverse, NN), gone, NN)
    return applied[rank:] - exact_dot(exact_dot(far, inverse, NN), gone, NN), sides


def carry_first_body(send, weights1, weights2, carried, gone):
    groups = send.shape[0]
    rank = weights2.shape[1]
    share = rank // groups
    applied = [stacked(send, level * share, share) for level in range(7)]
    rest = jnp.concatenate(applied[1:], 0) - exact_dot(weights1[...], applied[0], NN)
    carried[...] = rest[rank:] - exact_dot(weights2[...], rest[:rank], NN)
    gone[:rank, :] = applied[0]
    gone[rank:, :] = rest[:rank]


def carry_body(above, before, gone, side_weights, everyone, far, inverse, inverse_cols, carried):
    groups, rows, rank = everyone.shape
    share = rank // groups
    low = (above + 1) * share
    sides = side_weights.shape[0] // 2
    own = sides // groups
    parts = (rows - low - own) // own
    tree = jnp.concatenate(
        [stacked(everyone, low + own + part * own, own) for part in range(parts)], 1
    )
    found = exact_dot(tree, inverse_cols[...], NN)
    for place in range(2):
        weights = side_weights[place * sides : (place + 1) * sides, :]
        found = found - exact_dot(weights, gone[place * rank : (place + 1) * rank, :], NN)
    applied, found = carry_step(before[...], found, far[...], stacked(everyone, low, own), inverse[...])
    carried[: above * rank, :] = applied
    carried[above * rank :, :] = found


def carry_on_body(before, weights, carried):
    rank = weights.shape[1]
    carried[...] = before[rank:, :] - exact_dot(weights[...], before[:rank, :], NN)


def carry_last_body(before, weights, send):
    groups, rows, _ = send.shape
    rank = weights.shape[1]
    own = rows - rank
    carried = before[rank:, :] - close_dot(weights[...], before[:rank, :])
    for group in range(groups):
        send[group, :rank, :] = carried[:rank]
        send[group, rank:, :] = carried[rank + group * own : rank + (group + 1) * own]


def finish_body(mine, arrived, got, hot, out):
    rank = mine.shape[1]
    groups = got.shape[0]
    inverse = inverse_of(mine[:rank, :] + arrived[:rank, :] + identity(rank))
    top = exact_dot(mine[rank:, :] + arrived[rank:, :], inverse, NN)
    slope = jnp.concatenate([got[group, :rank, :] for group in range(groups)], 1)
    base = jnp.concatenate([got[group, rank:, :] for group in range(groups)], 1)
    out[...] = dot_left_parts(base - close_dot(top, slope), hot[...], NN)


def add_body(*refs):
    send = refs[-1]
    mine, arrived, others = refs[0], refs[1], refs[2:-1]
    count = mine.shape[0]
    total = mine[...] + arrived[...]
    for group in range(send.shape[0]):
        send[group, :count, :] = total
        for other in others:
            send[group, count : count + other.shape[0], :] = other[...]


def sum_to_all(mine, arrived, *others):
    groups = lax.axis_size("rhs")
    rows = sum(block.shape[0] for block in (mine,) + others)
    (send,) = run(add_body, [(groups, rows, mine.shape[1])], mine, arrived, *others)
    return lax.all_to_all(send, "rhs", 0, 0)


def route(height):
    pairs = []
    for leaf in range(128):
        if height in (4, 7):
            low = 1 if height == 4 else 4
            ring = (leaf >> low) & 7
            pairs.append((leaf, leaf & ~(7 << low) | ((ring ^ 6) << low)))
        else:
            pairs.append((leaf, leaf ^ (1 << (height - 1))))
    return pairs


def local(right_sides, leaf_inverse, bases, ordering):
    own, leaf = right_sides.shape
    piece = leaf_inverse.shape[1]
    levels, rank, _ = bases.shape
    groups = lax.axis_size("rhs")
    share = rank // groups
    sides = own * groups
    square = (rank, rank)
    swap = lambda block, height: lax.ppermute(block, "leaf", route(height))

    place = lax.axis_index("rhs").reshape(1)
    send, tree = run_loading(
        start_body,
        [
            (groups, levels * share + own, piece),
            (leaf // rank * own, rank),
        ],
        ordering,
        right_sides,
        leaf_inverse,
        bases,
    )
    got = lax.all_to_all(send, "rhs", 0, 0)
    rows = 28 * share
    (gram,) = run(gram_body, [(rows + groups * levels * own, rank)], got, send, bases)
    other = swap(gram, 1)
    total = gram + other
    shared = jnp.broadcast_to(total[: 7 * share][None], (groups, 7 * share, rank))
    parts = total[rows:].reshape(groups, levels * own, rank)
    everyone = lax.all_to_all(jnp.concatenate([shared, parts], 1), "rhs", 0, 0)

    panel, far1, own_weights, inverse1, side1 = run(
        first_body,
        [(6 * share + own, rank), (6 * rank, rank), (6 * share + own, rank), square, (own, rank)],
        everyone,
        gram,
        other,
    )
    arrived = swap(panel, 2)
    later, far_weights1 = run(
        first_rest_body,
        [(15 * share + 5 * own, rank), (6 * rank, rank)],
        everyone,
        gram,
        other,
        far1,
        own_weights,
        inverse1,
    )
    for height in (2, 3):
        above = 7 - height
        later_arrived = swap(later, height)
        arrived, later = lax.optimization_barrier((arrived, later))
        everyone = sum_to_all(panel, arrived, side1) if height == 2 else sum_to_all(panel, arrived, tree)
        if height == 3:
            everyone, carried = lax.optimization_barrier((everyone, carried))
        far, own_weights, inverse = run(
            functools.partial(level_factor_body, above),
            [(above * rank, rank), (above * share + own, rank), square],
            everyone,
            place=place,
        )
        if height == 2:
            (next_panel,) = run(
                level_panel_body, [(above * share + own, rank)], later, later_arrived, far, own_weights
            )
            arrived = swap(next_panel, 3)
            rest_rows = above * (above - 1) // 2 * share + (above - 1) * own
            later, far_weights2, side_weights = run(
                level_rest_body,
                [(rest_rows, rank), (above * rank, rank), (2 * sides, rank)],
                everyone,
                later,
                later_arrived,
                far,
                own_weights,
                inverse,
            )
            panel = next_panel
            carried, gone = run(
                carry_first_body,
                [(5 * rank, piece), (2 * rank, piece)],
                send,
                far_weights1,
                far_weights2,
            )
        else:
            (panels,) = run(
                functools.partial(level_all_body, above),
                [(above * (above + 1) // 2 * share + above * own, rank)],
                later,
                later_arrived,
                far,
                own_weights,
            )
            panels_arrived = swap(panels, 4)
            (carried,) = run(
                functools.partial(carry_body, above),
                [(4 * rank + sides, piece)],
                carried,
                gone,
                side_weights,
                everyone,
                far,
                inverse,
                leaf_inverse,
            )
    panels_arrived, carried = lax.optimization_barrier((panels_arrived, carried))
    everyone = sum_to_all(panels, panels_arrived)
    heights = lambda count: (count * rank + sides, rank)
    fifth, upper, weights = run(spread_body, [heights(3)] * 3, everyone)
    arrived = swap(fifth, 5)
    (sixth,) = run(functools.partial(spread_rest_body, 1), [heights(2)], everyone, upper, weights)
    sixth_arrived = swap(sixth, 5)
    everyone, sixth = lax.optimization_barrier((everyone, sixth))
    (seventh,) = run(functools.partial(spread_rest_body, 2), [heights(1)], everyone, upper, weights)
    seventh_arrived = swap(seventh, 5)
    (carried,) = run(carry_on_body, [(3 * rank + sides, piece)], carried, weights)
    upper, weights = run(factor_body, [heights(2)] * 2, fifth, arrived)
    (sixth,) = run(next_body, [heights(2)], sixth, sixth_arrived, upper, weights)
    arrived = swap(sixth, 6)
    sixth, seventh = lax.optimization_barrier((sixth, seventh))
    (seventh,) = run(rest_body, [heights(1)], seventh, seventh_arrived, upper, weights)
    seventh_arrived = swap(seventh, 6)
    (carried,) = run(carry_on_body, [(2 * rank + sides, piece)], carried, weights)
    upper, weights = run(factor_body, [heights(1)] * 2, sixth, arrived)
    (seventh,) = run(
        last_panel_body, [(rank + own, rank)], seventh, seventh_arrived, upper, weights, place=place
    )
    arrived = swap(seventh, 7)
    (send,) = run(carry_last_body, [(groups, rank + own, piece)], carried, weights)
    send, seventh = lax.optimization_barrier((send, seventh))
    got = lax.all_to_all(send, "rhs", 0, 0)
    late_order, carried = lax.optimization_barrier((ordering, carried))
    (hot,) = run(
        places_body, [jax.ShapeDtypeStruct((leaf, leaf), jnp.bfloat16)], late_order.reshape(leaf, 1)
    )
    (result,) = run(finish_body, [(own, leaf)], seventh, arrived, got, hot)
    return result


def solution(mesh):
    placed = (P("rhs", "leaf"), P("leaf", "rhs"), P(None, None, "leaf"), P("leaf", None))
    return jax.shard_map(
        local, mesh=mesh, in_specs=placed, out_specs=P("rhs", "leaf"), check_vma=False
    )
```
